128 devices in a mesh: blk: 32 (over z, x_hi, y), freq: 4 (over x_lo, core).
Axes of the slice: x: 4 (x_hi: 2, x_lo: 2; x = x_hi * 2 + x_lo), y: 4, z: 4, core: 2. Of those that a mesh axis runs over, the one named last changes fastest.
Arguments:
- raw: bfloat16 [32768, 1024], P(('blk', 'freq')), may hold values from -6 to 6
- seg_chan: int32 [32768], P(('blk', 'freq')), may hold values from 0 to 4095, as said below
- seg_win: int32 [32768], P(('blk', 'freq')), may hold values from 0 to 3
- file_count: int32 [128], P(('blk', 'freq')), may hold values from 0 to 256, as said below
Outputs:
- stacked: float32 [32, 128, 65536], P(None, 'freq', 'blk')
The draws below stay inside these ranges and needn't reach their ends.
Inputs may be any that keep to these rules, and one draw needn't show every extreme that they name: `seg_chan`: the live slots of all devices (those with index below the device's file_count) name each pair of channel and window exactly once together with seg_win. The segment of channel c belongs to the device at blk = c // 128 and freq = (c % 128) // 32; no device has more than 2 live slots for one such owner, and in every draw some device has exactly 2 for every owner. Dead slots hold arbitrary values. `file_count`: some device has exactly 256 live slots and some device none.
All inputs are finite; a program needn't handle non-finite values.
Results may differ from the reference program's by a relative error of at most 0.0057.
Values may be sent and summed in bfloat16 or wider, within the bound.
No kernel may reach another device: no remote copies, remote signals or barrier semaphores. Data moves between devices by JAX's collectives and lax.ppermute only.
A program may use at most 128 MiB of HBM per device.

```python
import math
import jax
import jax.numpy as jnp
from jax import lax

CHANNELS = 4096
SAMPLES = 1024
LAGS = 16
HALFWIN = 64
WIN = 4
FREQS = 512
CB = 128
QC = 32
SEG_DEV = 128
SLOTS = 256
N_BLK = 32
DEVICES = 128


def routing(key):
    half_count = DEVICES // 2
    base_load = SEG_DEV // DEVICES
    pairing = jax.random.permutation(jax.random.fold_in(key, 11), DEVICES)
    pair_tilt = jax.random.randint(jax.random.fold_in(key, 12), (half_count, 1), -base_load, base_load + 1)
    jitter = jax.random.randint(jax.random.fold_in(key, 13), (half_count, DEVICES), -base_load, base_load + 1)
    shifted = jnp.clip(pair_tilt + jitter, -base_load, base_load)
    shifted = shifted.at[0].set(base_load)
    load_table = jnp.zeros((DEVICES, DEVICES), jnp.int32)
    load_table = load_table.at[pairing[:half_count]].set(base_load + shifted)
    load_table = load_table.at[pairing[half_count:]].set(base_load - shifted)
    scores = jax.random.randint(jax.random.fold_in(key, 14), (DEVICES, SEG_DEV), 0, 1 << 30)
    item_order = jnp.argsort(scores, axis=1, stable=True).astype(jnp.int32)
    begin_at = jnp.cumsum(load_table, axis=0) - load_table
    upto_incl = jnp.cumsum(load_table, axis=1)
    counts = upto_incl[:, -1]
    slot_pos = jnp.arange(SLOTS, dtype=jnp.int32)
    owner_of = jnp.sum((upto_incl[:, None, :] <= slot_pos[None, :, None]).astype(jnp.int32), axis=2)
    owner_safe = jnp.minimum(owner_of, DEVICES - 1)
    before = jnp.take_along_axis(upto_incl, owner_safe, axis=1) - jnp.take_along_axis(load_table, owner_safe, axis=1)
    index_in = jnp.clip(jnp.take_along_axis(begin_at, owner_safe, axis=1) + slot_pos[None, :] - before, 0, SEG_DEV - 1)
    picked = item_order[owner_safe, index_in]
    quarters = DEVICES // N_BLK
    channel = owner_safe // quarters * CB + owner_safe % quarters * QC + picked % QC
    window = picked // QC
    is_dead = slot_pos[None, :] >= counts[:, None]
    mixing = jax.random.randint(jax.random.fold_in(key, 15), (DEVICES, SLOTS), 0, 1 << 20) + is_dead.astype(jnp.int32) * (1 << 21)
    shuffle = jnp.argsort(mixing, axis=1, stable=True)
    channel = jnp.take_along_axis(channel, shuffle, axis=1)
    window = jnp.take_along_axis(window, shuffle, axis=1)
    return (channel, window, counts, is_dead)


def draw_seg_chan(key, part):
    channel, window, counts, is_dead = routing(key)
    key = jax.random.fold_in(key, 3)
    filler = jax.random.randint(key, (DEVICES, SLOTS), 0, CHANNELS)
    return jnp.where(is_dead, filler, channel).reshape(-1).astype(jnp.int32)


def draw_seg_win(key, part):
    channel, window, counts, is_dead = routing(key)
    key = jax.random.fold_in(key, 5)
    filler = jax.random.randint(key, (DEVICES, SLOTS), 0, WIN)
    return jnp.where(is_dead, filler, window).reshape(-1).astype(jnp.int32)


def draw_file_count(key, part):
    channel, window, counts, is_dead = routing(key)
    return counts.astype(jnp.int32)


def level_of(rng, extent, shards, low, high):
    gain, own = 1.0, jax.random.fold_in(rng, 6)
    for dim, parts in shards:
        draws = jnp.exp(jax.random.uniform(jax.random.fold_in(own, dim), (parts,), jnp.float32, low / len(shards), high / len(shards)))
        gain = gain * jnp.repeat(draws, extent[dim] // parts).reshape([-1 if axis == dim else 1 for axis in range(len(extent))])
    return gain


def normal_values(stream_key, shape, width, limit, cuts=(), kind=jnp.bfloat16):
    values = jax.random.normal(stream_key, shape, jnp.float32) * width
    if len(cuts) > 0:
        values = level_of(stream_key, shape, cuts, -0.22, 0.18) * values
    return jnp.clip(values, min=-limit, max=limit).astype(kind)


def setup_inputs(seed: int = 0) -> dict:
    key_of = jax.random.split(jax.random.key(seed), 5)
    return {
        "raw": normal_values(key_of[0], (DEVICES * SLOTS, SAMPLES), 1.0, 6.0, ((0, 128),)),
        "seg_chan": draw_seg_chan(jax.random.fold_in(key_of[4], 71), 0),
        "seg_win": draw_seg_win(jax.random.fold_in(key_of[4], 71), 0),
        "file_count": draw_file_count(jax.random.fold_in(key_of[4], 71), 0),
    }


EPSILON = 1e-06

def taper_curve(samples):
    sample_pos = jnp.arange(samples, dtype=jnp.float32)
    return 0.5 - 0.5 * jnp.cos(2.0 * math.pi / samples * (sample_pos + 0.5))

def prepare(segments):
    values = segments.astype(jnp.float32)
    values = values - lax.optimization_barrier(jnp.mean(values, axis=1, keepdims=True))
    return (values * taper_curve(segments.shape[1])[None, :]).astype(jnp.bfloat16)

def basis_table(samples, freq_total):
    sample_pos = jnp.arange(samples, dtype=jnp.int32)[:, None]
    freq_pos = jnp.arange(freq_total, dtype=jnp.int32)[None, :]
    angles = 2.0 * math.pi / samples * (sample_pos * freq_pos % samples).astype(jnp.float32)
    return jnp.concatenate([jnp.cos(angles), -jnp.sin(angles)], axis=1).astype(jnp.bfloat16)

def whiten(tapered, freq_total, half_width):
    spectrum = jnp.dot(tapered, basis_table(tapered.shape[1], freq_total), preferred_element_type=jnp.float32)
    real_part = spectrum[:, :freq_total]
    imag_part = spectrum[:, freq_total:]
    energy = real_part * real_part + imag_part * imag_part
    freq_pos = jnp.arange(freq_total, dtype=jnp.int32)
    inside = (jnp.abs(freq_pos[:, None] - freq_pos[None, :]) <= half_width).astype(jnp.float32)
    smoother = inside / lax.optimization_barrier(jnp.sum(inside, axis=0, keepdims=True))
    smooth = jnp.dot(energy, smoother, precision=lax.Precision.HIGHEST)
    inverse = lax.rsqrt(smooth + EPSILON)
    return jnp.concatenate([real_part * inverse, imag_part * inverse], axis=1).astype(jnp.bfloat16)

def rotate(whitened, freq_start, lag_count, samples, norm_factor):
    band_size = whitened.shape[3]
    freq_pos = freq_start + jnp.arange(band_size, dtype=jnp.int32)
    lag_steps = jnp.arange(lag_count, dtype=jnp.int32) - lag_count // 2
    angles = 2.0 * math.pi / samples * (lag_steps[:, None] * freq_pos[None, :] % samples).astype(jnp.float32)
    weights = jnp.where(freq_pos == 0, 1.0, 2.0).astype(jnp.float32) * norm_factor
    cosine = (jnp.cos(angles) * weights[None, :])[None, :, None, :]
    sine_part = (jnp.sin(angles) * weights[None, :])[None, :, None, :]
    real_part = whitened[:, None, :, 0, :].astype(jnp.float32)
    imag_part = whitened[:, None, :, 1, :].astype(jnp.float32)
    turned = jnp.stack([real_part * cosine - imag_part * sine_part, real_part * sine_part + imag_part * cosine], axis=3)
    return turned.astype(jnp.bfloat16).reshape(whitened.shape[0] * lag_count, -1)

def reference(raw, seg_chan, seg_win, file_count):
    slot_pos = jnp.arange(DEVICES * SLOTS, dtype=jnp.int32)
    is_live = slot_pos % SLOTS < file_count[slot_pos // SLOTS]
    target = jnp.where(is_live, seg_chan * WIN + seg_win, CHANNELS * WIN)
    segments = jnp.zeros((CHANNELS * WIN, SAMPLES), jnp.bfloat16).at[target].set(raw, mode='drop')
    whitened = whiten(prepare(segments), FREQS, HALFWIN).reshape(CHANNELS, WIN, 2, FREQS)
    partners = whitened.reshape(CHANNELS, -1).astype(jnp.float32)
    norm_factor = 1.0 / math.sqrt(2.0 * WIN * FREQS)

    def one_block(block_start):
        own_rows = lax.dynamic_slice_in_dim(whitened, block_start, CB, 0)
        turned = rotate(own_rows, 0, LAGS, SAMPLES, norm_factor).astype(jnp.float32)
        return lax.dot_general(partners, turned, (((1,), (1,)), ((), ())), precision=lax.Precision.HIGHEST)
    starts = jnp.arange(N_BLK, dtype=jnp.int32) * CB
    result = lax.map(one_block, starts)
    result = jnp.transpose(result, (1, 0, 2)).reshape(N_BLK, CB, CHANNELS * LAGS)
    return result
```

```python
import functools
import math

import jax
import jax.numpy as jnp
import ml_dtypes
import numpy as np
from jax import lax
from jax.experimental import pallas as pl
from jax.experimental.pallas import tpu as pltpu
from jax.sharding import PartitionSpec as P

CHANNELS = 4096
SAMPLES = 1024
FREQS = 512
LAGS = 16
HALFWIN = 64
WIN = 4
EPSILON = 1e-06

NZ, NXH, NY = 4, 2, 4
QC = 32
HALF = QC // 2
SEG_DEV = QC * WIN
SLOTS = 256
DEVICES = 128
SPEC = WIN * 2 * FREQS
TAIL = 128
NT = 256
F32, BF16 = jnp.float32, jnp.bfloat16
VMEM_LIMIT = 48 * 1024 * 1024


def tables():
    n = np.arange(SAMPLES)[:, None]
    k = np.arange(FREQS)[None, :]
    angle = 2.0 * math.pi / SAMPLES * ((n * k) % SAMPLES)
    basis = np.concatenate([np.cos(angle), -np.sin(angle)], axis=1).astype(ml_dtypes.bfloat16)
    taper = (0.5 - 0.5 * np.cos(2.0 * math.pi / SAMPLES * (n[:, 0] + 0.5)))[None, :].astype(np.float32)
    pos = np.arange(FREQS)
    inside = (np.abs(pos[:, None] - pos[None, :]) <= HALFWIN).astype(np.float64)
    smoother = (inside / inside.sum(axis=0, keepdims=True)).astype(np.float32)
    lag = np.arange(LAGS)[:, None] - LAGS // 2
    phi = 2.0 * math.pi / SAMPLES * ((lag * pos[None, :]) % SAMPLES)
    gain = np.where(pos == 0, 1.0, 2.0)[None, :] / math.sqrt(2.0 * WIN * FREQS)
    return basis, taper, smoother, (gain * np.cos(phi)).astype(np.float32), (gain * np.sin(phi)).astype(np.float32)


def diagonal(size):
    return lax.broadcasted_iota(jnp.int32, (size, size), 0) == lax.broadcasted_iota(jnp.int32, (size, size), 1)


def pack_kernel(count_ref, chan_ref, win_ref, raw_ref, out_ref):
    chan = chan_ref[...]
    slot = lax.broadcasted_iota(jnp.int32, (1, SLOTS), 1)
    live = slot < count_ref[0]
    owner = jnp.where(live, chan // QC, -1).astype(F32)
    owner_col = jnp.sum(jnp.where(diagonal(SLOTS), owner, 0.0), axis=1, keepdims=True)
    row = lax.broadcasted_iota(jnp.int32, (SLOTS, SLOTS), 0)
    col = lax.broadcasted_iota(jnp.int32, (SLOTS, SLOTS), 1)
    earlier = jnp.where((owner_col == owner) & (row < col), 1.0, 0.0)
    rank = jnp.sum(earlier, axis=0, keepdims=True)
    flat = jnp.where(live, owner * 2.0 + rank, -1.0)
    pick = jnp.where(flat == row.astype(F32), 1.0, 0.0)
    out_ref[:, :SAMPLES] = jnp.dot(pick.astype(BF16), raw_ref[...], preferred_element_type=F32).astype(BF16)
    place = (win_ref[...] * QC + chan % QC + 1).astype(F32)
    place_col = jnp.sum(pick * place, axis=1, keepdims=True)
    out_ref[:, SAMPLES:] = jnp.broadcast_to(place_col, (SLOTS, TAIL)).astype(BF16)


def whiten_kernel(recv_ref, basis_ref, taper_ref, smoother_ref, out_ref):
    place_col = recv_ref[:, SAMPLES : SAMPLES + 1].astype(F32)
    place = jnp.sum(jnp.where(diagonal(SLOTS), place_col, 0.0), axis=0, keepdims=True)
    wanted = lax.broadcasted_iota(jnp.int32, (SEG_DEV, SLOTS), 0).astype(F32) + 1.0
    pick = jnp.where(place == wanted, 1.0, 0.0).astype(BF16)
    values = jnp.dot(pick, recv_ref[:, :SAMPLES], preferred_element_type=F32)
    values = values - jnp.sum(values, axis=1, keepdims=True) * (1.0 / SAMPLES)
    tapered = (values * taper_ref[...]).astype(BF16)
    spectrum = jnp.dot(tapered, basis_ref[...], preferred_element_type=F32)
    real, imag = spectrum[:, :FREQS], spectrum[:, FREQS:]
    energy = real * real + imag * imag
    smooth = jnp.dot(energy, smoother_ref[...], precision=lax.Precision.HIGHEST, preferred_element_type=F32)
    inverse = lax.rsqrt(smooth + EPSILON)
    real, imag = (real * inverse).astype(BF16), (imag * inverse).astype(BF16)
    for w in range(WIN):
        rows = slice(w * QC, (w + 1) * QC)
        out_ref[:, 2 * w * FREQS : (2 * w + 1) * FREQS] = real[rows]
        out_ref[:, (2 * w + 1) * FREQS : (2 * w + 2) * FREQS] = imag[rows]


def rotate_kernel(own_ref, cos_ref, sin_ref, out_ref, wide):
    wide[...] = own_ref[...].astype(F32)
    for g in range(FREQS // 128):
        cos = cos_ref[:, g * 128 : (g + 1) * 128]
        sin = sin_ref[:, g * 128 : (g + 1) * 128]
        for w in range(WIN):
            re = slice(2 * w * FREQS + g * 128, 2 * w * FREQS + (g + 1) * 128)
            im = slice((2 * w + 1) * FREQS + g * 128, (2 * w + 1) * FREQS + (g + 1) * 128)
            for i in range(16):
                a = wide[i : i + 1, re]
                b = wide[i : i + 1, im]
                out_ref[i * LAGS : (i + 1) * LAGS, re] = (a * cos - b * sin).astype(BF16)
                out_ref[i * LAGS : (i + 1) * LAGS, im] = (a * sin + b * cos).astype(BF16)


def target(out_ref, kind, part, coord, cols):
    if kind == "A":
        if part is None:
            return out_ref.at[pl.ds(2 * coord, 2), :, pl.ds(0, HALF), cols]
        return out_ref.at[2 * coord + part, :, pl.ds(0, HALF), cols]
    if part is None:
        return out_ref.at[:, coord, pl.ds(HALF, HALF), cols]
    return out_ref.at[pl.ds(4 * part, 4), coord, pl.ds(HALF, HALF), cols]


def matmul_kernel(kinds, coords_ref, *refs):
    n = len(kinds)
    pieces, rot_ref = refs[:n], refs[n]
    out_ref, left, acc, in_sem, out_sem = refs[-5:]
    step = pl.program_id(0)
    last = pl.num_programs(0) - 1
    slot = lax.rem(step, 2)
    starts = np.cumsum([0] + [p.shape[0] for p in pieces])

    def loads():
        return [
            pltpu.make_async_copy(p, left.at[pl.ds(int(starts[i]), p.shape[0])], in_sem.at[i])
            for i, p in enumerate(pieces)
        ]

    def stores(slot, step):
        cols = pl.ds(pl.multiple_of(step * NT, NT), NT)
        copies = []
        for i, (kind, part) in enumerate(kinds):
            units = pieces[i].shape[0] // HALF
            begin = int(starts[i]) // HALF
            if kind == "A" and part is None:
                src = acc.at[slot, pl.ds(begin // 4, 2)]
            elif kind == "A" or part is not None:
                src = acc.at[slot, begin // 4]
            if kind == "B" and part is None:
                for h in range(2):
                    copies.append(
                        pltpu.make_async_copy(
                            acc.at[slot, begin // 4 + h],
                            target(out_ref, kind, h, coords_ref[i], cols),
                            out_sem.at[slot, len(copies)],
                        )
                    )
            else:
                copies.append(
                    pltpu.make_async_copy(
                        src, target(out_ref, kind, part, coords_ref[i], cols), out_sem.at[slot, len(copies)]
                    )
                )
        return copies

    @pl.when(step == 0)
    def _():
        for c in loads():
            c.start()
        for c in loads():
            c.wait()

    @pl.when(step >= 2)
    def _():
        for c in stores(slot, step - 2):
            c.wait()

    product = lax.dot_general(left[...], rot_ref[...], (((1,), (1,)), ((), ())), preferred_element_type=F32)
    acc[slot] = product.reshape(acc.shape[1:])
    for c in stores(slot, step):
        c.start()

    @pl.when(step == last)
    def _():
        for c in stores(1 - slot, step - 1):
            c.wait()
        for c in stores(slot, step):
            c.wait()


def matmul(pieces, kinds, coords, rotated, out):
    rows = sum(p.shape[0] for p in pieces)
    columns = rotated.shape[0]
    operands = list(pieces) + [rotated]
    in_specs = [pl.BlockSpec(memory_space=pl.ANY)] * len(pieces) + [
        pl.BlockSpec((NT, SPEC), lambda s, c: (s, 0))
    ]
    aliases = {}
    if out is not None:
        operands.append(out)
        in_specs.append(pl.BlockSpec(memory_space=pl.ANY))
        aliases = {len(operands): 0}
    return pl.pallas_call(
        functools.partial(matmul_kernel, kinds),
        grid_spec=pltpu.PrefetchScalarGridSpec(
            num_scalar_prefetch=1,
            grid=(columns // NT,),
            in_specs=in_specs,
            out_specs=pl.BlockSpec(memory_space=pl.ANY),
            scratch_shapes=[
                pltpu.VMEM((rows, SPEC), BF16),
                pltpu.VMEM((2, rows // HALF // 4, 4, HALF, NT), F32),
                pltpu.SemaphoreType.DMA((len(pieces),)),
                pltpu.SemaphoreType.DMA((2, 2 * len(pieces))),
            ],
        ),
        out_shape=jax.ShapeDtypeStruct((NZ * NXH, NY, QC, columns), F32),
        input_output_aliases=aliases,
        compiler_params=pltpu.CompilerParams(
            dimension_semantics=("arbitrary",), vmem_limit_bytes=VMEM_LIMIT, has_side_effects=False
        ),
        cost_estimate=pl.CostEstimate(
            flops=2 * rows * columns * SPEC, bytes_accessed=2 * columns * SPEC + 4 * rows * columns, transcendentals=0
        ),
    )(jnp.stack(coords).astype(jnp.int32), *operands)


def shifted(value, dz, dxh, dy):
    pairs = []
    for z in range(NZ):
        for xh in range(NXH):
            for y in range(NY):
                to = (((z + dz) % NZ) * NXH + (xh + dxh) % NXH) * NY + (y + dy) % NY
                pairs.append(((z * NXH + xh) * NY + y, to))
    return lax.ppermute(value, "blk", pairs)


def local(raw, seg_chan, seg_win, file_count):
    basis, taper, smoother, cos, sin = (jnp.asarray(t) for t in tables())
    vmem = pl.BlockSpec(memory_space=pltpu.VMEM)
    packed = pl.pallas_call(
        pack_kernel,
        in_specs=[pl.BlockSpec(memory_space=pltpu.SMEM), vmem, vmem, vmem],
        out_specs=vmem,
        out_shape=jax.ShapeDtypeStruct((SLOTS, SAMPLES + TAIL), BF16),
        compiler_params=pltpu.CompilerParams(vmem_limit_bytes=VMEM_LIMIT),
    )(file_count, seg_chan.reshape(1, SLOTS), seg_win.reshape(1, SLOTS), raw)
    arrived = lax.all_to_all(
        packed.reshape(DEVICES, SLOTS // DEVICES, SAMPLES + TAIL),
        ("blk", "freq"),
        split_axis=0,
        concat_axis=0,
        tiled=True,
    ).reshape(SLOTS, SAMPLES + TAIL)
    white = pl.pallas_call(
        whiten_kernel,
        in_specs=[vmem] * 4,
        out_specs=vmem,
        out_shape=jax.ShapeDtypeStruct((QC, SPEC), BF16),
        compiler_params=pltpu.CompilerParams(vmem_limit_bytes=VMEM_LIMIT),
    )(arrived, basis, taper, smoother)

    own = lax.all_gather(white, "freq", axis=0, tiled=True)
    rotated = pl.pallas_call(
        rotate_kernel,
        grid=(own.shape[0] // 16,),
        in_specs=[
            pl.BlockSpec((16, SPEC), lambda s: (s, 0)),
            pl.BlockSpec((LAGS, FREQS), lambda s: (0, 0)),
            pl.BlockSpec((LAGS, FREQS), lambda s: (0, 0)),
        ],
        out_specs=pl.BlockSpec((16 * LAGS, SPEC), lambda s: (s, 0)),
        out_shape=jax.ShapeDtypeStruct((own.shape[0] * LAGS, SPEC), BF16),
        scratch_shapes=[pltpu.VMEM((16, SPEC), F32)],
        compiler_params=pltpu.CompilerParams(dimension_semantics=("arbitrary",), vmem_limit_bytes=VMEM_LIMIT),
        cost_estimate=pl.CostEstimate(flops=6 * 2048 * SPEC, bytes_accessed=2 * 2048 * SPEC, transcendentals=0),
    )(own, cos, sin)

    me = lax.axis_index("blk")
    z, xh, y = me // (NXH * NY), me // NY % NXH, me % NY
    other = shifted(white, 0, 1, 0)

    def spread(mine, theirs, step, place, count):
        held = jnp.concatenate([mine, theirs], axis=0)
        ahead = step(held, 1)
        behind = step(held, -1)
        far = [step(ahead[:HALF], 1), step(behind[HALF:], -1)]
        whole = jnp.zeros((8 * HALF, SPEC), BF16)
        parts = [
            (mine, place(0, 0)),
            (theirs, place(0, 1)),
            (ahead[:HALF], place(1, 0)),
            (ahead[HALF:], place(1, 1)),
            (behind[:HALF], place(-1, 0)),
            (behind[HALF:], place(-1, 1)),
            (far[0], place(2, 0)),
            (far[1], place(2, 1)),
        ]
        for value, spot in parts:
            whole = lax.dynamic_update_slice_in_dim(whole, value, spot * HALF, 0)
        return whole

    def along_y(value, d):
        return shifted(value, 0, 0, d)

    def along_z(value, d):
        return shifted(value, d, 0, 0)

    a8 = spread(
        white[:HALF], other[:HALF], along_y, lambda d, e: (xh + e) % NXH * NY + (y - d) % NY, NY
    )
    b8 = spread(
        white[HALF:], other[HALF:], along_z, lambda d, e: (z - d) % NZ * NXH + (xh + e) % NXH, NZ
    )
    a_ahead, a_behind = along_z(a8, 1), along_z(a8, -1)
    b_ahead, b_behind = along_y(b8, 1), along_y(b8, -1)
    cut = 4 * HALF
    a_far = [along_z(a_ahead[:cut], 1), along_z(a_behind[cut:], -1)]
    b_far = [along_y(b_ahead[:cut], 1), along_y(b_behind[cut:], -1)]

    out = matmul([a8, b8], [("A", None), ("B", None)], [z, y], rotated, None)
    out = matmul(
        [a_ahead, a_behind, b_ahead, b_behind],
        [("A", None), ("A", None), ("B", None), ("B", None)],
        [(z - 1) % NZ, (z + 1) % NZ, (y - 1) % NY, (y + 1) % NY],
        rotated,
        out,
    )
    out = matmul(
        a_far + b_far,
        [("A", 0), ("A", 1), ("B", 0), ("B", 1)],
        [(z + 2) % NZ, (z + 2) % NZ, (y + 2) % NY, (y + 2) % NY],
        rotated,
        out,
    )
    return out.reshape(NZ * NXH * NY, QC, -1)


def solution(mesh):
    in_specs = (
        P(("blk", "freq"), None),
        P(("blk", "freq")),
        P(("blk", "freq")),
        P(("blk", "freq")),
    )
    out_specs = P(None, "freq", "blk")
    return jax.shard_map(local, mesh=mesh, in_specs=in_specs, out_specs=out_specs, check_vma=False)
```

```python
import functools
import math

import jax
import jax.numpy as jnp
import ml_dtypes
import numpy as np
from jax import lax
from jax.experimental import pallas as pl
from jax.experimental.pallas import tpu as pltpu
from jax.sharding import PartitionSpec as P

SAMPLES = 1024
FREQS = 512
LAGS = 16
HALFWIN = 64
WIN = 4
EPSILON = 1e-06

NZ, NXH, NY = 4, 2, 4
NXL, NCORE = 2, 2
QC = 32
HALF = QC // 2
CB = QC * NXL * NCORE
SEG_DEV = QC * WIN
SLOTS = 256
DEVICES = 128
SPEC = WIN * 2 * FREQS
COLS = CB * LAGS
TAIL = 128
NT = 512
GROUP = 4
F32, BF16 = jnp.float32, jnp.bfloat16
MIB = 1024 * 1024
ANY = pl.BlockSpec(memory_space=pl.ANY)
VMEM = pl.BlockSpec(memory_space=pltpu.VMEM)
SMEM = pl.BlockSpec(memory_space=pltpu.SMEM)


def tables():
    n = np.arange(SAMPLES)[:, None]
    k = np.arange(FREQS)[None, :]
    angle = 2.0 * math.pi / SAMPLES * ((n * k) % SAMPLES)
    basis = np.concatenate([np.cos(angle), -np.sin(angle)], axis=1).astype(ml_dtypes.bfloat16)
    taper = (0.5 - 0.5 * np.cos(2.0 * math.pi / SAMPLES * (n[:, 0] + 0.5)))[None, :].astype(np.float32)
    pos = np.arange(FREQS)
    inside = (np.abs(pos[:, None] - pos[None, :]) <= HALFWIN).astype(np.float64)
    smoother = (inside / inside.sum(axis=0, keepdims=True)).astype(np.float32)
    lag = np.arange(128)[None, :] % LAGS - LAGS // 2
    phi = 2.0 * math.pi / SAMPLES * ((lag * pos[:, None]) % SAMPLES)
    gain = np.where(pos == 0, 1.0, 2.0)[:, None] / math.sqrt(2.0 * WIN * FREQS)
    turn = np.concatenate([gain * np.cos(phi), gain * np.sin(phi)], axis=0).astype(np.float32)
    return basis, taper, smoother, turn


def diagonal(size):
    return lax.broadcasted_iota(jnp.int32, (size, size), 0) == lax.broadcasted_iota(jnp.int32, (size, size), 1)


def pack_kernel(count_ref, chan_hbm, win_hbm, raw_hbm, out_ref, chan_ref, win_ref, raw_ref, sem):
    loads = [
        pltpu.make_async_copy(chan_hbm, chan_ref, sem.at[0]),
        pltpu.make_async_copy(win_hbm, win_ref, sem.at[1]),
        pltpu.make_async_copy(raw_hbm, raw_ref, sem.at[2]),
    ]
    for c in loads:
        c.start()
    loads[0].wait()
    loads[1].wait()
    chan = chan_ref[...]
    slot = lax.broadcasted_iota(jnp.int32, (1, SLOTS), 1)
    live = slot < count_ref[0]
    owner = jnp.where(live, chan // QC, -1).astype(F32)
    owner_col = jnp.sum(jnp.where(diagonal(SLOTS), owner, 0.0), axis=1, keepdims=True)
    row = lax.broadcasted_iota(jnp.int32, (SLOTS, SLOTS), 0)
    col = lax.broadcasted_iota(jnp.int32, (SLOTS, SLOTS), 1)
    earlier = jnp.where((owner_col == owner) & (row < col), 1.0, 0.0)
    rank = jnp.sum(earlier, axis=0, keepdims=True)
    flat = jnp.where(live, owner * 2.0 + rank, -1.0)
    pick = jnp.where(flat == row.astype(F32), 1.0, 0.0)
    place = (win_ref[...] * QC + chan % QC + 1).astype(F32)
    place_col = jnp.sum(pick * place, axis=1, keepdims=True)
    out_ref[:, SAMPLES:] = jnp.broadcast_to(place_col, (SLOTS, TAIL)).astype(BF16)
    loads[2].wait()
    out_ref[:, :SAMPLES] = jnp.dot(pick.astype(BF16), raw_ref[...], preferred_element_type=F32).astype(BF16)


def fetch_kernel(after_hbm, basis_hbm, taper_hbm, smoother_hbm, turn_hbm, basis_ref, taper_ref, smoother_ref, turn_ref, sem):
    del after_hbm
    pairs = [(basis_hbm, basis_ref), (taper_hbm, taper_ref), (smoother_hbm, smoother_ref), (turn_hbm, turn_ref)]
    loads = [pltpu.make_async_copy(s, d, sem.at[i]) for i, (s, d) in enumerate(pairs)]
    for c in loads:
        c.start()
    for c in loads:
        c.wait()


def whiten_kernel(core_ref, recv_ref, basis_ref, taper_ref, smoother_ref, out_ref):
    place_col = recv_ref[:, SAMPLES : SAMPLES + 1].astype(F32)
    place = jnp.sum(jnp.where(diagonal(SLOTS), place_col, 0.0), axis=0, keepdims=True)
    row = lax.broadcasted_iota(jnp.int32, (SEG_DEV, SLOTS), 0)
    wanted = row // QC * QC + (row + core_ref[0] * HALF) % QC + 1
    pick = jnp.where(place == wanted.astype(F32), 1.0, 0.0).astype(BF16)
    values = jnp.dot(pick, recv_ref[:, :SAMPLES], preferred_element_type=F32)
    values = values - jnp.sum(values, axis=1, keepdims=True) * (1.0 / SAMPLES)
    tapered = (values * taper_ref[...]).astype(BF16)
    spectrum = jnp.dot(tapered, basis_ref[...], preferred_element_type=F32)
    real, imag = spectrum[:, :FREQS], spectrum[:, FREQS:]
    energy = real * real + imag * imag
    smooth = jnp.dot(energy, smoother_ref[...], precision=lax.Precision.HIGHEST, preferred_element_type=F32)
    inverse = lax.rsqrt(smooth + EPSILON)
    real, imag = (real * inverse).astype(BF16), (imag * inverse).astype(BF16)
    for w in range(WIN):
        rows = slice(w * QC, (w + 1) * QC)
        out_ref[:, 2 * w * FREQS : (2 * w + 1) * FREQS] = real[rows]
        out_ref[:, (2 * w + 1) * FREQS : (2 * w + 2) * FREQS] = imag[rows]


def rotate_kernel(quarter_ref, own0, own1, own2, own3, turn_ref, out_ref, turned, expand):
    col = lax.broadcasted_iota(jnp.int32, (QC, COLS), 1) // LAGS
    row = lax.broadcasted_iota(jnp.int32, (QC, COLS), 0)
    for g, own in enumerate((own0, own1, own2, own3)):
        turned[:, g * QC : (g + 1) * QC] = own[...].T
        q = quarter_ref[g]
        channel = q * QC + (row + (q % NCORE) * HALF) % QC
        expand[g * QC : (g + 1) * QC, :] = jnp.where(col == channel, 1.0, 0.0).astype(BF16)
    step = 64
    per = FREQS // step

    def body(s, carry):
        w, k0 = s // per, pl.multiple_of(lax.rem(s, per) * step, step)
        re = pl.ds(pl.multiple_of(w * 2 * FREQS + k0, step), step)
        im = pl.ds(pl.multiple_of((w * 2 + 1) * FREQS + k0, step), step)
        cos = turn_ref[pl.ds(k0, step), :]
        sin = turn_ref[pl.ds(FREQS + k0, step), :]
        for n in range(COLS // 256):
            a2 = jnp.dot(turned[re, :], expand[:, n * 256 : (n + 1) * 256], preferred_element_type=F32)
            b2 = jnp.dot(turned[im, :], expand[:, n * 256 : (n + 1) * 256], preferred_element_type=F32)
            for h in range(2):
                a, b = a2[:, h * 128 : (h + 1) * 128], b2[:, h * 128 : (h + 1) * 128]
                cols = slice(n * 256 + h * 128, n * 256 + (h + 1) * 128)
                out_ref[re, cols] = (a * cos - b * sin).astype(BF16)
                out_ref[im, cols] = (a * sin + b * cos).astype(BF16)
        return carry

    lax.fori_loop(0, WIN * per, body, 0)


def matmul_kernel(count, ids_ref, *refs):
    mine, theirs, rot_ref = refs[:count], refs[count : 2 * count], refs[2 * count]
    out_ref, left, acc, in_sem, out_sem = refs[-5:]
    rows = GROUP * HALF
    units = 2 * count * GROUP
    loads = []
    for i in range(count):
        loads.append(
            pltpu.make_async_copy(mine[i].at[pl.ds(0, rows)], left.at[pl.ds(2 * i * rows, rows)], in_sem.at[2 * i])
        )
        loads.append(
            pltpu.make_async_copy(
                theirs[i].at[pl.ds(rows, rows)], left.at[pl.ds((2 * i + 1) * rows, rows)], in_sem.at[2 * i + 1]
            )
        )
    for c in loads:
        c.start()
    for c in loads:
        c.wait()

    def stores(slot, step):
        cols = pl.ds(pl.multiple_of(step * NT, NT), NT)
        return [
            pltpu.make_async_copy(acc.at[slot, u], out_ref.at[ids_ref[u], :, cols], out_sem.at[slot, u])
            for u in range(units)
        ]

    for step in range(COLS // NT):
        slot = step % 2
        if step >= 2:
            for c in stores(slot, step - 2):
                c.wait()
        product = jnp.dot(left[...], rot_ref[:, step * NT : (step + 1) * NT], preferred_element_type=F32)
        acc[slot] = product.reshape(units, HALF, NT)
        for c in stores(slot, step):
            c.start()
    for step in range(COLS // NT - 2, COLS // NT):
        for c in stores(step % 2, step):
            c.wait()


def matmul(mine, theirs, ids, rotated, out):
    count = len(mine)
    rows = 2 * count * GROUP * HALF
    operands = [jnp.concatenate(ids), *mine, *theirs, rotated]
    in_specs = [SMEM] + [ANY] * (2 * count) + [VMEM]
    aliases = {}
    if out is not None:
        aliases = {len(operands): 0}
        operands.append(out)
        in_specs.append(ANY)
    return pl.pallas_call(
        functools.partial(matmul_kernel, count),
        in_specs=in_specs,
        out_specs=ANY,
        scratch_shapes=[
            pltpu.VMEM((rows, SPEC), BF16),
            pltpu.VMEM((2, rows // HALF, HALF, NT), F32),
            pltpu.SemaphoreType.DMA((2 * count,)),
            pltpu.SemaphoreType.DMA((2, rows // HALF)),
        ],
        out_shape=jax.ShapeDtypeStruct((NZ * NXH * NY * 2, HALF, COLS), F32),
        input_output_aliases=aliases,
        compiler_params=pltpu.CompilerParams(vmem_limit_bytes=20 * MIB),
        cost_estimate=pl.CostEstimate(
            flops=2 * rows * COLS * SPEC, bytes_accessed=2 * rows * SPEC + 4 * rows * COLS, transcendentals=0
        ),
    )(*operands)


def permuted(value, move):
    sizes = (NZ, NXH, NY, NXL, NCORE)
    pairs = []
    for source in range(DEVICES):
        place = np.unravel_index(source, sizes)
        to = [int(t) % s for t, s in zip(move(*(int(p) for p in place)), sizes, strict=True)]
        pairs.append((source, int(np.ravel_multi_index(to, sizes))))
    return lax.ppermute(value, ("blk", "freq"), pairs)


def first(value, d):
    return permuted(value, lambda z, xh, y, xl, c: (z + d * c, xh, y + d * (1 - c), xl, c))


def second(value, d):
    return permuted(value, lambda z, xh, y, xl, c: (z + d * (1 - c), xh, y + d * c, xl, c))


def across(value):
    return permuted(value, lambda z, xh, y, xl, c: (z, xh + 1, y, xl, c))


def sibling(value):
    return permuted(value, lambda z, xh, y, xl, c: (z, xh, y, xl, c + 1))


def neighbour(value):
    return permuted(value, lambda z, xh, y, xl, c: (z, xh, y, xl + 1, c))


def grouped(units):
    return jnp.concatenate([u[:HALF] for u in units] + [u[HALF:] for u in units], axis=0)


def local(raw, seg_chan, seg_win, file_count):
    basis, taper, smoother, turn = (jnp.asarray(t) for t in tables())
    blk, freq = lax.axis_index("blk"), lax.axis_index("freq")
    z, xh, y = blk // (NXH * NY), blk // NY % NXH, blk % NY
    xl, core = freq // NCORE, freq % NCORE

    packed = pl.pallas_call(
        pack_kernel,
        in_specs=[SMEM, ANY, ANY, ANY],
        out_specs=VMEM,
        out_shape=jax.ShapeDtypeStruct((SLOTS, SAMPLES + TAIL), BF16),
        scratch_shapes=[
            pltpu.VMEM((1, SLOTS), jnp.int32),
            pltpu.VMEM((1, SLOTS), jnp.int32),
            pltpu.VMEM((SLOTS, SAMPLES), BF16),
            pltpu.SemaphoreType.DMA((3,)),
        ],
        compiler_params=pltpu.CompilerParams(vmem_limit_bytes=8 * MIB),
    )(file_count, seg_chan.reshape(1, SLOTS), seg_win.reshape(1, SLOTS), raw)
    arrived = lax.all_to_all(
        packed.reshape(DEVICES, SLOTS // DEVICES, SAMPLES + TAIL),
        ("blk", "freq"),
        split_axis=0,
        concat_axis=0,
        tiled=True,
    ).reshape(SLOTS, SAMPLES + TAIL)
    tabled = (basis, taper, smoother, turn)
    basis, taper, smoother, turn = pl.pallas_call(
        fetch_kernel,
        in_specs=[ANY] * 5,
        out_specs=[VMEM] * 4,
        out_shape=[jax.ShapeDtypeStruct(t.shape, t.dtype) for t in tabled],
        scratch_shapes=[pltpu.SemaphoreType.DMA((4,))],
        compiler_params=pltpu.CompilerParams(vmem_limit_bytes=8 * MIB),
        cost_estimate=pl.CostEstimate(flops=0, bytes_accessed=8 * MIB, transcendentals=0),
    )(packed, *tabled)
    white = pl.pallas_call(
        whiten_kernel,
        in_specs=[SMEM] + [VMEM] * 4,
        out_specs=VMEM,
        out_shape=jax.ShapeDtypeStruct((QC, SPEC), BF16),
        compiler_params=pltpu.CompilerParams(vmem_limit_bytes=8 * MIB),
    )(core.reshape(1), arrived, basis, taper, smoother)

    sib = sibling(white)
    unit = jnp.concatenate([white[:HALF], sib[HALF:]], axis=0)
    beyond = across(unit)
    ahead, behind = first(unit, 1), first(unit, -1)
    facing = neighbour(white)
    facing_sib = sibling(facing)

    quarters = jnp.stack([(xl ^ (g // 2)) * NCORE + (core ^ (g % 2)) for g in range(4)]).astype(jnp.int32)
    rotated = pl.pallas_call(
        rotate_kernel,
        in_specs=[SMEM] + [VMEM] * 5,
        out_specs=VMEM,
        out_shape=jax.ShapeDtypeStruct((SPEC, COLS), BF16),
        scratch_shapes=[pltpu.VMEM((SPEC, CB), BF16), pltpu.VMEM((CB, COLS), BF16)],
        compiler_params=pltpu.CompilerParams(vmem_limit_bytes=8 * MIB),
        cost_estimate=pl.CostEstimate(flops=2 * CB * SPEC * COLS * 4, bytes_accessed=MIB, transcendentals=0),
    )(quarters, white, sib, facing, facing_sib, turn)

    pair = first(jnp.concatenate([beyond, ahead], axis=0), 1)
    beyond_behind = first(beyond, -1)
    beyond_far = first(beyond_behind, -1)
    near = grouped([unit, beyond, ahead, behind])
    rest = grouped([pair[:QC], pair[QC:], beyond_behind, beyond_far])
    near_up, near_down = second(near, 1), second(near, -1)
    rest_up, rest_down = second(rest, 1), second(rest, -1)
    near_far, rest_far = second(near_up, 1), second(rest_down, -1)

    def ids(offsets, dq):
        found = []
        for c in (core, 1 - core):
            for dp, dx in offsets:
                p0, q0 = jnp.where(c == 0, y, z), jnp.where(c == 0, z, y)
                p1, q1 = (p0 + dp) % 4, (q0 + dq) % 4
                zz, yy = jnp.where(c == 0, q1, p1), jnp.where(c == 0, p1, q1)
                found.append(((zz * NXH + (xh + dx) % NXH) * NY + yy) * 2 + c)
        return jnp.stack(found).astype(jnp.int32)

    near_at = [(0, 0), (0, 1), (-1, 0), (1, 0)]
    rest_at = [(-1, 1), (-2, 0), (1, 1), (2, 1)]
    out = None
    for arrays in (
        [(near, near_at, 0), (rest, rest_at, 0)],
        [(near_up, near_at, -1), (near_down, near_at, 1)],
        [(rest_up, rest_at, -1), (rest_down, rest_at, 1)],
        [(near_far, near_at, -2), (rest_far, rest_at, 2)],
    ):
        out = matmul(
            [a for a, _, _ in arrays],
            [sibling(a) for a, _, _ in arrays],
            [ids(at, dq) for _, at, dq in arrays],
            rotated,
            out,
        )
    return out.reshape(NZ * NXH * NY, QC, COLS)


def solution(mesh):
    in_specs = (
        P(("blk", "freq"), None),
        P(("blk", "freq")),
        P(("blk", "freq")),
        P(("blk", "freq")),
    )
    out_specs = P(None, "freq", "blk")
    return jax.shard_map(local, mesh=mesh, in_specs=in_specs, out_specs=out_specs, check_vma=False)
```

```python
import functools
import math

import jax
import jax.numpy as jnp
import ml_dtypes
import numpy as np
from jax import lax
from jax.experimental import pallas as pl
from jax.experimental.pallas import tpu as pltpu
from jax.sharding import PartitionSpec as P

SAMPLES = 1024
FREQS = 512
LAGS = 16
HALFWIN = 64
WIN = 4
EPSILON = 1e-06

NZ, NXH, NY = 4, 2, 4
NXL, NCORE = 2, 2
QC = 32
HALF = QC // 2
CB = QC * NXL * NCORE
SEG_DEV = QC * WIN
SLOTS = 256
DEVICES = 128
SPEC = WIN * 2 * FREQS
COLS = CB * LAGS
TAIL = 128
NT = 512
TILES = COLS // NT
GROUP = 4
F32, BF16 = jnp.float32, jnp.bfloat16
MIB = 1024 * 1024
SMALL = pl.CostEstimate(flops=1024, bytes_accessed=1024, transcendentals=0)
TOKEN = jax.ShapeDtypeStruct((8, 128), F32)
ANY = pl.BlockSpec(memory_space=pl.ANY)
HBM = pl.BlockSpec(memory_space=pltpu.HBM)
VMEM = pl.BlockSpec(memory_space=pltpu.VMEM)
SMEM = pl.BlockSpec(memory_space=pltpu.SMEM)


def tables():
    n = np.arange(SAMPLES)[:, None]
    k = np.arange(FREQS)[None, :]
    angle = 2.0 * math.pi / SAMPLES * ((n * k) % SAMPLES)
    basis = np.concatenate([np.cos(angle), -np.sin(angle)], axis=1).astype(ml_dtypes.bfloat16)
    taper = (0.5 - 0.5 * np.cos(2.0 * math.pi / SAMPLES * (n[:, 0] + 0.5)))[None, :].astype(np.float32)
    pos = np.arange(FREQS)[:, None]
    lag = np.arange(128)[None, :] % LAGS - LAGS // 2
    phi = 2.0 * math.pi / SAMPLES * ((lag * pos) % SAMPLES)
    gain = np.where(pos == 0, 1.0, 2.0) / math.sqrt(2.0 * WIN * FREQS)
    turn = np.concatenate([gain * np.cos(phi), gain * np.sin(phi)], axis=0).astype(np.float32)
    return basis, taper, turn


def diagonal(size):
    return lax.broadcasted_iota(jnp.int32, (size, size), 0) == lax.broadcasted_iota(jnp.int32, (size, size), 1)


def pack_kernel(count_ref, chan_hbm, win_hbm, raw_hbm, out_ref, chan_ref, win_ref, raw_ref, sem):
    loads = [
        pltpu.make_async_copy(chan_hbm, chan_ref, sem.at[0]),
        pltpu.make_async_copy(win_hbm, win_ref, sem.at[1]),
        pltpu.make_async_copy(raw_hbm, raw_ref, sem.at[2]),
    ]
    for c in loads:
        c.start()
    loads[0].wait()
    loads[1].wait()
    chan = chan_ref[...]
    slot = lax.broadcasted_iota(jnp.int32, (1, SLOTS), 1)
    live = slot < count_ref[0]
    owner = jnp.where(live, chan // QC, -1).astype(F32)
    owner_col = jnp.sum(jnp.where(diagonal(SLOTS), owner, 0.0), axis=1, keepdims=True)
    row = lax.broadcasted_iota(jnp.int32, (SLOTS, SLOTS), 0)
    col = lax.broadcasted_iota(jnp.int32, (SLOTS, SLOTS), 1)
    earlier = jnp.where((owner_col == owner) & (row < col), 1.0, 0.0)
    rank = jnp.sum(earlier, axis=0, keepdims=True)
    flat = jnp.where(live, owner * 2.0 + rank, -1.0)
    pick = jnp.where(flat == row.astype(F32), 1.0, 0.0)
    place = (win_ref[...] * QC + chan % QC + 1).astype(F32)
    place_col = jnp.sum(pick * place, axis=1, keepdims=True)
    out_ref[:, SAMPLES:] = jnp.broadcast_to(place_col, (SLOTS, TAIL)).astype(BF16)
    loads[2].wait()
    out_ref[:, :SAMPLES] = jnp.dot(pick.astype(BF16), raw_ref[...], preferred_element_type=F32).astype(BF16)


def fetch_kernel(after_hbm, basis_hbm, taper_hbm, basis_ref, taper_ref, sem):
    del after_hbm
    loads = [
        pltpu.make_async_copy(basis_hbm, basis_ref, sem.at[0]),
        pltpu.make_async_copy(taper_hbm, taper_ref, sem.at[1]),
    ]
    for c in loads:
        c.start()
    for c in loads:
        c.wait()


def band_mean(energy):
    row = lax.broadcasted_iota(jnp.int32, (FREQS, FREQS), 0)
    col = lax.broadcasted_iota(jnp.int32, (FREQS, FREQS), 1)
    inside = jnp.where(jnp.abs(row - col) <= HALFWIN, 1.0, 0.0).astype(BF16)
    high = energy.astype(BF16)
    left = energy - high.astype(F32)
    middle = left.astype(BF16)
    low = (left - middle.astype(F32)).astype(BF16)
    total = jnp.dot(low, inside, preferred_element_type=F32)
    total = total + jnp.dot(middle, inside, preferred_element_type=F32)
    total = total + jnp.dot(high, inside, preferred_element_type=F32)
    pos = lax.broadcasted_iota(jnp.int32, (1, FREQS), 1)
    count = jnp.minimum(pos, HALFWIN) + jnp.minimum(FREQS - 1 - pos, HALFWIN) + 1
    return total / count.astype(F32)


def whiten_kernel(place_ref, recv_ref, basis_ref, taper_ref, out_ref):
    place_col = recv_ref[:, SAMPLES : SAMPLES + 1].astype(F32)
    place = jnp.sum(jnp.where(diagonal(SLOTS), place_col, 0.0), axis=0, keepdims=True)
    row = lax.broadcasted_iota(jnp.int32, (SEG_DEV, SLOTS), 0)
    wanted = row // QC * QC + (row + place_ref[4] * HALF) % QC + 1
    pick = jnp.where(place == wanted.astype(F32), 1.0, 0.0).astype(BF16)
    values = jnp.dot(pick, recv_ref[:, :SAMPLES], preferred_element_type=F32)
    values = values - jnp.sum(values, axis=1, keepdims=True) * (1.0 / SAMPLES)
    tapered = (values * taper_ref[...]).astype(BF16)
    spectrum = jnp.dot(tapered, basis_ref[...], preferred_element_type=F32)
    real, imag = spectrum[:, :FREQS], spectrum[:, FREQS:]
    inverse = lax.rsqrt(band_mean(real * real + imag * imag) + EPSILON)
    real, imag = (real * inverse).astype(BF16), (imag * inverse).astype(BF16)
    for w in range(WIN):
        rows = slice(w * QC, (w + 1) * QC)
        out_ref[:, 2 * w * FREQS : (2 * w + 1) * FREQS] = real[rows]
        out_ref[:, (2 * w + 1) * FREQS : (2 * w + 2) * FREQS] = imag[rows]


def group_kernel(moves, n_in, *refs):
    outs, sem = refs[n_in:-1], refs[-1]
    copies = [
        pltpu.make_async_copy(
            refs[i].at[pl.ds(h * HALF, HALF)], outs[o].at[pl.ds(p * HALF, HALF)], sem.at[n]
        )
        for n, (i, h, o, p) in enumerate(moves)
    ]
    for c in copies:
        c.start()
    for c in copies:
        c.wait()


def grouped(moves, halves, arrays, after):
    return pl.pallas_call(
        functools.partial(group_kernel, moves, len(arrays) + len(after)),
        in_specs=[ANY] * (len(arrays) + len(after)),
        out_specs=[ANY] * len(halves),
        out_shape=[jax.ShapeDtypeStruct((n * HALF, SPEC), BF16) for n in halves],
        scratch_shapes=[pltpu.SemaphoreType.DMA((len(moves),))],
        compiler_params=pltpu.CompilerParams(vmem_limit_bytes=MIB),
        cost_estimate=SMALL,
    )(*arrays, *after)


def gate_kernel(*refs):
    del refs


def gated(value, after):
    return pl.pallas_call(
        gate_kernel,
        in_specs=[ANY] * (1 + len(after)),
        out_specs=ANY,
        out_shape=jax.ShapeDtypeStruct(value.shape, value.dtype),
        input_output_aliases={0: 0},
        compiler_params=pltpu.CompilerParams(vmem_limit_bytes=MIB),
        cost_estimate=SMALL,
    )(value, *after)


def rotate_kernel(place_ref, own0, own1, own2, own3, turn_hbm, out_ref, token_ref, turn_ref, whole, turned, expand, sem):
    load = pltpu.make_async_copy(turn_hbm, turn_ref, sem.at[0])
    load.start()
    col = lax.broadcasted_iota(jnp.int32, (HALF, COLS), 1) // LAGS
    row = lax.broadcasted_iota(jnp.int32, (HALF, COLS), 0)
    for g, own in enumerate((own0, own1, own2, own3)):
        whole[g * QC : (g + 1) * QC, :] = own[...]
    for k in range(0, SPEC, FREQS):
        turned[k : k + FREQS, :] = whole[:, k : k + FREQS].T
    xl, core = place_ref[3], place_ref[4]
    halves = [(0, 0, 0), (0, 0, 1), (0, 1, 1), (0, 1, 0), (1, 0, 0), (1, 1, 0), (1, 1, 1), (1, 0, 1)]
    for g, (chip, other, flip) in enumerate(halves):
        quarter = (1 - xl if chip else xl) * NCORE + (1 - core if other else core)
        base = quarter * QC + (1 - core if flip else core) * HALF
        expand[g * HALF : (g + 1) * HALF, :] = jnp.where(col == base + row, 1.0, 0.0).astype(BF16)
    load.wait()
    token_ref[...] = jnp.zeros_like(token_ref)
    step = 256
    per = FREQS // step

    def body(s, carry):
        w, k0 = s // per, pl.multiple_of(lax.rem(s, per) * step, step)
        re = pl.ds(pl.multiple_of(w * 2 * FREQS + k0, step), step)
        im = pl.ds(pl.multiple_of((w * 2 + 1) * FREQS + k0, step), step)
        cos = turn_ref[pl.ds(k0, step), :]
        sin = turn_ref[pl.ds(FREQS + k0, step), :]
        for n in range(COLS // 256):
            a2 = jnp.dot(turned[re, :], expand[:, n * 256 : (n + 1) * 256], preferred_element_type=F32)
            b2 = jnp.dot(turned[im, :], expand[:, n * 256 : (n + 1) * 256], preferred_element_type=F32)
            for h in range(2):
                a, b = a2[:, h * 128 : (h + 1) * 128], b2[:, h * 128 : (h + 1) * 128]
                cols = slice(n * 256 + h * 128, n * 256 + (h + 1) * 128)
                out_ref[re, cols] = (a * cos - b * sin).astype(BF16)
                out_ref[im, cols] = (a * sin + b * cos).astype(BF16)
        return carry

    lax.fori_loop(0, WIN * per, body, 0)


def matmul_kernel(sources, n_in, place_ref, *refs):
    rot_ref = refs[n_in]
    out_ref, token_ref, left, acc, in_sem, out_sem = refs[-6:]
    rows = GROUP * HALF
    z, xh, y, core = place_ref[0], place_ref[1], place_ref[2], place_ref[4]
    loads = [
        pltpu.make_async_copy(refs[i].at[pl.ds(row, rows)], left.at[pl.ds(n * rows, rows)], in_sem.at[n])
        for n, (i, row, _, _, _) in enumerate(sources)
    ]
    for c in loads:
        c.start()
    token_ref[...] = jnp.zeros_like(token_ref)
    ids = []
    for _, _, other, offsets, dq in sources:
        c = 1 - core if other else core
        for dp, dx in offsets:
            p = lax.rem(jnp.where(c == 0, y, z) + dp + 4, 4)
            q = lax.rem(jnp.where(c == 0, z, y) + dq + 4, 4)
            block = (jnp.where(c == 0, q, p) * NXH + lax.rem(xh + dx, NXH)) * NY + jnp.where(c == 0, p, q)
            ids.append(block * 2 + c)
    for c in loads:
        c.wait()

    def stores(step):
        cols = pl.ds(step * NT, NT)
        slot = step % 2
        return [
            pltpu.make_async_copy(acc.at[slot, u], out_ref.at[i, :, cols], out_sem.at[slot, u])
            for u, i in enumerate(ids)
        ]

    for step in range(TILES):
        if step >= 2:
            for c in stores(step - 2):
                c.wait()
        product = jnp.dot(left[...], rot_ref[:, step * NT : (step + 1) * NT], preferred_element_type=F32)
        acc[step % 2] = product.reshape(acc.shape[1:])
        for c in stores(step):
            c.start()
    for step in range(TILES - 2, TILES):
        for c in stores(step):
            c.wait()


def matmul(place, carried, rotated, out):
    arrays, sources = [], []
    for value, theirs, at, dq in carried:
        n = len(arrays)
        arrays += [value, theirs]
        sources += [(n, 0, False, at, dq), (n + 1, GROUP * HALF, True, at, dq)]
    rows = len(sources) * GROUP * HALF
    operands = [place, *arrays, rotated]
    in_specs = [SMEM] + [ANY] * len(arrays) + [VMEM]
    aliases = {}
    if out is not None:
        aliases = {len(operands): 0}
        operands.append(out)
        in_specs.append(ANY)
    return pl.pallas_call(
        functools.partial(matmul_kernel, sources, len(arrays)),
        in_specs=in_specs,
        out_specs=[ANY, VMEM],
        scratch_shapes=[
            pltpu.VMEM((rows, SPEC), BF16),
            pltpu.VMEM((2, rows // HALF, HALF, NT), F32),
            pltpu.SemaphoreType.DMA((len(sources),)),
            pltpu.SemaphoreType.DMA((2, rows // HALF)),
        ],
        out_shape=[jax.ShapeDtypeStruct((NZ * NXH * NY * 2, HALF, COLS), F32), TOKEN],
        input_output_aliases=aliases,
        compiler_params=pltpu.CompilerParams(vmem_limit_bytes=12 * MIB),
        cost_estimate=pl.CostEstimate(
            flops=3 * rows * COLS * SPEC, bytes_accessed=2 * rows * SPEC + 4 * rows * COLS, transcendentals=0
        ),
    )(*operands)


def permuted(value, move):
    sizes = (NZ, NXH, NY, NXL, NCORE)
    pairs = []
    for source in range(DEVICES):
        place = np.unravel_index(source, sizes)
        to = [int(t) % s for t, s in zip(move(*(int(p) for p in place)), sizes, strict=True)]
        pairs.append((source, int(np.ravel_multi_index(to, sizes))))
    return lax.ppermute(value, ("blk", "freq"), pairs)


def first(value, d):
    return permuted(value, lambda z, xh, y, xl, c: (z + d * c, xh, y + d * (1 - c), xl, c))


def second(value, d):
    return permuted(value, lambda z, xh, y, xl, c: (z + d * (1 - c), xh, y + d * c, xl, c))


def across(value):
    return permuted(value, lambda z, xh, y, xl, c: (z, xh + 1, y, xl, c))


def sibling(value):
    return permuted(value, lambda z, xh, y, xl, c: (z, xh, y, xl, c + 1))


def neighbour(value):
    return permuted(value, lambda z, xh, y, xl, c: (z, xh, y, xl + 1, c))


def local(raw, seg_chan, seg_win, file_count):
    basis, taper, turn = (jnp.asarray(t) for t in tables())
    blk, freq = lax.axis_index("blk"), lax.axis_index("freq")
    z, xh, y = blk // (NXH * NY), blk // NY % NXH, blk % NY
    place = jnp.stack([z, xh, y, freq // NCORE, freq % NCORE]).astype(jnp.int32)

    packed = pl.pallas_call(
        pack_kernel,
        in_specs=[SMEM, HBM, HBM, HBM],
        out_specs=VMEM,
        out_shape=jax.ShapeDtypeStruct((SLOTS, SAMPLES + TAIL), BF16),
        scratch_shapes=[
            pltpu.VMEM((1, SLOTS), jnp.int32),
            pltpu.VMEM((1, SLOTS), jnp.int32),
            pltpu.VMEM((SLOTS, SAMPLES), BF16),
            pltpu.SemaphoreType.DMA((3,)),
        ],
        compiler_params=pltpu.CompilerParams(vmem_limit_bytes=8 * MIB),
    )(file_count, seg_chan.reshape(1, SLOTS), seg_win.reshape(1, SLOTS), raw)
    arrived = lax.all_to_all(
        packed.reshape(DEVICES, SLOTS // DEVICES, SAMPLES + TAIL),
        ("blk", "freq"),
        split_axis=0,
        concat_axis=0,
        tiled=True,
    ).reshape(SLOTS, SAMPLES + TAIL)
    basis, taper = pl.pallas_call(
        fetch_kernel,
        in_specs=[ANY, HBM, HBM],
        out_specs=[VMEM] * 2,
        out_shape=[jax.ShapeDtypeStruct(t.shape, t.dtype) for t in (basis, taper)],
        scratch_shapes=[pltpu.SemaphoreType.DMA((2,))],
        compiler_params=pltpu.CompilerParams(vmem_limit_bytes=MIB),
        cost_estimate=SMALL,
    )(packed, basis, taper)
    white = pl.pallas_call(
        whiten_kernel,
        in_specs=[SMEM] + [VMEM] * 3,
        out_specs=VMEM,
        out_shape=jax.ShapeDtypeStruct((QC, SPEC), BF16),
        compiler_params=pltpu.CompilerParams(vmem_limit_bytes=8 * MIB),
    )(place, arrived, basis, taper)

    sib = sibling(white)
    unit = jnp.concatenate([white[:HALF], sib[HALF:]], axis=0)
    beyond = across(unit)
    ahead, behind = first(unit, 1), first(unit, -1)
    facing = neighbour(gated(unit, [ahead, behind]))
    facing_sib = sibling(facing)
    two = [(i, h, 0, 2 * i + h) for i in range(2) for h in range(2)]
    pair = first(grouped(two, [4], [beyond, ahead], [])[0], 1)
    beyond_behind = first(beyond, -1)
    beyond_far = first(beyond, 2)
    moves = [(i, h, 0, h * GROUP + i) for i in range(GROUP) for h in range(2)]
    (near,) = grouped(moves, [8], [unit, beyond, ahead, behind], [])
    near_up, near_down = second(near, 1), second(near, -1)
    moves = [(0, 0, 0, 0), (0, 1, 0, 4), (0, 2, 0, 1), (0, 3, 0, 5)]
    moves += [(i, h, 0, h * GROUP + i + 1) for i in (1, 2) for h in range(2)]
    (rest,) = grouped(moves, [8], [pair, beyond_behind, beyond_far], [])
    rest_up, rest_down = second(rest, 1), second(rest, -1)
    rotated, _ = pl.pallas_call(
        rotate_kernel,
        in_specs=[SMEM] + [VMEM] * 4 + [HBM],
        out_specs=[VMEM, VMEM],
        out_shape=[jax.ShapeDtypeStruct((SPEC, COLS), BF16), TOKEN],
        scratch_shapes=[
            pltpu.VMEM((2 * FREQS, 128), F32),
            pltpu.VMEM((CB, SPEC), BF16),
            pltpu.VMEM((SPEC, CB), BF16),
            pltpu.VMEM((CB, COLS), BF16),
            pltpu.SemaphoreType.DMA((1,)),
        ],
        compiler_params=pltpu.CompilerParams(vmem_limit_bytes=8 * MIB),
        cost_estimate=pl.CostEstimate(flops=2 * CB * SPEC * COLS * 5, bytes_accessed=MIB, transcendentals=0),
    )(place, white, sib, facing, facing_sib, turn)

    near_at = [(0, 0), (0, 1), (-1, 0), (1, 0)]
    rest_at = [(-1, 1), (-2, 0), (1, 1), (2, 1)]

    def product(out, *carried):
        return matmul(place, [(value, sibling(value), at, dq) for value, at, dq in carried], rotated, out)

    out, done = product(None, (near, near_at, 0), (near_down, near_at, 1))
    near_up = gated(near_up, [done])
    near_far = second(near_up, 1)
    out, done = product(out, (rest, rest_at, 0))
    rest_down = gated(rest_down, [done, rest_up])
    rest_far = second(rest_down, -1)
    out, _ = product(out, (near_up, near_at, -1), (rest_up, rest_at, -1))
    out, done = product(out, (rest_down, rest_at, 1), (near_far, near_at, -2))
    out, _ = product(out, (gated(rest_far, [done]), rest_at, 2))
    return out.reshape(NZ * NXH * NY, QC, COLS)


def solution(mesh):
    in_specs = (
        P(("blk", "freq"), None),
        P(("blk", "freq")),
        P(("blk", "freq")),
        P(("blk", "freq")),
    )
    out_specs = P(None, "freq", "blk")
    return jax.shard_map(local, mesh=mesh, in_specs=in_specs, out_specs=out_specs, check_vma=False)
```

```python
import functools
import math

import jax
import jax.numpy as jnp
import ml_dtypes
import numpy as np
from jax import lax
from jax.experimental import pallas as pl
from jax.experimental.pallas import tpu as pltpu
from jax.sharding import PartitionSpec as P

SAMPLES = 1024
FREQS = 512
LAGS = 16
HALFWIN = 64
WIN = 4
EPSILON = 1e-06

NZ, NXH, NY = 4, 2, 4
NXL, NCORE = 2, 2
QC = 32
HALF = QC // 2
CB = QC * NXL * NCORE
SEG_DEV = QC * WIN
SLOTS = 256
DEVICES = 128
SPEC = WIN * 2 * FREQS
COLS = CB * LAGS
TAIL = 128
NT = 512
TILES = COLS // NT
GROUP = 4
F32, BF16 = jnp.float32, jnp.bfloat16
MIB = 1024 * 1024
SMALL = pl.CostEstimate(flops=1024, bytes_accessed=1024, transcendentals=0)
TOKEN = jax.ShapeDtypeStruct((8, 128), F32)
ANY = pl.BlockSpec(memory_space=pl.ANY)
HBM = pl.BlockSpec(memory_space=pltpu.HBM)
VMEM = pl.BlockSpec(memory_space=pltpu.VMEM)
SMEM = pl.BlockSpec(memory_space=pltpu.SMEM)


def tables():
    n = np.arange(SAMPLES)[:, None]
    k = np.arange(FREQS)[None, :]
    angle = 2.0 * math.pi / SAMPLES * ((n * k) % SAMPLES)
    basis = np.concatenate([np.cos(angle), -np.sin(angle)], axis=1).astype(ml_dtypes.bfloat16)
    taper = (0.5 - 0.5 * np.cos(2.0 * math.pi / SAMPLES * (n[:, 0] + 0.5)))[None, :].astype(np.float32)
    pos = np.arange(FREQS)[:, None]
    lag = np.arange(128)[None, :] % LAGS - LAGS // 2
    phi = 2.0 * math.pi / SAMPLES * ((lag * pos) % SAMPLES)
    gain = np.where(pos == 0, 1.0, 2.0) / math.sqrt(2.0 * WIN * FREQS)
    turn = np.concatenate([gain * np.cos(phi), gain * np.sin(phi)], axis=0).astype(np.float32)
    return basis, taper, turn


def diagonal(size):
    return lax.broadcasted_iota(jnp.int32, (size, size), 0) == lax.broadcasted_iota(jnp.int32, (size, size), 1)


def pack_kernel(count_ref, chan_hbm, win_hbm, raw_hbm, out_ref, chan_ref, win_ref, raw_ref, sem):
    loads = [
        pltpu.make_async_copy(chan_hbm, chan_ref, sem.at[0]),
        pltpu.make_async_copy(win_hbm, win_ref, sem.at[1]),
        pltpu.make_async_copy(raw_hbm, raw_ref, sem.at[2]),
    ]
    for c in loads:
        c.start()
    loads[0].wait()
    loads[1].wait()
    chan = chan_ref[...]
    slot = lax.broadcasted_iota(jnp.int32, (1, SLOTS), 1)
    live = slot < count_ref[0]
    owner = jnp.where(live, chan // QC, -1).astype(F32)
    owner_col = jnp.sum(jnp.where(diagonal(SLOTS), owner, 0.0), axis=1, keepdims=True)
    row = lax.broadcasted_iota(jnp.int32, (SLOTS, SLOTS), 0)
    col = lax.broadcasted_iota(jnp.int32, (SLOTS, SLOTS), 1)
    earlier = jnp.where((owner_col == owner) & (row < col), 1.0, 0.0)
    rank = jnp.sum(earlier, axis=0, keepdims=True)
    flat = jnp.where(live, owner * 2.0 + rank, -1.0)
    pick = jnp.where(flat == row.astype(F32), 1.0, 0.0)
    place = (win_ref[...] * QC + chan % QC + 1).astype(F32)
    place_col = jnp.sum(pick * place, axis=1, keepdims=True)
    out_ref[:, SAMPLES:] = jnp.broadcast_to(place_col, (SLOTS, TAIL)).astype(BF16)
    loads[2].wait()
    out_ref[:, :SAMPLES] = jnp.dot(pick.astype(BF16), raw_ref[...], preferred_element_type=F32).astype(BF16)


def fetch_kernel(after_hbm, basis_hbm, taper_hbm, basis_ref, taper_ref, sem):
    del after_hbm
    loads = [
        pltpu.make_async_copy(basis_hbm, basis_ref, sem.at[0]),
        pltpu.make_async_copy(taper_hbm, taper_ref, sem.at[1]),
    ]
    for c in loads:
        c.start()
    for c in loads:
        c.wait()


def band_mean(energy):
    row = lax.broadcasted_iota(jnp.int32, (FREQS, FREQS), 0)
    col = lax.broadcasted_iota(jnp.int32, (FREQS, FREQS), 1)
    inside = jnp.where(jnp.abs(row - col) <= HALFWIN, 1.0, 0.0).astype(BF16)
    high = energy.astype(BF16)
    left = energy - high.astype(F32)
    middle = left.astype(BF16)
    low = (left - middle.astype(F32)).astype(BF16)
    total = jnp.dot(low, inside, preferred_element_type=F32)
    total = total + jnp.dot(middle, inside, preferred_element_type=F32)
    total = total + jnp.dot(high, inside, preferred_element_type=F32)
    pos = lax.broadcasted_iota(jnp.int32, (1, FREQS), 1)
    count = jnp.minimum(pos, HALFWIN) + jnp.minimum(FREQS - 1 - pos, HALFWIN) + 1
    return total / count.astype(F32)


def whiten_kernel(place_ref, recv_ref, basis_ref, taper_ref, out_ref):
    place_col = recv_ref[:, SAMPLES : SAMPLES + 1].astype(F32)
    place = jnp.sum(jnp.where(diagonal(SLOTS), place_col, 0.0), axis=0, keepdims=True)
    row = lax.broadcasted_iota(jnp.int32, (SEG_DEV, SLOTS), 0)
    wanted = row // QC * QC + (row + place_ref[4] * HALF) % QC + 1
    pick = jnp.where(place == wanted.astype(F32), 1.0, 0.0).astype(BF16)
    values = jnp.dot(pick, recv_ref[:, :SAMPLES], preferred_element_type=F32)
    values = values - jnp.sum(values, axis=1, keepdims=True) * (1.0 / SAMPLES)
    tapered = (values * taper_ref[...]).astype(BF16)
    spectrum = jnp.dot(tapered, basis_ref[...], preferred_element_type=F32)
    real, imag = spectrum[:, :FREQS], spectrum[:, FREQS:]
    inverse = lax.rsqrt(band_mean(real * real + imag * imag) + EPSILON)
    real, imag = (real * inverse).astype(BF16), (imag * inverse).astype(BF16)
    for w in range(WIN):
        rows = slice(w * QC, (w + 1) * QC)
        out_ref[:, 2 * w * FREQS : (2 * w + 1) * FREQS] = real[rows]
        out_ref[:, (2 * w + 1) * FREQS : (2 * w + 2) * FREQS] = imag[rows]


def group_kernel(moves, n_in, *refs):
    outs, sem = refs[n_in:-1], refs[-1]
    copies = [
        pltpu.make_async_copy(
            refs[i].at[pl.ds(h * HALF, HALF)], outs[o].at[pl.ds(p * HALF, HALF)], sem.at[n]
        )
        for n, (i, h, o, p) in enumerate(moves)
    ]
    for c in copies:
        c.start()
    for c in copies:
        c.wait()


def grouped(moves, halves, arrays, after):
    return pl.pallas_call(
        functools.partial(group_kernel, moves, len(arrays) + len(after)),
        in_specs=[ANY] * (len(arrays) + len(after)),
        out_specs=[ANY] * len(halves),
        out_shape=[jax.ShapeDtypeStruct((n * HALF, SPEC), BF16) for n in halves],
        scratch_shapes=[pltpu.SemaphoreType.DMA((len(moves),))],
        compiler_params=pltpu.CompilerParams(vmem_limit_bytes=MIB),
        cost_estimate=SMALL,
    )(*arrays, *after)


def gate_kernel(*refs):
    del refs


def gated(value, after):
    return pl.pallas_call(
        gate_kernel,
        in_specs=[ANY] * (1 + len(after)),
        out_specs=ANY,
        out_shape=jax.ShapeDtypeStruct(value.shape, value.dtype),
        input_output_aliases={0: 0},
        compiler_params=pltpu.CompilerParams(vmem_limit_bytes=MIB),
        cost_estimate=SMALL,
    )(value, *after)


def rotate_kernel(place_ref, own0, own1, own2, own3, turn_hbm, out_ref, token_ref, turn_ref, whole, turned, expand, sem):
    load = pltpu.make_async_copy(turn_hbm, turn_ref, sem.at[0])
    load.start()
    col = lax.broadcasted_iota(jnp.int32, (HALF, COLS), 1) // LAGS
    row = lax.broadcasted_iota(jnp.int32, (HALF, COLS), 0)
    for g, own in enumerate((own0, own1, own2, own3)):
        whole[g * QC : (g + 1) * QC, :] = own[...]
    for k in range(0, SPEC, FREQS):
        turned[k : k + FREQS, :] = whole[:, k : k + FREQS].T
    xl, core = place_ref[3], place_ref[4]
    halves = [(0, 0, 0), (0, 0, 1), (0, 1, 1), (0, 1, 0), (1, 0, 0), (1, 1, 0), (1, 1, 1), (1, 0, 1)]
    for g, (chip, other, flip) in enumerate(halves):
        quarter = (1 - xl if chip else xl) * NCORE + (1 - core if other else core)
        base = quarter * QC + (1 - core if flip else core) * HALF
        expand[g * HALF : (g + 1) * HALF, :] = jnp.where(col == base + row, 1.0, 0.0).astype(BF16)
    load.wait()
    token_ref[...] = jnp.zeros_like(token_ref)
    step = 256
    per = FREQS // step

    def body(s, carry):
        w, k0 = s // per, pl.multiple_of(lax.rem(s, per) * step, step)
        re = pl.ds(pl.multiple_of(w * 2 * FREQS + k0, step), step)
        im = pl.ds(pl.multiple_of((w * 2 + 1) * FREQS + k0, step), step)
        cos = turn_ref[pl.ds(k0, step), :]
        sin = turn_ref[pl.ds(FREQS + k0, step), :]
        for n in range(COLS // 256):
            a2 = jnp.dot(turned[re, :], expand[:, n * 256 : (n + 1) * 256], preferred_element_type=F32)
            b2 = jnp.dot(turned[im, :], expand[:, n * 256 : (n + 1) * 256], preferred_element_type=F32)
            for h in range(2):
                a, b = a2[:, h * 128 : (h + 1) * 128], b2[:, h * 128 : (h + 1) * 128]
                cols = slice(n * 256 + h * 128, n * 256 + (h + 1) * 128)
                out_ref[re, cols] = (a * cos - b * sin).astype(BF16)
                out_ref[im, cols] = (a * sin + b * cos).astype(BF16)
        return carry

    lax.fori_loop(0, WIN * per, body, 0)


def matmul_kernel(sources, n_in, place_ref, *refs):
    rot_ref = refs[n_in]
    out_ref, token_ref, left, acc, in_sem, out_sem = refs[-6:]
    z, xh, y, core = place_ref[0], place_ref[1], place_ref[2], place_ref[4]
    loads, begin = [], 0
    for n, (i, row, _, offsets, _) in enumerate(sources):
        rows = len(offsets) * HALF
        loads.append(
            pltpu.make_async_copy(refs[i].at[pl.ds(row, rows)], left.at[pl.ds(begin, rows)], in_sem.at[n])
        )
        begin += rows
    for c in loads:
        c.start()
    token_ref[...] = jnp.zeros_like(token_ref)
    ids = []
    for _, _, other, offsets, dq in sources:
        c = 1 - core if other else core
        for dp, dx in offsets:
            p = lax.rem(jnp.where(c == 0, y, z) + dp + 4, 4)
            q = lax.rem(jnp.where(c == 0, z, y) + dq + 4, 4)
            block = (jnp.where(c == 0, q, p) * NXH + lax.rem(xh + dx, NXH)) * NY + jnp.where(c == 0, p, q)
            ids.append(block * 2 + c)
    for c in loads:
        c.wait()

    def stores(step):
        cols = pl.ds(step * NT, NT)
        slot = step % 2
        return [
            pltpu.make_async_copy(acc.at[slot, u], out_ref.at[i, :, cols], out_sem.at[slot, u])
            for u, i in enumerate(ids)
        ]

    for step in range(TILES):
        if step >= 2:
            for c in stores(step - 2):
                c.wait()
        product = jnp.dot(left[...], rot_ref[:, step * NT : (step + 1) * NT], preferred_element_type=F32)
        acc[step % 2] = product.reshape(acc.shape[1:])
        for c in stores(step):
            c.start()
    for step in range(TILES - 2, TILES):
        for c in stores(step):
            c.wait()


def matmul(place, carried, rotated, out):
    arrays = [value for value, _, _, _ in carried]
    sources = [(n, len(at) * HALF if other else 0, other, at, dq) for n, (_, other, at, dq) in enumerate(carried)]
    rows = sum(len(at) for _, _, at, _ in carried) * HALF
    operands = [place, *arrays, rotated]
    in_specs = [SMEM] + [ANY] * len(arrays) + [VMEM]
    aliases = {}
    if out is not None:
        aliases = {len(operands): 0}
        operands.append(out)
        in_specs.append(ANY)
    return pl.pallas_call(
        functools.partial(matmul_kernel, sources, len(arrays)),
        in_specs=in_specs,
        out_specs=[ANY, VMEM],
        scratch_shapes=[
            pltpu.VMEM((rows, SPEC), BF16),
            pltpu.VMEM((2, rows // HALF, HALF, NT), F32),
            pltpu.SemaphoreType.DMA((len(sources),)),
            pltpu.SemaphoreType.DMA((2, rows // HALF)),
        ],
        out_shape=[jax.ShapeDtypeStruct((NZ * NXH * NY * 2, HALF, COLS), F32), TOKEN],
        input_output_aliases=aliases,
        compiler_params=pltpu.CompilerParams(vmem_limit_bytes=12 * MIB),
        cost_estimate=pl.CostEstimate(
            flops=3 * rows * COLS * SPEC, bytes_accessed=2 * rows * SPEC + 4 * rows * COLS, transcendentals=0
        ),
    )(*operands)


def permuted(value, move):
    sizes = (NZ, NXH, NY, NXL, NCORE)
    pairs = []
    for source in range(DEVICES):
        place = np.unravel_index(source, sizes)
        to = [int(t) % s for t, s in zip(move(*(int(p) for p in place)), sizes, strict=True)]
        pairs.append((source, int(np.ravel_multi_index(to, sizes))))
    return lax.ppermute(value, ("blk", "freq"), pairs)


def first(value, d):
    return permuted(value, lambda z, xh, y, xl, c: (z + d * c, xh, y + d * (1 - c), xl, c))


def second(value, d):
    return permuted(value, lambda z, xh, y, xl, c: (z + d * (1 - c), xh, y + d * c, xl, c))


def across(value):
    return permuted(value, lambda z, xh, y, xl, c: (z, xh + 1, y, xl, c))


def sibling(value):
    return permuted(value, lambda z, xh, y, xl, c: (z, xh, y, xl, c + 1))


def neighbour(value):
    return permuted(value, lambda z, xh, y, xl, c: (z, xh, y, xl + 1, c))


def local(raw, seg_chan, seg_win, file_count):
    basis, taper, turn = (jnp.asarray(t) for t in tables())
    blk, freq = lax.axis_index("blk"), lax.axis_index("freq")
    z, xh, y = blk // (NXH * NY), blk // NY % NXH, blk % NY
    place = jnp.stack([z, xh, y, freq // NCORE, freq % NCORE]).astype(jnp.int32)

    packed = pl.pallas_call(
        pack_kernel,
        in_specs=[SMEM, HBM, HBM, HBM],
        out_specs=VMEM,
        out_shape=jax.ShapeDtypeStruct((SLOTS, SAMPLES + TAIL), BF16),
        scratch_shapes=[
            pltpu.VMEM((1, SLOTS), jnp.int32),
            pltpu.VMEM((1, SLOTS), jnp.int32),
            pltpu.VMEM((SLOTS, SAMPLES), BF16),
            pltpu.SemaphoreType.DMA((3,)),
        ],
        compiler_params=pltpu.CompilerParams(vmem_limit_bytes=8 * MIB),
    )(file_count, seg_chan.reshape(1, SLOTS), seg_win.reshape(1, SLOTS), raw)
    arrived = lax.all_to_all(
        packed.reshape(DEVICES, SLOTS // DEVICES, SAMPLES + TAIL),
        ("blk", "freq"),
        split_axis=0,
        concat_axis=0,
        tiled=True,
    ).reshape(SLOTS, SAMPLES + TAIL)
    basis, taper = pl.pallas_call(
        fetch_kernel,
        in_specs=[ANY, HBM, HBM],
        out_specs=[VMEM] * 2,
        out_shape=[jax.ShapeDtypeStruct(t.shape, t.dtype) for t in (basis, taper)],
        scratch_shapes=[pltpu.SemaphoreType.DMA((2,))],
        compiler_params=pltpu.CompilerParams(vmem_limit_bytes=MIB),
        cost_estimate=SMALL,
    )(packed, basis, taper)
    white = pl.pallas_call(
        whiten_kernel,
        in_specs=[SMEM] + [VMEM] * 3,
        out_specs=VMEM,
        out_shape=jax.ShapeDtypeStruct((QC, SPEC), BF16),
        compiler_params=pltpu.CompilerParams(vmem_limit_bytes=8 * MIB),
    )(place, arrived, basis, taper)

    sib = sibling(white)
    unit = jnp.concatenate([white[:HALF], sib[HALF:]], axis=0)
    beyond = across(unit)
    ahead, behind = first(unit, 1), first(unit, -1)
    facing = neighbour(unit)
    facing_sib = sibling(facing)
    two = [(i, h, 0, 2 * i + h) for i in range(2) for h in range(2)]
    pair = first(grouped(two, [4], [beyond, ahead], [])[0], 1)
    beyond_behind = first(beyond, -1)
    beyond_far = first(beyond, 2)
    arrays = [unit, beyond, ahead, behind, beyond_behind, beyond_far, pair]
    moves = [(i, h, 0, 8 * h + i) for i in range(6) for h in range(2)]
    moves += [(6, 2 * i + h, 0, 8 * h + 6 + i) for i in range(2) for h in range(2)]
    line_at = [(0, 0), (0, 1), (-1, 0), (1, 0), (1, 1), (2, 1), (-1, 1), (-2, 0)]
    (line,) = grouped(moves, [16], arrays, [facing_sib])
    up, down = second(line, 1), second(line, -1)
    rotated, _ = pl.pallas_call(
        rotate_kernel,
        in_specs=[SMEM] + [VMEM] * 4 + [HBM],
        out_specs=[VMEM, VMEM],
        out_shape=[jax.ShapeDtypeStruct((SPEC, COLS), BF16), TOKEN],
        scratch_shapes=[
            pltpu.VMEM((2 * FREQS, 128), F32),
            pltpu.VMEM((CB, SPEC), BF16),
            pltpu.VMEM((SPEC, CB), BF16),
            pltpu.VMEM((CB, COLS), BF16),
            pltpu.SemaphoreType.DMA((1,)),
        ],
        compiler_params=pltpu.CompilerParams(vmem_limit_bytes=8 * MIB),
        cost_estimate=pl.CostEstimate(flops=2 * CB * SPEC * COLS * 5, bytes_accessed=MIB, transcendentals=0),
    )(place, white, sib, facing, facing_sib, turn)

    out, done = matmul(place, [(line, False, line_at, 0), (sibling(line), True, line_at, 0)], rotated, None)
    up, down = gated(up, [done]), gated(down, [done])
    parts = [[(i, 8 * h + 4 * i + u, i, 4 * h + u) for h in range(2) for u in range(4)] for i in range(2)]
    turn_up, turn_down = grouped(parts[0] + parts[1], [8, 8], [up, down], [])
    far_up, far_down = second(turn_up, 1), second(turn_down, -1)
    out, _ = matmul(place, [(up, False, line_at, -1), (down, False, line_at, 1)], rotated, out)
    out, done = matmul(place, [(sibling(up), True, line_at, -1), (sibling(down), True, line_at, 1)], rotated, out)
    far_up, far_down = gated(far_up, [done]), gated(far_down, [done])
    halves = [(far_up, line_at[:4], -2), (far_down, line_at[4:], 2)]
    out, _ = matmul(place, [(value, False, at, dq) for value, at, dq in halves], rotated, out)
    out, _ = matmul(place, [(sibling(value), True, at, dq) for value, at, dq in halves], rotated, out)
    return out.reshape(NZ * NXH * NY, QC, COLS)


def solution(mesh):
    in_specs = (
        P(("blk", "freq"), None),
        P(("blk", "freq")),
        P(("blk", "freq")),
        P(("blk", "freq")),
    )
    out_specs = P(None, "freq", "blk")
    return jax.shard_map(local, mesh=mesh, in_specs=in_specs, out_specs=out_specs, check_vma=False)
```

```python
import functools
import math

import jax
import jax.numpy as jnp
import ml_dtypes
import numpy as np
from jax import lax
from jax.experimental import pallas as pl
from jax.experimental.pallas import tpu as pltpu
from jax.sharding import PartitionSpec as P

SAMPLES = 1024
FREQS = 512
LAGS = 16
HALFWIN = 64
WIN = 4
EPSILON = 1e-06

NZ, NXH, NY = 4, 2, 4
NXL, NCORE = 2, 2
QC = 32
HALF = QC // 2
CB = QC * NXL * NCORE
SEG_DEV = QC * WIN
SLOTS = 256
DEVICES = 128
SPEC = WIN * 2 * FREQS
COLS = CB * LAGS
SIDE = COLS // NXL
TAIL = 128
NT = 512
TILES = COLS // NT
GROUP = 4
F32, BF16 = jnp.float32, jnp.bfloat16
MIB = 1024 * 1024
SMALL = pl.CostEstimate(flops=1024, bytes_accessed=1024, transcendentals=0)
TOKEN = jax.ShapeDtypeStruct((8, 128), F32)
ANY = pl.BlockSpec(memory_space=pl.ANY)
HBM = pl.BlockSpec(memory_space=pltpu.HBM)
VMEM = pl.BlockSpec(memory_space=pltpu.VMEM)
SMEM = pl.BlockSpec(memory_space=pltpu.SMEM)


def tables():
    n = np.arange(SAMPLES)[:, None]
    k = np.arange(FREQS)[None, :]
    angle = 2.0 * math.pi / SAMPLES * ((n * k) % SAMPLES)
    basis = np.concatenate([np.cos(angle), -np.sin(angle)], axis=1).astype(ml_dtypes.bfloat16)
    taper = (0.5 - 0.5 * np.cos(2.0 * math.pi / SAMPLES * (n[:, 0] + 0.5)))[None, :].astype(np.float32)
    pos = np.arange(FREQS)[:, None]
    lag = np.arange(128)[None, :] % LAGS - LAGS // 2
    phi = 2.0 * math.pi / SAMPLES * ((lag * pos) % SAMPLES)
    gain = np.where(pos == 0, 1.0, 2.0) / math.sqrt(2.0 * WIN * FREQS)
    turn = np.concatenate([gain * np.cos(phi), gain * np.sin(phi)], axis=0).astype(np.float32)
    return basis, taper, turn


def diagonal(size):
    return lax.broadcasted_iota(jnp.int32, (size, size), 0) == lax.broadcasted_iota(jnp.int32, (size, size), 1)


def pack_kernel(count_ref, chan_hbm, win_hbm, raw_hbm, out_ref, chan_ref, win_ref, raw_ref, sem):
    loads = [
        pltpu.make_async_copy(chan_hbm, chan_ref, sem.at[0]),
        pltpu.make_async_copy(win_hbm, win_ref, sem.at[1]),
        pltpu.make_async_copy(raw_hbm, raw_ref, sem.at[2]),
    ]
    for c in loads:
        c.start()
    loads[0].wait()
    loads[1].wait()
    chan = chan_ref[...]
    slot = lax.broadcasted_iota(jnp.int32, (1, SLOTS), 1)
    live = slot < count_ref[0]
    owner = jnp.where(live, chan // QC, -1).astype(F32)
    owner_col = jnp.sum(jnp.where(diagonal(SLOTS), owner, 0.0), axis=1, keepdims=True)
    row = lax.broadcasted_iota(jnp.int32, (SLOTS, SLOTS), 0)
    col = lax.broadcasted_iota(jnp.int32, (SLOTS, SLOTS), 1)
    earlier = jnp.where((owner_col == owner) & (row < col), 1.0, 0.0)
    rank = jnp.sum(earlier, axis=0, keepdims=True)
    flat = jnp.where(live, owner * 2.0 + rank, -1.0)
    pick = jnp.where(flat == row.astype(F32), 1.0, 0.0)
    place = (win_ref[...] * QC + chan % QC + 1).astype(F32)
    place_col = jnp.sum(pick * place, axis=1, keepdims=True)
    out_ref[:, SAMPLES:] = jnp.broadcast_to(place_col, (SLOTS, TAIL)).astype(BF16)
    loads[2].wait()
    out_ref[:, :SAMPLES] = jnp.dot(pick.astype(BF16), raw_ref[...], preferred_element_type=F32).astype(BF16)


def fetch_kernel(after_hbm, basis_hbm, taper_hbm, basis_ref, taper_ref, sem):
    del after_hbm
    loads = [
        pltpu.make_async_copy(basis_hbm, basis_ref, sem.at[0]),
        pltpu.make_async_copy(taper_hbm, taper_ref, sem.at[1]),
    ]
    for c in loads:
        c.start()
    for c in loads:
        c.wait()


def band_mean(energy):
    row = lax.broadcasted_iota(jnp.int32, (FREQS, FREQS), 0)
    col = lax.broadcasted_iota(jnp.int32, (FREQS, FREQS), 1)
    inside = jnp.where(jnp.abs(row - col) <= HALFWIN, 1.0, 0.0).astype(BF16)
    high = energy.astype(BF16)
    left = energy - high.astype(F32)
    middle = left.astype(BF16)
    low = (left - middle.astype(F32)).astype(BF16)
    total = jnp.dot(low, inside, preferred_element_type=F32)
    total = total + jnp.dot(middle, inside, preferred_element_type=F32)
    total = total + jnp.dot(high, inside, preferred_element_type=F32)
    pos = lax.broadcasted_iota(jnp.int32, (1, FREQS), 1)
    count = jnp.minimum(pos, HALFWIN) + jnp.minimum(FREQS - 1 - pos, HALFWIN) + 1
    return total / count.astype(F32)


def whiten_kernel(place_ref, recv_ref, basis_ref, taper_ref, out_ref):
    place_col = recv_ref[:, SAMPLES : SAMPLES + 1].astype(F32)
    place = jnp.sum(jnp.where(diagonal(SLOTS), place_col, 0.0), axis=0, keepdims=True)
    row = lax.broadcasted_iota(jnp.int32, (SEG_DEV, SLOTS), 0)
    wanted = row // QC * QC + (row + place_ref[4] * HALF) % QC + 1
    pick = jnp.where(place == wanted.astype(F32), 1.0, 0.0).astype(BF16)
    values = jnp.dot(pick, recv_ref[:, :SAMPLES], preferred_element_type=F32)
    values = values - jnp.sum(values, axis=1, keepdims=True) * (1.0 / SAMPLES)
    tapered = (values * taper_ref[...]).astype(BF16)
    spectrum = jnp.dot(tapered, basis_ref[...], preferred_element_type=F32)
    real, imag = spectrum[:, :FREQS], spectrum[:, FREQS:]
    inverse = lax.rsqrt(band_mean(real * real + imag * imag) + EPSILON)
    real, imag = (real * inverse).astype(BF16), (imag * inverse).astype(BF16)
    for w in range(WIN):
        rows = slice(w * QC, (w + 1) * QC)
        out_ref[:, 2 * w * FREQS : (2 * w + 1) * FREQS] = real[rows]
        out_ref[:, (2 * w + 1) * FREQS : (2 * w + 2) * FREQS] = imag[rows]


def group_kernel(moves, n_in, *refs):
    outs = refs[n_in:]
    for i, h, o, p in moves:
        outs[o][p * HALF : (p + 1) * HALF, :] = refs[i][h * HALF : (h + 1) * HALF, :]


def grouped(moves, halves, arrays, after):
    return pl.pallas_call(
        functools.partial(group_kernel, moves, len(arrays) + len(after)),
        in_specs=[VMEM] * len(arrays) + [ANY] * len(after),
        out_specs=[VMEM] * len(halves),
        out_shape=[jax.ShapeDtypeStruct((n * HALF, SPEC), BF16) for n in halves],
        compiler_params=pltpu.CompilerParams(vmem_limit_bytes=MIB),
        cost_estimate=pl.CostEstimate(flops=0, bytes_accessed=2 * MIB, transcendentals=0),
    )(*arrays, *after)


def gate_kernel(*refs):
    del refs


def gated(value, after):
    return pl.pallas_call(
        gate_kernel,
        in_specs=[ANY] * (1 + len(after)),
        out_specs=ANY,
        out_shape=jax.ShapeDtypeStruct(value.shape, value.dtype),
        input_output_aliases={0: 0},
        compiler_params=pltpu.CompilerParams(vmem_limit_bytes=MIB),
        cost_estimate=SMALL,
    )(value, *after)


def rotate_kernel(halves, place_ref, own0, own1, turn_hbm, out_ref, token_ref, turn_ref, whole, turned, expand, sem):
    load = pltpu.make_async_copy(turn_hbm, turn_ref, sem.at[0])
    load.start()
    col = lax.broadcasted_iota(jnp.int32, (HALF, SIDE), 1) // LAGS
    row = lax.broadcasted_iota(jnp.int32, (HALF, SIDE), 0)
    for g, own in enumerate((own0, own1)):
        whole[g * QC : (g + 1) * QC, :] = own[...]
    for k in range(0, SPEC, FREQS):
        turned[k : k + FREQS, :] = whole[:, k : k + FREQS].T
    core = place_ref[4]
    for g, (other, flip) in enumerate(halves):
        base = (1 - core if other else core) * QC + (1 - core if flip else core) * HALF
        expand[g * HALF : (g + 1) * HALF, :] = jnp.where(col == base + row, 1.0, 0.0).astype(BF16)
    load.wait()
    token_ref[...] = jnp.zeros_like(token_ref)
    step = 256
    per = FREQS // step

    def body(s, carry):
        w, k0 = s // per, pl.multiple_of(lax.rem(s, per) * step, step)
        re = pl.ds(pl.multiple_of(w * 2 * FREQS + k0, step), step)
        im = pl.ds(pl.multiple_of((w * 2 + 1) * FREQS + k0, step), step)
        cos = turn_ref[pl.ds(k0, step), :]
        sin = turn_ref[pl.ds(FREQS + k0, step), :]
        for n in range(SIDE // 256):
            a2 = jnp.dot(turned[re, :], expand[:, n * 256 : (n + 1) * 256], preferred_element_type=F32)
            b2 = jnp.dot(turned[im, :], expand[:, n * 256 : (n + 1) * 256], preferred_element_type=F32)
            for h in range(2):
                a, b = a2[:, h * 128 : (h + 1) * 128], b2[:, h * 128 : (h + 1) * 128]
                cols = slice(n * 256 + h * 128, n * 256 + (h + 1) * 128)
                out_ref[re, cols] = (a * cos - b * sin).astype(BF16)
                out_ref[im, cols] = (a * sin + b * cos).astype(BF16)
        return carry

    lax.fori_loop(0, WIN * per, body, 0)


def rotate(place, halves, own0, own1, turn):
    return pl.pallas_call(
        functools.partial(rotate_kernel, halves),
        in_specs=[SMEM, VMEM, VMEM, HBM],
        out_specs=[VMEM, VMEM],
        out_shape=[jax.ShapeDtypeStruct((SPEC, SIDE), BF16), TOKEN],
        scratch_shapes=[
            pltpu.VMEM((2 * FREQS, 128), F32),
            pltpu.VMEM((2 * QC, SPEC), BF16),
            pltpu.VMEM((SPEC, 2 * QC), BF16),
            pltpu.VMEM((2 * QC, SIDE), BF16),
            pltpu.SemaphoreType.DMA((1,)),
        ],
        compiler_params=pltpu.CompilerParams(vmem_limit_bytes=8 * MIB),
        cost_estimate=SMALL,
    )(place, own0, own1, turn)


def matmul_kernel(sources, n_in, place_ref, *refs):
    rot_refs = refs[n_in : n_in + 2]
    out_ref, token_ref, left, acc, in_sem, out_sem = refs[-6:]
    z, xh, y, xl, core = (place_ref[i] for i in range(5))
    loads, begin = [], 0
    for n in range(n_in):
        rows = refs[n].shape[0]
        loads.append(pltpu.make_async_copy(refs[n], left.at[pl.ds(begin, rows)], in_sem.at[n]))
        begin += rows
    for c in loads:
        c.start()
    token_ref[...] = jnp.zeros_like(token_ref)
    ids = []
    for other, offsets, dq in sources:
        c = 1 - core if other else core
        for dp, dx in offsets:
            p = lax.rem(jnp.where(c == 0, y, z) + dp + 4, 4)
            q = lax.rem(jnp.where(c == 0, z, y) + dq + 4, 4)
            block = (jnp.where(c == 0, q, p) * NXH + lax.rem(xh + dx, NXH)) * NY + jnp.where(c == 0, p, q)
            ids.append(block * 2 + c)
    for c in loads:
        c.wait()

    def stores(step):
        chip, part = divmod(step, SIDE // NT)
        cols = pl.ds(pl.multiple_of((1 - xl if chip else xl) * SIDE + part * NT, NT), NT)
        slot = step % 2
        return [
            pltpu.make_async_copy(acc.at[slot, u], out_ref.at[i, :, cols], out_sem.at[slot, u])
            for u, i in enumerate(ids)
        ]

    for step in range(TILES):
        if step >= 2:
            for c in stores(step - 2):
                c.wait()
        chip, part = divmod(step, SIDE // NT)
        tile = rot_refs[chip][:, part * NT : (part + 1) * NT]
        product = jnp.dot(left[...], tile, preferred_element_type=F32)
        acc[step % 2] = product.reshape(acc.shape[1:])
        for c in stores(step):
            c.start()
    for step in range(TILES - 2, TILES):
        for c in stores(step):
            c.wait()


def matmul(place, carried, rotated, out):
    arrays = [value for value, _, _, _ in carried]
    sources = [(other, at, dq) for _, other, at, dq in carried]
    rows = sum(len(at) for _, _, at, _ in carried) * HALF
    operands = [place, *arrays, *rotated]
    in_specs = [SMEM] + [ANY] * len(arrays) + [VMEM] * 2
    aliases = {}
    if out is not None:
        aliases = {len(operands): 0}
        operands.append(out)
        in_specs.append(ANY)
    return pl.pallas_call(
        functools.partial(matmul_kernel, sources, len(arrays)),
        in_specs=in_specs,
        out_specs=[ANY, VMEM],
        scratch_shapes=[
            pltpu.VMEM((rows, SPEC), BF16),
            pltpu.VMEM((2, rows // HALF, HALF, NT), F32),
            pltpu.SemaphoreType.DMA((len(sources),)),
            pltpu.SemaphoreType.DMA((2, rows // HALF)),
        ],
        out_shape=[jax.ShapeDtypeStruct((NZ * NXH * NY * 2, HALF, COLS), F32), TOKEN],
        input_output_aliases=aliases,
        compiler_params=pltpu.CompilerParams(vmem_limit_bytes=12 * MIB),
        cost_estimate=SMALL,
    )(*operands)


def permuted(value, move):
    sizes = (NZ, NXH, NY, NXL, NCORE)
    pairs = []
    for source in range(DEVICES):
        place = np.unravel_index(source, sizes)
        to = [int(t) % s for t, s in zip(move(*(int(p) for p in place)), sizes, strict=True)]
        pairs.append((source, int(np.ravel_multi_index(to, sizes))))
    return lax.ppermute(value, ("blk", "freq"), pairs)


def first(value, d):
    return permuted(value, lambda z, xh, y, xl, c: (z + d * c, xh, y + d * (1 - c), xl, c))


def second(value, d, swap=0):
    return permuted(value, lambda z, xh, y, xl, c: (z + d * (1 - c), xh, y + d * c, xl, c + swap))


def across(value):
    return permuted(value, lambda z, xh, y, xl, c: (z, xh + 1, y, xl, c))


def sibling(value):
    return permuted(value, lambda z, xh, y, xl, c: (z, xh, y, xl, c + 1))


def neighbour(value):
    return permuted(value, lambda z, xh, y, xl, c: (z, xh, y, xl + 1, c))


def local(raw, seg_chan, seg_win, file_count):
    basis, taper, turn = (jnp.asarray(t) for t in tables())
    blk, freq = lax.axis_index("blk"), lax.axis_index("freq")
    z, xh, y = blk // (NXH * NY), blk // NY % NXH, blk % NY
    place = jnp.stack([z, xh, y, freq // NCORE, freq % NCORE]).astype(jnp.int32)

    packed = pl.pallas_call(
        pack_kernel,
        in_specs=[SMEM, HBM, HBM, HBM],
        out_specs=VMEM,
        out_shape=jax.ShapeDtypeStruct((SLOTS, SAMPLES + TAIL), BF16),
        scratch_shapes=[
            pltpu.VMEM((1, SLOTS), jnp.int32),
            pltpu.VMEM((1, SLOTS), jnp.int32),
            pltpu.VMEM((SLOTS, SAMPLES), BF16),
            pltpu.SemaphoreType.DMA((3,)),
        ],
        compiler_params=pltpu.CompilerParams(vmem_limit_bytes=8 * MIB),
    )(file_count, seg_chan.reshape(1, SLOTS), seg_win.reshape(1, SLOTS), raw)
    arrived = lax.all_to_all(
        packed.reshape(DEVICES, SLOTS // DEVICES, SAMPLES + TAIL),
        ("blk", "freq"),
        split_axis=0,
        concat_axis=0,
        tiled=True,
    ).reshape(SLOTS, SAMPLES + TAIL)
    basis, taper = pl.pallas_call(
        fetch_kernel,
        in_specs=[ANY, HBM, HBM],
        out_specs=[VMEM] * 2,
        out_shape=[jax.ShapeDtypeStruct(t.shape, t.dtype) for t in (basis, taper)],
        scratch_shapes=[pltpu.SemaphoreType.DMA((2,))],
        compiler_params=pltpu.CompilerParams(vmem_limit_bytes=MIB),
        cost_estimate=SMALL,
    )(packed, basis, taper)
    white = pl.pallas_call(
        whiten_kernel,
        in_specs=[SMEM] + [VMEM] * 3,
        out_specs=VMEM,
        out_shape=jax.ShapeDtypeStruct((QC, SPEC), BF16),
        compiler_params=pltpu.CompilerParams(vmem_limit_bytes=8 * MIB),
    )(place, arrived, basis, taper)

    sib = sibling(white)
    unit = jnp.concatenate([white[:HALF], sib[HALF:]], axis=0)
    beyond = across(unit)
    ahead, behind = first(unit, 1), first(unit, -1)
    opposite = first(unit, 2)
    near_side, token = rotate(place, [(0, 0), (0, 1), (1, 1), (1, 0)], white, sib, turn)
    beyond_ahead, beyond_behind, beyond_opposite = first(beyond, 1), first(beyond, -1), first(beyond, 2)
    (turned,) = grouped([(0, h, 0, h) for h in range(2)], [2], [unit], [ahead, behind, opposite, token])
    facing = neighbour(turned)
    facing_sib = sibling(facing)
    arrays = [unit, ahead, behind, opposite, beyond, beyond_ahead, beyond_behind, beyond_opposite]
    line_at = [(0, 0), (-1, 0), (1, 0), (2, 0), (0, 1), (-1, 1), (1, 1), (2, 1)]
    moves = [(i, h, h, i) for i in range(8) for h in range(2)]
    moves += [(i, h, h + 2, p) for i, h, _, p in moves]
    kept, given, later_kept, later_given = grouped(moves, [8] * 4, arrays, [facing])
    far_side, _ = rotate(place, [(0, 0), (1, 0), (1, 1), (0, 1)], facing, facing_sib, turn)
    rotated = (near_side, far_side)
    kept_up, given_down = second(kept, 1), second(given, -1, swap=1)
    later_kept, later_given = gated(later_kept, [facing_sib]), gated(later_given, [facing_sib])
    kept_down, given_up = second(later_kept, -1), second(later_given, 1, swap=1)

    def product(out, *carried):
        return matmul(place, [(value, other, line_at, dq) for value, other, dq in carried], rotated, out)

    out, done = product(None, (kept, False, 0), (sibling(given), True, 0))
    kept_up, given_down = gated(kept_up, [done]), gated(given_down, [done])
    kept_far, given_far = second(kept_up, 1), first(given_down, -1)
    out, _ = product(out, (kept_up, False, -1), (given_down, True, 1))
    out, _ = product(out, (kept_down, False, 1), (given_up, True, -1))
    out, _ = product(out, (kept_far, False, -2), (given_far, True, 2))
    return out.reshape(NZ * NXH * NY, QC, COLS)


def solution(mesh):
    in_specs = (
        P(("blk", "freq"), None),
        P(("blk", "freq")),
        P(("blk", "freq")),
        P(("blk", "freq")),
    )
    out_specs = P(None, "freq", "blk")
    return jax.shard_map(local, mesh=mesh, in_specs=in_specs, out_specs=out_specs, check_vma=False)
```

```python
import functools
import math

import jax
import jax.numpy as jnp
import ml_dtypes
import numpy as np
from jax import lax
from jax.experimental import pallas as pl
from jax.experimental.pallas import tpu as pltpu
from jax.sharding import PartitionSpec as P

SAMPLES = 1024
FREQS = 512
FINE = 64
LAGS = 16
HALFWIN = 64
WIN = 4
EPSILON = 1e-06

NZ, NXH, NY = 4, 2, 4
NXL, NCORE = 2, 2
QC = 32
HALF = QC // 2
CB = QC * NXL * NCORE
SEG_DEV = QC * WIN
SLOTS = 256
DEVICES = 128
SPEC = WIN * 2 * FREQS
COLS = CB * LAGS
SIDE = COLS // NXL
TAIL = 128
NT = 1024
TILES = COLS // NT
GROUP = 4
F32, BF16 = jnp.float32, jnp.bfloat16
MIB = 1024 * 1024
SMALL = pl.CostEstimate(flops=1024, bytes_accessed=1024, transcendentals=0)
TOKEN = jax.ShapeDtypeStruct((8, 128), F32)
ANY = pl.BlockSpec(memory_space=pl.ANY)
HBM = pl.BlockSpec(memory_space=pltpu.HBM)
VMEM = pl.BlockSpec(memory_space=pltpu.VMEM)
SMEM = pl.BlockSpec(memory_space=pltpu.SMEM)


def tables():
    n = np.arange(SAMPLES)[:, None]
    k = np.arange(FREQS)[None, :]
    angle = 2.0 * math.pi / SAMPLES * ((n * k) % SAMPLES)
    basis = np.concatenate([np.cos(angle), -np.sin(angle)], axis=1).astype(ml_dtypes.bfloat16)
    taper = (0.5 - 0.5 * np.cos(2.0 * math.pi / SAMPLES * (n[:, 0] + 0.5)))[None, :].astype(np.float32)
    lag = np.arange(128)[None, :] % LAGS - LAGS // 2
    coarse = 2.0 * math.pi / SAMPLES * ((lag * FINE * np.arange(FREQS // FINE)[:, None]) % SAMPLES)
    fine = 2.0 * math.pi / SAMPLES * ((lag * np.arange(FINE)[:, None]) % SAMPLES)
    gain = 2.0 / math.sqrt(2.0 * WIN * FREQS)
    turn = np.concatenate([np.cos(coarse), np.sin(coarse), gain * np.cos(fine), gain * np.sin(fine)], axis=0)
    turn = turn.astype(np.float32)
    return basis, taper, turn


def diagonal(size):
    return lax.broadcasted_iota(jnp.int32, (size, size), 0) == lax.broadcasted_iota(jnp.int32, (size, size), 1)


def pack_kernel(count_ref, key_ref, raw_ref, out_ref):
    key = key_ref[...]
    chan = key // WIN
    slot = lax.broadcasted_iota(jnp.int32, (1, SLOTS), 1)
    live = slot < count_ref[0]
    owner = jnp.where(live, chan // QC, -1).astype(F32)
    owner_col = jnp.sum(jnp.where(diagonal(SLOTS), owner, 0.0), axis=1, keepdims=True)
    row = lax.broadcasted_iota(jnp.int32, (SLOTS, SLOTS), 0)
    col = lax.broadcasted_iota(jnp.int32, (SLOTS, SLOTS), 1)
    earlier = jnp.where((owner_col == owner) & (row < col), 1.0, 0.0)
    rank = jnp.sum(earlier, axis=0, keepdims=True)
    flat = jnp.where(live, owner * 2.0 + rank, -1.0)
    pick = jnp.where(flat == row.astype(F32), 1.0, 0.0)
    place = (key % WIN * QC + chan % QC + 1).astype(F32)
    place_col = jnp.sum(pick * place, axis=1, keepdims=True)
    out_ref[:, SAMPLES:] = jnp.broadcast_to(place_col, (SLOTS, TAIL)).astype(BF16)
    out_ref[:, :SAMPLES] = jnp.dot(pick.astype(BF16), raw_ref[...], preferred_element_type=F32).astype(BF16)


def fetch_kernel(after_hbm, basis_hbm, taper_hbm, turn_hbm, basis_ref, taper_ref, turn_ref, sem):
    del after_hbm
    loads = [
        pltpu.make_async_copy(basis_hbm, basis_ref, sem.at[0]),
        pltpu.make_async_copy(taper_hbm, taper_ref, sem.at[1]),
        pltpu.make_async_copy(turn_hbm, turn_ref, sem.at[2]),
    ]
    for c in loads:
        c.start()
    for c in loads:
        c.wait()


def band_mean(energy):
    row = lax.broadcasted_iota(jnp.int32, (FREQS, FREQS), 0)
    col = lax.broadcasted_iota(jnp.int32, (FREQS, FREQS), 1)
    inside = jnp.where(jnp.abs(row - col) <= HALFWIN, 1.0, 0.0).astype(BF16)
    high = energy.astype(BF16)
    left = energy - high.astype(F32)
    middle = left.astype(BF16)
    low = (left - middle.astype(F32)).astype(BF16)
    total = jnp.dot(low, inside, preferred_element_type=F32)
    total = total + jnp.dot(middle, inside, preferred_element_type=F32)
    total = total + jnp.dot(high, inside, preferred_element_type=F32)
    pos = lax.broadcasted_iota(jnp.int32, (1, FREQS), 1)
    count = jnp.minimum(pos, HALFWIN) + jnp.minimum(FREQS - 1 - pos, HALFWIN) + 1
    return total / count.astype(F32)


def whiten_kernel(place_ref, recv_ref, basis_ref, taper_ref, out_ref):
    place_col = recv_ref[:, SAMPLES : SAMPLES + 1].astype(F32)
    place = jnp.sum(jnp.where(diagonal(SLOTS), place_col, 0.0), axis=0, keepdims=True)
    row = lax.broadcasted_iota(jnp.int32, (SEG_DEV, SLOTS), 0)
    wanted = row // QC * QC + (row + place_ref[4] * HALF) % QC + 1
    pick = jnp.where(place == wanted.astype(F32), 1.0, 0.0).astype(BF16)
    values = jnp.dot(pick, recv_ref[:, :SAMPLES], preferred_element_type=F32)
    values = values - jnp.sum(values, axis=1, keepdims=True) * (1.0 / SAMPLES)
    tapered = (values * taper_ref[...]).astype(BF16)
    spectrum = jnp.dot(tapered, basis_ref[...], preferred_element_type=F32)
    real, imag = spectrum[:, :FREQS], spectrum[:, FREQS:]
    inverse = lax.rsqrt(band_mean(real * real + imag * imag) + EPSILON)
    real, imag = (real * inverse).astype(BF16), (imag * inverse).astype(BF16)
    for w in range(WIN):
        rows = slice(w * QC, (w + 1) * QC)
        out_ref[:, 2 * w * FREQS : (2 * w + 1) * FREQS] = real[rows]
        out_ref[:, (2 * w + 1) * FREQS : (2 * w + 2) * FREQS] = imag[rows]


def group_kernel(moves, n_in, *refs):
    outs = refs[n_in:]
    for i, h, o, p in moves:
        outs[o][p * HALF : (p + 1) * HALF, :] = refs[i][h * HALF : (h + 1) * HALF, :]


def grouped(moves, halves, arrays, after):
    return pl.pallas_call(
        functools.partial(group_kernel, moves, len(arrays) + len(after)),
        in_specs=[VMEM] * len(arrays) + [ANY] * len(after),
        out_specs=[VMEM] * len(halves),
        out_shape=[jax.ShapeDtypeStruct((n * HALF, SPEC), BF16) for n in halves],
        compiler_params=pltpu.CompilerParams(vmem_limit_bytes=MIB),
        cost_estimate=pl.CostEstimate(flops=0, bytes_accessed=2 * MIB, transcendentals=0),
    )(*arrays, *after)


def gate_kernel(*refs):
    del refs


def gated(value, after):
    return pl.pallas_call(
        gate_kernel,
        in_specs=[ANY] * (1 + len(after)),
        out_specs=ANY,
        out_shape=jax.ShapeDtypeStruct(value.shape, value.dtype),
        input_output_aliases={0: 0},
        compiler_params=pltpu.CompilerParams(vmem_limit_bytes=MIB),
        cost_estimate=SMALL,
    )(value, *after)


def rotate_kernel(halves, place_ref, own0, own1, small_ref, out_ref, token_ref, turn_ref, whole, turned, expand):
    col = lax.broadcasted_iota(jnp.int32, (HALF, SIDE), 1) // LAGS
    row = lax.broadcasted_iota(jnp.int32, (HALF, SIDE), 0)
    for g, own in enumerate((own0, own1)):
        whole[g * QC : (g + 1) * QC, :] = own[...]
    for k in range(0, SPEC, FREQS):
        turned[k : k + FREQS, :] = whole[:, k : k + FREQS].T
    core = place_ref[4]
    for g, (other, flip) in enumerate(halves):
        base = (1 - core if other else core) * QC + (1 - core if flip else core) * HALF
        expand[g * HALF : (g + 1) * HALF, :] = jnp.where(col == base + row, 1.0, 0.0).astype(BF16)
    many = FREQS // FINE
    fine_cos = small_ref[2 * many : 2 * many + FINE, :]
    fine_sin = small_ref[2 * many + FINE :, :]
    first_half = jnp.where(lax.broadcasted_iota(jnp.int32, (FINE, 128), 0) == 0, 0.5, 1.0)
    for a in range(many):
        cos, sin = small_ref[a : a + 1, :], small_ref[many + a : many + a + 1, :]
        weight = first_half if a == 0 else 1.0
        turn_ref[a * FINE : (a + 1) * FINE, :] = (cos * fine_cos - sin * fine_sin) * weight
        turn_ref[FREQS + a * FINE : FREQS + (a + 1) * FINE, :] = (sin * fine_cos + cos * fine_sin) * weight
    token_ref[...] = jnp.zeros_like(token_ref)
    step = 256
    per = FREQS // step

    def body(s, carry):
        w, k0 = s // per, pl.multiple_of(lax.rem(s, per) * step, step)
        re = pl.ds(pl.multiple_of(w * 2 * FREQS + k0, step), step)
        im = pl.ds(pl.multiple_of((w * 2 + 1) * FREQS + k0, step), step)
        cos = turn_ref[pl.ds(k0, step), :]
        sin = turn_ref[pl.ds(FREQS + k0, step), :]
        for n in range(SIDE // 256):
            a2 = jnp.dot(turned[re, :], expand[:, n * 256 : (n + 1) * 256], preferred_element_type=F32)
            b2 = jnp.dot(turned[im, :], expand[:, n * 256 : (n + 1) * 256], preferred_element_type=F32)
            for h in range(2):
                a, b = a2[:, h * 128 : (h + 1) * 128], b2[:, h * 128 : (h + 1) * 128]
                cols = slice(n * 256 + h * 128, n * 256 + (h + 1) * 128)
                out_ref[re, cols] = (a * cos - b * sin).astype(BF16)
                out_ref[im, cols] = (a * sin + b * cos).astype(BF16)
        return carry

    lax.fori_loop(0, WIN * per, body, 0)


def rotate(place, halves, own0, own1, turn):
    return pl.pallas_call(
        functools.partial(rotate_kernel, halves),
        in_specs=[SMEM, VMEM, VMEM, VMEM],
        out_specs=[VMEM, VMEM],
        out_shape=[jax.ShapeDtypeStruct((SPEC, SIDE), BF16), TOKEN],
        scratch_shapes=[
            pltpu.VMEM((2 * FREQS, 128), F32),
            pltpu.VMEM((2 * QC, SPEC), BF16),
            pltpu.VMEM((SPEC, 2 * QC), BF16),
            pltpu.VMEM((2 * QC, SIDE), BF16),
        ],
        compiler_params=pltpu.CompilerParams(vmem_limit_bytes=8 * MIB),
        cost_estimate=SMALL,
    )(place, own0, own1, turn)


def matmul_kernel(sources, n_in, place_ref, *refs):
    rot_refs = refs[n_in : n_in + 2]
    out_ref, token_ref, left, acc, in_sem, out_sem = refs[-6:]
    z, xh, y, xl, core = (place_ref[i] for i in range(5))
    loads, begin = [], 0
    for n in range(n_in):
        rows = refs[n].shape[0]
        loads.append(pltpu.make_async_copy(refs[n], left.at[pl.ds(begin, rows)], in_sem.at[n]))
        begin += rows
    for c in loads:
        c.start()
    token_ref[...] = jnp.zeros_like(token_ref)
    ids = []
    for other, offsets, dq in sources:
        c = 1 - core if other else core
        for dp, dx in offsets:
            p = lax.rem(jnp.where(c == 0, y, z) + dp + 4, 4)
            q = lax.rem(jnp.where(c == 0, z, y) + dq + 4, 4)
            block = (jnp.where(c == 0, q, p) * NXH + lax.rem(xh + dx, NXH)) * NY + jnp.where(c == 0, p, q)
            ids.append(block * 2 + c)
    for c in loads:
        c.wait()

    def stores(step):
        chip, part = divmod(step, SIDE // NT)
        cols = pl.ds(pl.multiple_of((1 - xl if chip else xl) * SIDE + part * NT, NT), NT)
        slot = step % 2
        return [
            pltpu.make_async_copy(acc.at[slot, u], out_ref.at[i, :, cols], out_sem.at[slot, u])
            for u, i in enumerate(ids)
        ]

    for step in range(TILES):
        if step >= 2:
            for c in stores(step - 2):
                c.wait()
        chip, part = divmod(step, SIDE // NT)
        tile = rot_refs[chip][:, part * NT : (part + 1) * NT]
        product = jnp.dot(left[...], tile, preferred_element_type=F32)
        acc[step % 2] = product.reshape(acc.shape[1:])
        for c in stores(step):
            c.start()
    for step in range(TILES - 2, TILES):
        for c in stores(step):
            c.wait()


def matmul(place, carried, rotated, out):
    arrays = [value for value, _, _, _ in carried]
    sources = [(other, at, dq) for _, other, at, dq in carried]
    rows = sum(len(at) for _, _, at, _ in carried) * HALF
    operands = [place, *arrays, *rotated]
    in_specs = [SMEM] + [ANY] * len(arrays) + [VMEM] * 2
    aliases = {}
    if out is not None:
        aliases = {len(operands): 0}
        operands.append(out)
        in_specs.append(ANY)
    return pl.pallas_call(
        functools.partial(matmul_kernel, sources, len(arrays)),
        in_specs=in_specs,
        out_specs=[ANY, VMEM],
        scratch_shapes=[
            pltpu.VMEM((rows, SPEC), BF16),
            pltpu.VMEM((2, rows // HALF, HALF, NT), F32),
            pltpu.SemaphoreType.DMA((len(sources),)),
            pltpu.SemaphoreType.DMA((2, rows // HALF)),
        ],
        out_shape=[jax.ShapeDtypeStruct((NZ * NXH * NY * 2, HALF, COLS), F32), TOKEN],
        input_output_aliases=aliases,
        compiler_params=pltpu.CompilerParams(vmem_limit_bytes=12 * MIB),
        cost_estimate=SMALL,
    )(*operands)


def permuted(value, move):
    sizes = (NZ, NXH, NY, NXL, NCORE)
    pairs = []
    for source in range(DEVICES):
        place = np.unravel_index(source, sizes)
        to = [int(t) % s for t, s in zip(move(*(int(p) for p in place)), sizes, strict=True)]
        pairs.append((source, int(np.ravel_multi_index(to, sizes))))
    return lax.ppermute(value, ("blk", "freq"), pairs)


def first(value, d):
    return permuted(value, lambda z, xh, y, xl, c: (z + d * c, xh, y + d * (1 - c), xl, c))


def second(value, d, swap=0):
    return permuted(value, lambda z, xh, y, xl, c: (z + d * (1 - c), xh, y + d * c, xl, c + swap))


def across(value):
    return permuted(value, lambda z, xh, y, xl, c: (z, xh + 1, y, xl, c))


def sibling(value):
    return permuted(value, lambda z, xh, y, xl, c: (z, xh, y, xl, c + 1))


def neighbour(value):
    return permuted(value, lambda z, xh, y, xl, c: (z, xh, y, xl + 1, c))


def local(raw, seg_chan, seg_win, file_count):
    basis, taper, turn = (jnp.asarray(t) for t in tables())
    blk, freq = lax.axis_index("blk"), lax.axis_index("freq")
    z, xh, y = blk // (NXH * NY), blk // NY % NXH, blk % NY
    place = jnp.stack([z, xh, y, freq // NCORE, freq % NCORE]).astype(jnp.int32)

    packed = pl.pallas_call(
        pack_kernel,
        in_specs=[SMEM, VMEM, VMEM],
        out_specs=VMEM,
        out_shape=jax.ShapeDtypeStruct((SLOTS, SAMPLES + TAIL), BF16),
        compiler_params=pltpu.CompilerParams(vmem_limit_bytes=8 * MIB),
    )(file_count, (seg_chan * WIN + seg_win).reshape(1, SLOTS), raw)
    arrived = lax.all_to_all(
        packed.reshape(DEVICES, SLOTS // DEVICES, SAMPLES + TAIL),
        ("blk", "freq"),
        split_axis=0,
        concat_axis=0,
        tiled=True,
    ).reshape(SLOTS, SAMPLES + TAIL)
    basis, taper, turn = pl.pallas_call(
        fetch_kernel,
        in_specs=[ANY, HBM, HBM, HBM],
        out_specs=[VMEM] * 3,
        out_shape=[jax.ShapeDtypeStruct(t.shape, t.dtype) for t in (basis, taper, turn)],
        scratch_shapes=[pltpu.SemaphoreType.DMA((3,))],
        compiler_params=pltpu.CompilerParams(vmem_limit_bytes=MIB),
        cost_estimate=SMALL,
    )(packed, basis, taper, turn)
    white = pl.pallas_call(
        whiten_kernel,
        in_specs=[SMEM] + [VMEM] * 3,
        out_specs=VMEM,
        out_shape=jax.ShapeDtypeStruct((QC, SPEC), BF16),
        compiler_params=pltpu.CompilerParams(vmem_limit_bytes=8 * MIB),
    )(place, arrived, basis, taper)

    sib = sibling(white)
    unit = jnp.concatenate([white[:HALF], sib[HALF:]], axis=0)
    beyond = across(unit)
    ahead, behind = first(unit, 1), first(unit, -1)
    opposite = first(unit, 2)
    near_side, token = rotate(place, [(0, 0), (0, 1), (1, 1), (1, 0)], white, sib, turn)
    beyond_ahead, beyond_behind, beyond_opposite = first(beyond, 1), first(beyond, -1), first(beyond, 2)
    (turned,) = grouped([(0, h, 0, h) for h in range(2)], [2], [unit], [ahead, behind, opposite, token])
    facing = neighbour(turned)
    facing_sib = sibling(facing)
    arrays = [unit, ahead, behind, opposite, beyond, beyond_ahead, beyond_behind, beyond_opposite]
    line_at = [(0, 0), (-1, 0), (1, 0), (2, 0), (0, 1), (-1, 1), (1, 1), (2, 1)]
    moves = [(i, h, h, i) for i in range(8) for h in range(2)]
    moves += [(i, h, h + 2, p) for i, h, _, p in moves]
    kept, given, later_kept, later_given = grouped(moves, [8] * 4, arrays, [facing])
    far_side, _ = rotate(place, [(0, 0), (1, 0), (1, 1), (0, 1)], facing, facing_sib, turn)
    rotated = (near_side, far_side)
    kept_up, given_down = second(kept, 1), second(given, -1, swap=1)
    later_kept, later_given = gated(later_kept, [facing_sib]), gated(later_given, [facing_sib])
    kept_down, given_up = second(later_kept, -1), second(later_given, 1, swap=1)

    def product(out, *carried):
        return matmul(place, [(value, other, line_at, dq) for value, other, dq in carried], rotated, out)

    out, done = product(None, (kept, False, 0), (sibling(given), True, 0))
    kept_up, given_down = gated(kept_up, [done]), gated(given_down, [done])
    kept_far, given_far = second(kept_up, 1), first(given_down, -1)
    out, _ = product(out, (kept_up, False, -1), (given_down, True, 1))
    out, _ = product(out, (kept_down, False, 1), (given_up, True, -1))
    out, _ = product(out, (kept_far, False, -2), (given_far, True, 2))
    return out.reshape(NZ * NXH * NY, QC, COLS)


def solution(mesh):
    in_specs = (
        P(("blk", "freq"), None),
        P(("blk", "freq")),
        P(("blk", "freq")),
        P(("blk", "freq")),
    )
    out_specs = P(None, "freq", "blk")
    return jax.shard_map(local, mesh=mesh, in_specs=in_specs, out_specs=out_specs, check_vma=False)
```

```python
import functools
import math

import jax
import jax.numpy as jnp
import ml_dtypes
import numpy as np
from jax import lax
from jax.experimental import pallas as pl
from jax.experimental.pallas import tpu as pltpu
from jax.sharding import PartitionSpec as P

SAMPLES = 1024
FREQS = 512
FINE = 64
LAGS = 16
HALFWIN = 64
WIN = 4
EPSILON = 1e-06

NZ, NXH, NY = 4, 2, 4
NXL, NCORE = 2, 2
QC = 32
HALF = QC // 2
CB = QC * NXL * NCORE
SEG_DEV = QC * WIN
SLOTS = 256
DEVICES = 128
SPEC = WIN * 2 * FREQS
COLS = CB * LAGS
SIDE = COLS // NXL
TAIL = 128
NT = 1024
TILES = COLS // NT
GROUP = 4
F32, BF16 = jnp.float32, jnp.bfloat16
MIB = 1024 * 1024
SMALL = pl.CostEstimate(flops=1024, bytes_accessed=1024, transcendentals=0)
TOKEN = jax.ShapeDtypeStruct((8, 128), F32)
ANY = pl.BlockSpec(memory_space=pl.ANY)
HBM = pl.BlockSpec(memory_space=pltpu.HBM)
VMEM = pl.BlockSpec(memory_space=pltpu.VMEM)
SMEM = pl.BlockSpec(memory_space=pltpu.SMEM)


def tables():
    n = np.arange(SAMPLES)[:, None]
    k = np.arange(FREQS)[None, :]
    angle = 2.0 * math.pi / SAMPLES * ((n * k) % SAMPLES)
    basis = np.concatenate([np.cos(angle), -np.sin(angle)], axis=1).astype(ml_dtypes.bfloat16)
    taper = (0.5 - 0.5 * np.cos(2.0 * math.pi / SAMPLES * (n[:, 0] + 0.5)))[None, :].astype(np.float32)
    lag = np.arange(128)[None, :] % LAGS - LAGS // 2
    coarse = 2.0 * math.pi / SAMPLES * ((lag * FINE * np.arange(FREQS // FINE)[:, None]) % SAMPLES)
    fine = 2.0 * math.pi / SAMPLES * ((lag * np.arange(FINE)[:, None]) % SAMPLES)
    gain = 2.0 / math.sqrt(2.0 * WIN * FREQS)
    turn = np.concatenate([np.cos(coarse), np.sin(coarse), gain * np.cos(fine), gain * np.sin(fine)], axis=0)
    turn = turn.astype(np.float32)
    return basis, taper, turn


def diagonal(size):
    return lax.broadcasted_iota(jnp.int32, (size, size), 0) == lax.broadcasted_iota(jnp.int32, (size, size), 1)


def pack_kernel(count_ref, key_ref, raw_ref, out_ref):
    key = key_ref[...]
    chan = key // WIN
    slot = lax.broadcasted_iota(jnp.int32, (1, SLOTS), 1)
    live = slot < count_ref[0]
    owner = jnp.where(live, chan // QC, -1).astype(F32)
    owner_col = jnp.sum(jnp.where(diagonal(SLOTS), owner, 0.0), axis=1, keepdims=True)
    row = lax.broadcasted_iota(jnp.int32, (SLOTS, SLOTS), 0)
    col = lax.broadcasted_iota(jnp.int32, (SLOTS, SLOTS), 1)
    earlier = jnp.where((owner_col == owner) & (row < col), 1.0, 0.0)
    rank = jnp.sum(earlier, axis=0, keepdims=True)
    flat = jnp.where(live, owner * 2.0 + rank, -1.0)
    pick = jnp.where(flat == row.astype(F32), 1.0, 0.0)
    place = (key % WIN * QC + chan % QC + 1).astype(F32)
    place_col = jnp.sum(pick * place, axis=1, keepdims=True)
    place_all = jnp.broadcast_to(place_col, (SLOTS, TAIL)).astype(BF16)
    out_ref[:, :, SAMPLES:] = place_all.reshape(DEVICES, SLOTS // DEVICES, TAIL)
    sent = jnp.dot(pick.astype(BF16), raw_ref[...], preferred_element_type=F32).astype(BF16)
    out_ref[:, :, :SAMPLES] = sent.reshape(DEVICES, SLOTS // DEVICES, SAMPLES)


def fetch_kernel(after_hbm, basis_hbm, taper_hbm, turn_hbm, basis_ref, taper_ref, turn_ref, sem):
    del after_hbm
    loads = [
        pltpu.make_async_copy(basis_hbm, basis_ref, sem.at[0]),
        pltpu.make_async_copy(taper_hbm, taper_ref, sem.at[1]),
        pltpu.make_async_copy(turn_hbm, turn_ref, sem.at[2]),
    ]
    for c in loads:
        c.start()
    for c in loads:
        c.wait()


def band_mean(energy):
    row = lax.broadcasted_iota(jnp.int32, (FREQS, FREQS), 0)
    col = lax.broadcasted_iota(jnp.int32, (FREQS, FREQS), 1)
    inside = jnp.where(jnp.abs(row - col) <= HALFWIN, 1.0, 0.0).astype(BF16)
    high = energy.astype(BF16)
    left = energy - high.astype(F32)
    middle = left.astype(BF16)
    low = (left - middle.astype(F32)).astype(BF16)
    rows = energy.shape[0]
    sums = jnp.dot(jnp.concatenate([low, middle, high], axis=0), inside, preferred_element_type=F32)
    total = sums[:rows] + sums[rows : 2 * rows] + sums[2 * rows :]
    pos = lax.broadcasted_iota(jnp.int32, (1, FREQS), 1)
    count = jnp.minimum(pos, HALFWIN) + jnp.minimum(FREQS - 1 - pos, HALFWIN) + 1
    return total / count.astype(F32)


def whiten_kernel(place_ref, recv_ref, basis_ref, taper_ref, out_ref):
    place_col = recv_ref[:, SAMPLES : SAMPLES + 1].astype(F32)
    place = jnp.sum(jnp.where(diagonal(SLOTS), place_col, 0.0), axis=0, keepdims=True)
    row = lax.broadcasted_iota(jnp.int32, (SEG_DEV, SLOTS), 0)
    wanted = row // QC * QC + (row + place_ref[4] * HALF) % QC + 1
    pick = jnp.where(place == wanted.astype(F32), 1.0, 0.0).astype(BF16)
    values = jnp.dot(pick, recv_ref[:, :SAMPLES], preferred_element_type=F32)
    values = values - jnp.sum(values, axis=1, keepdims=True) * (1.0 / SAMPLES)
    tapered = (values * taper_ref[...]).astype(BF16)
    spectrum = jnp.dot(tapered, basis_ref[...], preferred_element_type=F32)
    real, imag = spectrum[:, :FREQS], spectrum[:, FREQS:]
    inverse = lax.rsqrt(band_mean(real * real + imag * imag) + EPSILON)
    real, imag = (real * inverse).astype(BF16), (imag * inverse).astype(BF16)
    for w in range(WIN):
        rows = slice(w * QC, (w + 1) * QC)
        out_ref[:, 2 * w * FREQS : (2 * w + 1) * FREQS] = real[rows]
        out_ref[:, (2 * w + 1) * FREQS : (2 * w + 2) * FREQS] = imag[rows]


def group_kernel(moves, n_in, *refs):
    outs = refs[n_in:]
    for i, h, o, p in moves:
        outs[o][p * HALF : (p + 1) * HALF, :] = refs[i][h * HALF : (h + 1) * HALF, :]


def grouped(moves, halves, arrays, after):
    return pl.pallas_call(
        functools.partial(group_kernel, moves, len(arrays) + len(after)),
        in_specs=[VMEM] * len(arrays) + [ANY] * len(after),
        out_specs=[VMEM] * len(halves),
        out_shape=[jax.ShapeDtypeStruct((n * HALF, SPEC), BF16) for n in halves],
        compiler_params=pltpu.CompilerParams(vmem_limit_bytes=MIB),
        cost_estimate=pl.CostEstimate(flops=0, bytes_accessed=2 * MIB, transcendentals=0),
    )(*arrays, *after)


def gate_kernel(*refs):
    del refs


def gated(value, after):
    return pl.pallas_call(
        gate_kernel,
        in_specs=[ANY] * (1 + len(after)),
        out_specs=ANY,
        out_shape=jax.ShapeDtypeStruct(value.shape, value.dtype),
        input_output_aliases={0: 0},
        compiler_params=pltpu.CompilerParams(vmem_limit_bytes=MIB),
        cost_estimate=SMALL,
    )(value, *after)


def rotate_kernel(halves, place_ref, own0, own1, small_ref, out_ref, token_ref, turn_ref, whole, turned, expand):
    col = lax.broadcasted_iota(jnp.int32, (HALF, SIDE), 1) // LAGS
    row = lax.broadcasted_iota(jnp.int32, (HALF, SIDE), 0)
    for g, own in enumerate((own0, own1)):
        whole[g * QC : (g + 1) * QC, :] = own[...]
    for k in range(0, SPEC, FREQS):
        turned[k : k + FREQS, :] = whole[:, k : k + FREQS].T
    core = place_ref[4]
    for g, (other, flip) in enumerate(halves):
        base = (1 - core if other else core) * QC + (1 - core if flip else core) * HALF
        expand[g * HALF : (g + 1) * HALF, :] = jnp.where(col == base + row, 1.0, 0.0).astype(BF16)
    many = FREQS // FINE
    fine_cos = small_ref[2 * many : 2 * many + FINE, :]
    fine_sin = small_ref[2 * many + FINE :, :]
    first_half = jnp.where(lax.broadcasted_iota(jnp.int32, (FINE, 128), 0) == 0, 0.5, 1.0)
    for a in range(many):
        cos, sin = small_ref[a : a + 1, :], small_ref[many + a : many + a + 1, :]
        weight = first_half if a == 0 else 1.0
        turn_ref[a * FINE : (a + 1) * FINE, :] = (cos * fine_cos - sin * fine_sin) * weight
        turn_ref[FREQS + a * FINE : FREQS + (a + 1) * FINE, :] = (sin * fine_cos + cos * fine_sin) * weight
    token_ref[...] = jnp.zeros_like(token_ref)
    step = 256
    per = FREQS // step

    def body(s, carry):
        w, k0 = s // per, pl.multiple_of(lax.rem(s, per) * step, step)
        re = pl.ds(pl.multiple_of(w * 2 * FREQS + k0, step), step)
        im = pl.ds(pl.multiple_of((w * 2 + 1) * FREQS + k0, step), step)
        cos = turn_ref[pl.ds(k0, step), :]
        sin = turn_ref[pl.ds(FREQS + k0, step), :]
        for n in range(SIDE // 256):
            a2 = jnp.dot(turned[re, :], expand[:, n * 256 : (n + 1) * 256], preferred_element_type=F32)
            b2 = jnp.dot(turned[im, :], expand[:, n * 256 : (n + 1) * 256], preferred_element_type=F32)
            for h in range(2):
                a, b = a2[:, h * 128 : (h + 1) * 128], b2[:, h * 128 : (h + 1) * 128]
                cols = slice(n * 256 + h * 128, n * 256 + (h + 1) * 128)
                out_ref[re, cols] = (a * cos - b * sin).astype(BF16)
                out_ref[im, cols] = (a * sin + b * cos).astype(BF16)
        return carry

    lax.fori_loop(0, WIN * per, body, 0)


def rotate(place, halves, own0, own1, turn):
    return pl.pallas_call(
        functools.partial(rotate_kernel, halves),
        in_specs=[SMEM, VMEM, VMEM, VMEM],
        out_specs=[VMEM, VMEM],
        out_shape=[jax.ShapeDtypeStruct((SPEC, SIDE), BF16), TOKEN],
        scratch_shapes=[
            pltpu.VMEM((2 * FREQS, 128), F32),
            pltpu.VMEM((2 * QC, SPEC), BF16),
            pltpu.VMEM((SPEC, 2 * QC), BF16),
            pltpu.VMEM((2 * QC, SIDE), BF16),
        ],
        compiler_params=pltpu.CompilerParams(vmem_limit_bytes=8 * MIB),
        cost_estimate=SMALL,
    )(place, own0, own1, turn)


def matmul_kernel(sources, n_in, place_ref, *refs):
    rot_refs = refs[n_in : n_in + 2]
    out_ref, token_ref, left, acc, in_sem, out_sem = refs[-6:]
    z, xh, y, xl, core = (place_ref[i] for i in range(5))
    loads, begin = [], 0
    for n in range(n_in):
        rows = refs[n].shape[0]
        loads.append(pltpu.make_async_copy(refs[n], left.at[pl.ds(begin, rows)], in_sem.at[n]))
        begin += rows
    for c in loads:
        c.start()
    token_ref[...] = jnp.zeros_like(token_ref)
    ids = []
    for other, offsets, dq in sources:
        c = 1 - core if other else core
        for dp, dx in offsets:
            p = lax.rem(jnp.where(c == 0, y, z) + dp + 4, 4)
            q = lax.rem(jnp.where(c == 0, z, y) + dq + 4, 4)
            block = (jnp.where(c == 0, q, p) * NXH + lax.rem(xh + dx, NXH)) * NY + jnp.where(c == 0, p, q)
            ids.append(block * 2 + c)
    for c in loads:
        c.wait()

    def stores(step):
        chip, part = divmod(step, SIDE // NT)
        cols = pl.ds(pl.multiple_of((1 - xl if chip else xl) * SIDE + part * NT, NT), NT)
        slot = step % 2
        return [
            pltpu.make_async_copy(acc.at[slot, u], out_ref.at[i, :, cols], out_sem.at[slot, u])
            for u, i in enumerate(ids)
        ]

    for step in range(TILES):
        if step >= 2:
            for c in stores(step - 2):
                c.wait()
        chip, part = divmod(step, SIDE // NT)
        tile = rot_refs[chip][:, part * NT : (part + 1) * NT]
        product = jnp.dot(left[...], tile, preferred_element_type=F32)
        acc[step % 2] = product.reshape(acc.shape[1:])
        for c in stores(step):
            c.start()
    for step in range(TILES - 2, TILES):
        for c in stores(step):
            c.wait()


def matmul(place, carried, rotated, out):
    arrays = [value for value, _, _, _ in carried]
    sources = [(other, at, dq) for _, other, at, dq in carried]
    rows = sum(len(at) for _, _, at, _ in carried) * HALF
    operands = [place, *arrays, *rotated]
    in_specs = [SMEM] + [ANY] * len(arrays) + [VMEM] * 2
    aliases = {}
    if out is not None:
        aliases = {len(operands): 0}
        operands.append(out)
        in_specs.append(ANY)
    return pl.pallas_call(
        functools.partial(matmul_kernel, sources, len(arrays)),
        in_specs=in_specs,
        out_specs=[ANY, VMEM],
        scratch_shapes=[
            pltpu.VMEM((rows, SPEC), BF16),
            pltpu.VMEM((2, rows // HALF, HALF, NT), F32),
            pltpu.SemaphoreType.DMA((len(sources),)),
            pltpu.SemaphoreType.DMA((2, rows // HALF)),
        ],
        out_shape=[jax.ShapeDtypeStruct((NZ * NXH * NY * 2, HALF, COLS), F32), TOKEN],
        input_output_aliases=aliases,
        compiler_params=pltpu.CompilerParams(vmem_limit_bytes=12 * MIB),
        cost_estimate=SMALL,
    )(*operands)


def permuted(value, move):
    sizes = (NZ, NXH, NY, NXL, NCORE)
    pairs = []
    for source in range(DEVICES):
        place = np.unravel_index(source, sizes)
        to = [int(t) % s for t, s in zip(move(*(int(p) for p in place)), sizes, strict=True)]
        pairs.append((source, int(np.ravel_multi_index(to, sizes))))
    return lax.ppermute(value, ("blk", "freq"), pairs)


def first(value, d):
    return permuted(value, lambda z, xh, y, xl, c: (z + d * c, xh, y + d * (1 - c), xl, c))


def second(value, d, swap=0):
    return permuted(value, lambda z, xh, y, xl, c: (z + d * (1 - c), xh, y + d * c, xl, c + swap))


def across(value):
    return permuted(value, lambda z, xh, y, xl, c: (z, xh + 1, y, xl, c))


def sibling(value):
    return permuted(value, lambda z, xh, y, xl, c: (z, xh, y, xl, c + 1))


def neighbour(value):
    return permuted(value, lambda z, xh, y, xl, c: (z, xh, y, xl + 1, c))


def local(raw, seg_chan, seg_win, file_count):
    basis, taper, turn = (jnp.asarray(t) for t in tables())
    blk, freq = lax.axis_index("blk"), lax.axis_index("freq")
    z, xh, y = blk // (NXH * NY), blk // NY % NXH, blk % NY
    place = jnp.stack([z, xh, y, freq // NCORE, freq % NCORE]).astype(jnp.int32)

    packed = pl.pallas_call(
        pack_kernel,
        in_specs=[SMEM, VMEM, VMEM],
        out_specs=VMEM,
        out_shape=jax.ShapeDtypeStruct((DEVICES, SLOTS // DEVICES, SAMPLES + TAIL), BF16),
        compiler_params=pltpu.CompilerParams(vmem_limit_bytes=8 * MIB),
    )(file_count, (seg_chan * WIN + seg_win).reshape(1, SLOTS), raw)
    arrived = lax.all_to_all(
        packed,
        ("blk", "freq"),
        split_axis=0,
        concat_axis=0,
        tiled=True,
    ).reshape(SLOTS, SAMPLES + TAIL)
    basis, taper, turn = pl.pallas_call(
        fetch_kernel,
        in_specs=[ANY, HBM, HBM, HBM],
        out_specs=[VMEM] * 3,
        out_shape=[jax.ShapeDtypeStruct(t.shape, t.dtype) for t in (basis, taper, turn)],
        scratch_shapes=[pltpu.SemaphoreType.DMA((3,))],
        compiler_params=pltpu.CompilerParams(vmem_limit_bytes=MIB),
        cost_estimate=SMALL,
    )(packed, basis, taper, turn)
    white = pl.pallas_call(
        whiten_kernel,
        in_specs=[SMEM] + [VMEM] * 3,
        out_specs=VMEM,
        out_shape=jax.ShapeDtypeStruct((QC, SPEC), BF16),
        compiler_params=pltpu.CompilerParams(vmem_limit_bytes=8 * MIB),
    )(place, arrived, basis, taper)

    sib = sibling(white)
    unit = jnp.concatenate([white[:HALF], sib[HALF:]], axis=0)
    beyond = across(unit)
    ahead, behind = first(unit, 1), first(unit, -1)
    opposite = first(unit, 2)
    near_side, token = rotate(place, [(0, 0), (0, 1), (1, 1), (1, 0)], white, sib, turn)
    beyond_ahead, beyond_behind, beyond_opposite = first(beyond, 1), first(beyond, -1), first(beyond, 2)
    (turned,) = grouped([(0, h, 0, h) for h in range(2)], [2], [unit], [ahead, behind, opposite])
    facing = neighbour(turned)
    facing_sib = sibling(facing)
    arrays = [unit, ahead, behind, opposite, beyond, beyond_ahead, beyond_behind, beyond_opposite]
    line_at = [(0, 0), (-1, 0), (1, 0), (2, 0), (0, 1), (-1, 1), (1, 1), (2, 1)]
    moves = [(i, h, h, i) for i in range(8) for h in range(2)]
    moves += [(i, h, h + 2, p) for i, h, _, p in moves]
    kept, given, later_kept, later_given = grouped(moves, [8] * 4, arrays, [facing, token])
    far_side, _ = rotate(place, [(0, 0), (1, 0), (1, 1), (0, 1)], facing, facing_sib, turn)
    rotated = (near_side, far_side)
    kept_up, given_down = second(kept, 1), second(given, -1, swap=1)
    later_kept, later_given = gated(later_kept, [facing_sib]), gated(later_given, [facing_sib])
    kept_down, given_up = second(later_kept, -1), second(later_given, 1, swap=1)

    def product(out, *carried):
        return matmul(place, [(value, other, line_at, dq) for value, other, dq in carried], rotated, out)

    out, done = product(None, (kept, False, 0), (sibling(given), True, 0))
    kept_up, given_down = gated(kept_up, [done]), gated(given_down, [done])
    kept_far, given_far = second(kept_up, 1), first(given_down, -1)
    out, _ = product(out, (kept_up, False, -1), (given_down, True, 1))
    out, _ = product(out, (kept_down, False, 1), (given_up, True, -1))
    out, _ = product(out, (kept_far, False, -2), (given_far, True, 2))
    return out.reshape(NZ * NXH * NY, QC, COLS)


def solution(mesh):
    in_specs = (
        P(("blk", "freq"), None),
        P(("blk", "freq")),
        P(("blk", "freq")),
        P(("blk", "freq")),
    )
    out_specs = P(None, "freq", "blk")
    return jax.shard_map(local, mesh=mesh, in_specs=in_specs, out_specs=out_specs, check_vma=False)
```

```python
import functools
import math

import jax
import jax.numpy as jnp
import ml_dtypes
import numpy as np
from jax import lax
from jax.experimental import pallas as pl
from jax.experimental.pallas import tpu as pltpu
from jax.sharding import PartitionSpec as P

SAMPLES = 1024
FREQS = 512
FINE = 64
LAGS = 16
HALFWIN = 64
WIN = 4
EPSILON = 1e-06

NZ, NXH, NY = 4, 2, 4
NXL, NCORE = 2, 2
QC = 32
HALF = QC // 2
CB = QC * NXL * NCORE
SEG_DEV = QC * WIN
SLOTS = 256
DEVICES = 128
SPEC = WIN * 2 * FREQS
COLS = CB * LAGS
SIDE = COLS // NXL
TAIL = 128
NT = 1024
TILES = COLS // NT
GROUP = 4
F32, BF16 = jnp.float32, jnp.bfloat16
MIB = 1024 * 1024
SMALL = pl.CostEstimate(flops=1024, bytes_accessed=1024, transcendentals=0)
TOKEN = jax.ShapeDtypeStruct((8, 128), F32)
ANY = pl.BlockSpec(memory_space=pl.ANY)
HBM = pl.BlockSpec(memory_space=pltpu.HBM)
VMEM = pl.BlockSpec(memory_space=pltpu.VMEM)
SMEM = pl.BlockSpec(memory_space=pltpu.SMEM)


def tables():
    n = np.arange(SAMPLES)[:, None]
    k = np.arange(FREQS)[None, :]
    angle = 2.0 * math.pi / SAMPLES * ((n * k) % SAMPLES)
    basis = np.concatenate([np.cos(angle), -np.sin(angle)], axis=1).astype(ml_dtypes.bfloat16)
    taper = (0.5 - 0.5 * np.cos(2.0 * math.pi / SAMPLES * (n[:, 0] + 0.5)))[None, :].astype(np.float32)
    lag = np.arange(128)[None, :] % LAGS - LAGS // 2
    coarse = 2.0 * math.pi / SAMPLES * ((lag * FINE * np.arange(FREQS // FINE)[:, None]) % SAMPLES)
    fine = 2.0 * math.pi / SAMPLES * ((lag * np.arange(FINE)[:, None]) % SAMPLES)
    gain = 2.0 / math.sqrt(2.0 * WIN * FREQS)
    turn = np.concatenate([np.cos(coarse), np.sin(coarse), gain * np.cos(fine), gain * np.sin(fine)], axis=0)
    turn = turn.astype(np.float32)
    return basis, taper, turn


def diagonal(size):
    return lax.broadcasted_iota(jnp.int32, (size, size), 0) == lax.broadcasted_iota(jnp.int32, (size, size), 1)


def pack_kernel(count_ref, key_ref, raw_ref, out_ref):
    key = key_ref[...]
    chan = key // WIN
    slot = lax.broadcasted_iota(jnp.int32, (1, SLOTS), 1)
    live = slot < count_ref[0]
    owner = jnp.where(live, chan // QC, -1).astype(F32)
    owner_col = jnp.sum(jnp.where(diagonal(SLOTS), owner, 0.0), axis=1, keepdims=True)
    row = lax.broadcasted_iota(jnp.int32, (SLOTS, SLOTS), 0)
    col = lax.broadcasted_iota(jnp.int32, (SLOTS, SLOTS), 1)
    earlier = jnp.where((owner_col == owner) & (row < col), 1.0, 0.0)
    rank = jnp.sum(earlier, axis=0, keepdims=True)
    flat = jnp.where(live, owner * 2.0 + rank, -1.0)
    pick = jnp.where(flat == row.astype(F32), 1.0, 0.0)
    place = (key % WIN * QC + chan % QC + 1).astype(F32)
    place_col = jnp.sum(pick * place, axis=1, keepdims=True)
    out_ref[:, SAMPLES:] = jnp.broadcast_to(place_col, (SLOTS, TAIL)).astype(BF16)
    out_ref[:, :SAMPLES] = jnp.dot(pick.astype(BF16), raw_ref[...], preferred_element_type=F32).astype(BF16)


def fetch_kernel(after_hbm, basis_hbm, taper_hbm, turn_hbm, basis_ref, taper_ref, turn_ref, sem):
    del after_hbm
    loads = [
        pltpu.make_async_copy(basis_hbm, basis_ref, sem.at[0]),
        pltpu.make_async_copy(taper_hbm, taper_ref, sem.at[1]),
        pltpu.make_async_copy(turn_hbm, turn_ref, sem.at[2]),
    ]
    for c in loads:
        c.start()
    for c in loads:
        c.wait()


def band_mean(energy):
    row = lax.broadcasted_iota(jnp.int32, (FREQS, FREQS), 0)
    col = lax.broadcasted_iota(jnp.int32, (FREQS, FREQS), 1)
    inside = jnp.where(jnp.abs(row - col) <= HALFWIN, 1.0, 0.0).astype(BF16)
    high = energy.astype(BF16)
    left = energy - high.astype(F32)
    middle = left.astype(BF16)
    low = (left - middle.astype(F32)).astype(BF16)
    rows = energy.shape[0]
    sums = jnp.dot(jnp.concatenate([low, middle, high], axis=0), inside, preferred_element_type=F32)
    total = sums[:rows] + sums[rows : 2 * rows] + sums[2 * rows :]
    pos = lax.broadcasted_iota(jnp.int32, (1, FREQS), 1)
    count = jnp.minimum(pos, HALFWIN) + jnp.minimum(FREQS - 1 - pos, HALFWIN) + 1
    return total / count.astype(F32)


def whiten_kernel(place_ref, recv_ref, basis_ref, taper_ref, out_ref):
    place_col = recv_ref[:, SAMPLES : SAMPLES + 1].astype(F32)
    place = jnp.sum(jnp.where(diagonal(SLOTS), place_col, 0.0), axis=0, keepdims=True)
    row = lax.broadcasted_iota(jnp.int32, (SEG_DEV, SLOTS), 0)
    wanted = row // QC * QC + (row + place_ref[4] * HALF) % QC + 1
    pick = jnp.where(place == wanted.astype(F32), 1.0, 0.0).astype(BF16)
    values = jnp.dot(pick, recv_ref[:, :SAMPLES], preferred_element_type=F32)
    values = values - jnp.sum(values, axis=1, keepdims=True) * (1.0 / SAMPLES)
    tapered = (values * taper_ref[...]).astype(BF16)
    spectrum = jnp.dot(tapered, basis_ref[...], preferred_element_type=F32)
    real, imag = spectrum[:, :FREQS], spectrum[:, FREQS:]
    inverse = lax.rsqrt(band_mean(real * real + imag * imag) + EPSILON)
    real, imag = (real * inverse).astype(BF16), (imag * inverse).astype(BF16)
    for w in range(WIN):
        rows = slice(w * QC, (w + 1) * QC)
        out_ref[:, 2 * w * FREQS : (2 * w + 1) * FREQS] = real[rows]
        out_ref[:, (2 * w + 1) * FREQS : (2 * w + 2) * FREQS] = imag[rows]


def group_kernel(moves, n_in, *refs):
    outs = refs[n_in:]
    for i, h, o, p in moves:
        outs[o][p * HALF : (p + 1) * HALF, :] = refs[i][h * HALF : (h + 1) * HALF, :]


def grouped(moves, halves, arrays, after):
    return pl.pallas_call(
        functools.partial(group_kernel, moves, len(arrays) + len(after)),
        in_specs=[VMEM] * len(arrays) + [ANY] * len(after),
        out_specs=[VMEM] * len(halves),
        out_shape=[jax.ShapeDtypeStruct((n * HALF, SPEC), BF16) for n in halves],
        compiler_params=pltpu.CompilerParams(vmem_limit_bytes=MIB),
        cost_estimate=pl.CostEstimate(flops=0, bytes_accessed=2 * MIB, transcendentals=0),
    )(*arrays, *after)


def gate_kernel(*refs):
    del refs


def gated(value, after):
    return pl.pallas_call(
        gate_kernel,
        in_specs=[ANY] * (1 + len(after)),
        out_specs=ANY,
        out_shape=jax.ShapeDtypeStruct(value.shape, value.dtype),
        input_output_aliases={0: 0},
        compiler_params=pltpu.CompilerParams(vmem_limit_bytes=MIB),
        cost_estimate=SMALL,
    )(value, *after)


def rotate_kernel(halves, place_ref, own0, own1, small_ref, out_ref, token_ref, turn_ref, whole, turned, expand):
    col = lax.broadcasted_iota(jnp.int32, (HALF, SIDE), 1) // LAGS
    row = lax.broadcasted_iota(jnp.int32, (HALF, SIDE), 0)
    for g, own in enumerate((own0, own1)):
        whole[g * QC : (g + 1) * QC, :] = own[...]
    for k in range(0, SPEC, FREQS):
        turned[k : k + FREQS, :] = whole[:, k : k + FREQS].T
    core = place_ref[4]
    for g, (other, flip) in enumerate(halves):
        base = (1 - core if other else core) * QC + (1 - core if flip else core) * HALF
        expand[g * HALF : (g + 1) * HALF, :] = jnp.where(col == base + row, 1.0, 0.0).astype(BF16)
    many = FREQS // FINE
    fine_cos = small_ref[2 * many : 2 * many + FINE, :]
    fine_sin = small_ref[2 * many + FINE :, :]
    first_half = jnp.where(lax.broadcasted_iota(jnp.int32, (FINE, 128), 0) == 0, 0.5, 1.0)
    for a in range(many):
        cos, sin = small_ref[a : a + 1, :], small_ref[many + a : many + a + 1, :]
        weight = first_half if a == 0 else 1.0
        turn_ref[a * FINE : (a + 1) * FINE, :] = (cos * fine_cos - sin * fine_sin) * weight
        turn_ref[FREQS + a * FINE : FREQS + (a + 1) * FINE, :] = (sin * fine_cos + cos * fine_sin) * weight
    token_ref[...] = jnp.zeros_like(token_ref)
    step = 256
    per = FREQS // step

    def body(s, carry):
        w, k0 = s // per, pl.multiple_of(lax.rem(s, per) * step, step)
        re = pl.ds(pl.multiple_of(w * 2 * FREQS + k0, step), step)
        im = pl.ds(pl.multiple_of((w * 2 + 1) * FREQS + k0, step), step)
        cos = turn_ref[pl.ds(k0, step), :]
        sin = turn_ref[pl.ds(FREQS + k0, step), :]
        for n in range(SIDE // 256):
            a2 = jnp.dot(turned[re, :], expand[:, n * 256 : (n + 1) * 256], preferred_element_type=F32)
            b2 = jnp.dot(turned[im, :], expand[:, n * 256 : (n + 1) * 256], preferred_element_type=F32)
            for h in range(2):
                a, b = a2[:, h * 128 : (h + 1) * 128], b2[:, h * 128 : (h + 1) * 128]
                cols = slice(n * 256 + h * 128, n * 256 + (h + 1) * 128)
                out_ref[re, cols] = (a * cos - b * sin).astype(BF16)
                out_ref[im, cols] = (a * sin + b * cos).astype(BF16)
        return carry

    lax.fori_loop(0, WIN * per, body, 0)


def rotate(place, halves, own0, own1, turn):
    return pl.pallas_call(
        functools.partial(rotate_kernel, halves),
        in_specs=[SMEM, VMEM, VMEM, VMEM],
        out_specs=[VMEM, VMEM],
        out_shape=[jax.ShapeDtypeStruct((SPEC, SIDE), BF16), TOKEN],
        scratch_shapes=[
            pltpu.VMEM((2 * FREQS, 128), F32),
            pltpu.VMEM((2 * QC, SPEC), BF16),
            pltpu.VMEM((SPEC, 2 * QC), BF16),
            pltpu.VMEM((2 * QC, SIDE), BF16),
        ],
        compiler_params=pltpu.CompilerParams(vmem_limit_bytes=8 * MIB),
        cost_estimate=SMALL,
    )(place, own0, own1, turn)


def matmul_kernel(sources, n_in, place_ref, *refs):
    rot_refs = refs[n_in : n_in + 2]
    out_ref, token_ref, left, acc, in_sem, out_sem = refs[-6:]
    z, xh, y, xl, core = (place_ref[i] for i in range(5))
    loads, begin = [], 0
    for n in range(n_in):
        rows = refs[n].shape[0]
        loads.append(pltpu.make_async_copy(refs[n], left.at[pl.ds(begin, rows)], in_sem.at[n]))
        begin += rows
    for c in loads:
        c.start()
    token_ref[...] = jnp.zeros_like(token_ref)
    ids = []
    for other, offsets, dq in sources:
        c = 1 - core if other else core
        for dp, dx in offsets:
            p = lax.rem(jnp.where(c == 0, y, z) + dp + 4, 4)
            q = lax.rem(jnp.where(c == 0, z, y) + dq + 4, 4)
            block = (jnp.where(c == 0, q, p) * NXH + lax.rem(xh + dx, NXH)) * NY + jnp.where(c == 0, p, q)
            ids.append(block * 2 + c)
    for c in loads:
        c.wait()

    def stores(step):
        chip, part = divmod(step, SIDE // NT)
        cols = pl.ds(pl.multiple_of((1 - xl if chip else xl) * SIDE + part * NT, NT), NT)
        slot = step % 2
        return [
            pltpu.make_async_copy(acc.at[slot, u], out_ref.at[i, :, cols], out_sem.at[slot, u])
            for u, i in enumerate(ids)
        ]

    for step in range(TILES):
        if step >= 2:
            for c in stores(step - 2):
                c.wait()
        chip, part = divmod(step, SIDE // NT)
        tile = rot_refs[chip][:, part * NT : (part + 1) * NT]
        product = jnp.dot(left[...], tile, preferred_element_type=F32)
        acc[step % 2] = product.reshape(acc.shape[1:])
        for c in stores(step):
            c.start()
    for step in range(TILES - 2, TILES):
        for c in stores(step):
            c.wait()


def matmul(place, carried, rotated, out):
    arrays = [value for value, _, _, _ in carried]
    sources = [(other, at, dq) for _, other, at, dq in carried]
    rows = sum(len(at) for _, _, at, _ in carried) * HALF
    operands = [place, *arrays, *rotated]
    in_specs = [SMEM] + [ANY] * len(arrays) + [VMEM] * 2
    aliases = {}
    if out is not None:
        aliases = {len(operands): 0}
        operands.append(out)
        in_specs.append(ANY)
    return pl.pallas_call(
        functools.partial(matmul_kernel, sources, len(arrays)),
        in_specs=in_specs,
        out_specs=[ANY, VMEM],
        scratch_shapes=[
            pltpu.VMEM((rows, SPEC), BF16),
            pltpu.VMEM((2, rows // HALF, HALF, NT), F32),
            pltpu.SemaphoreType.DMA((len(sources),)),
            pltpu.SemaphoreType.DMA((2, rows // HALF)),
        ],
        out_shape=[jax.ShapeDtypeStruct((NZ * NXH * NY * 2, HALF, COLS), F32), TOKEN],
        input_output_aliases=aliases,
        compiler_params=pltpu.CompilerParams(vmem_limit_bytes=12 * MIB),
        cost_estimate=SMALL,
    )(*operands)


def permuted(value, move):
    sizes = (NZ, NXH, NY, NXL, NCORE)
    pairs = []
    for source in range(DEVICES):
        place = np.unravel_index(source, sizes)
        to = [int(t) % s for t, s in zip(move(*(int(p) for p in place)), sizes, strict=True)]
        pairs.append((source, int(np.ravel_multi_index(to, sizes))))
    return lax.ppermute(value, ("blk", "freq"), pairs)


def first(value, d):
    return permuted(value, lambda z, xh, y, xl, c: (z + d * c, xh, y + d * (1 - c), xl, c))


def second(value, d, swap=0):
    return permuted(value, lambda z, xh, y, xl, c: (z + d * (1 - c), xh, y + d * c, xl, c + swap))


def across(value):
    return permuted(value, lambda z, xh, y, xl, c: (z, xh + 1, y, xl, c))


def sibling(value):
    return permuted(value, lambda z, xh, y, xl, c: (z, xh, y, xl, c + 1))


def neighbour(value):
    return permuted(value, lambda z, xh, y, xl, c: (z, xh, y, xl + 1, c))


def local(raw, seg_chan, seg_win, file_count):
    basis, taper, turn = (jnp.asarray(t) for t in tables())
    blk, freq = lax.axis_index("blk"), lax.axis_index("freq")
    z, xh, y = blk // (NXH * NY), blk // NY % NXH, blk % NY
    place = jnp.stack([z, xh, y, freq // NCORE, freq % NCORE]).astype(jnp.int32)

    packed = pl.pallas_call(
        pack_kernel,
        in_specs=[SMEM, VMEM, VMEM],
        out_specs=VMEM,
        out_shape=jax.ShapeDtypeStruct((SLOTS, SAMPLES + TAIL), BF16),
        compiler_params=pltpu.CompilerParams(vmem_limit_bytes=8 * MIB),
    )(file_count, (seg_chan * WIN + seg_win).reshape(1, SLOTS), raw)
    arrived = lax.all_to_all(
        packed.reshape(DEVICES, SLOTS // DEVICES, SAMPLES + TAIL),
        ("blk", "freq"),
        split_axis=0,
        concat_axis=0,
        tiled=True,
    ).reshape(SLOTS, SAMPLES + TAIL)
    basis, taper, turn = pl.pallas_call(
        fetch_kernel,
        in_specs=[ANY, HBM, HBM, HBM],
        out_specs=[VMEM] * 3,
        out_shape=[jax.ShapeDtypeStruct(t.shape, t.dtype) for t in (basis, taper, turn)],
        scratch_shapes=[pltpu.SemaphoreType.DMA((3,))],
        compiler_params=pltpu.CompilerParams(vmem_limit_bytes=MIB),
        cost_estimate=SMALL,
    )(packed, basis, taper, turn)
    white = pl.pallas_call(
        whiten_kernel,
        in_specs=[SMEM] + [VMEM] * 3,
        out_specs=VMEM,
        out_shape=jax.ShapeDtypeStruct((QC, SPEC), BF16),
        compiler_params=pltpu.CompilerParams(vmem_limit_bytes=8 * MIB),
    )(place, arrived, basis, taper)

    sib = sibling(white)
    unit = jnp.concatenate([white[:HALF], sib[HALF:]], axis=0)
    beyond = across(unit)
    ahead, behind = first(unit, 1), first(unit, -1)
    opposite = first(unit, 2)
    near_side, token = rotate(place, [(0, 0), (0, 1), (1, 1), (1, 0)], white, sib, turn)
    beyond_ahead, beyond_behind, beyond_opposite = first(beyond, 1), first(beyond, -1), first(beyond, 2)
    (turned,) = grouped([(0, h, 0, h) for h in range(2)], [2], [unit], [ahead, behind, opposite])
    facing = neighbour(turned)
    facing_sib = sibling(facing)
    arrays = [unit, ahead, behind, opposite, beyond, beyond_ahead, beyond_behind, beyond_opposite]
    line_at = [(0, 0), (-1, 0), (1, 0), (2, 0), (0, 1), (-1, 1), (1, 1), (2, 1)]
    moves = [(i, h, h, i) for i in range(8) for h in range(2)]
    moves += [(i, h, h + 2, p) for i, h, _, p in moves]
    kept, given, later_kept, later_given = grouped(moves, [8] * 4, arrays, [facing, token])
    far_side, _ = rotate(place, [(0, 0), (1, 0), (1, 1), (0, 1)], facing, facing_sib, turn)
    rotated = (near_side, far_side)
    kept_up, given_down = second(kept, 1), second(given, -1, swap=1)
    later_kept, later_given = gated(later_kept, [facing_sib]), gated(later_given, [facing_sib])
    kept_down, given_up = second(later_kept, -1), second(later_given, 1, swap=1)

    def product(out, *carried):
        return matmul(place, [(value, other, line_at, dq) for value, other, dq in carried], rotated, out)

    out, done = product(None, (kept, False, 0), (sibling(given), True, 0))
    kept_up, given_down = gated(kept_up, [done]), gated(given_down, [done])
    kept_far, given_far = second(kept_up, 1), first(given_down, -1)
    out, _ = product(out, (kept_up, False, -1), (given_down, True, 1))
    out, _ = product(out, (kept_down, False, 1), (given_up, True, -1))
    out, _ = product(out, (kept_far, False, -2), (given_far, True, 2))
    return out.reshape(NZ * NXH * NY, QC, COLS)


def solution(mesh):
    in_specs = (
        P(("blk", "freq"), None),
        P(("blk", "freq")),
        P(("blk", "freq")),
        P(("blk", "freq")),
    )
    out_specs = P(None, "freq", "blk")
    return jax.shard_map(local, mesh=mesh, in_specs=in_specs, out_specs=out_specs, check_vma=False)
```

```python
import functools
import math

import jax
import jax.numpy as jnp
import ml_dtypes
import numpy as np
from jax import lax
from jax.experimental import pallas as pl
from jax.experimental.pallas import tpu as pltpu
from jax.sharding import PartitionSpec as P

SAMPLES = 1024
FREQS = 512
FINE = 64
LAGS = 16
HALFWIN = 64
WIN = 4
EPSILON = 1e-06

NZ, NXH, NY = 4, 2, 4
NXL, NCORE = 2, 2
QC = 32
HALF = QC // 2
CB = QC * NXL * NCORE
SEG_DEV = QC * WIN
SLOTS = 256
DEVICES = 128
SPEC = WIN * 2 * FREQS
COLS = CB * LAGS
SIDE = COLS // NXL
TAIL = 128
NT = 1024
TILES = COLS // NT
GROUP = 4
F32, BF16 = jnp.float32, jnp.bfloat16
MIB = 1024 * 1024
SMALL = pl.CostEstimate(flops=1024, bytes_accessed=1024, transcendentals=0)
TOKEN = jax.ShapeDtypeStruct((8, 128), F32)
ANY = pl.BlockSpec(memory_space=pl.ANY)
HBM = pl.BlockSpec(memory_space=pltpu.HBM)
VMEM = pl.BlockSpec(memory_space=pltpu.VMEM)
SMEM = pl.BlockSpec(memory_space=pltpu.SMEM)


def tables():
    n = np.arange(SAMPLES)[:, None]
    k = np.arange(FREQS)[None, :]
    angle = 2.0 * math.pi / SAMPLES * ((n * k) % SAMPLES)
    basis = np.concatenate([np.cos(angle), -np.sin(angle)], axis=1).astype(ml_dtypes.bfloat16)
    taper = (0.5 - 0.5 * np.cos(2.0 * math.pi / SAMPLES * (n[:, 0] + 0.5)))[None, :].astype(np.float32)
    lag = np.arange(128)[None, :] % LAGS - LAGS // 2
    coarse = 2.0 * math.pi / SAMPLES * ((lag * FINE * np.arange(FREQS // FINE)[:, None]) % SAMPLES)
    fine = 2.0 * math.pi / SAMPLES * ((lag * np.arange(FINE)[:, None]) % SAMPLES)
    gain = 2.0 / math.sqrt(2.0 * WIN * FREQS)
    turn = np.concatenate([np.cos(coarse), np.sin(coarse), gain * np.cos(fine), gain * np.sin(fine)], axis=0)
    turn = turn.astype(np.float32)
    return basis, taper, turn


def diagonal(size):
    return lax.broadcasted_iota(jnp.int32, (size, size), 0) == lax.broadcasted_iota(jnp.int32, (size, size), 1)


def pack_kernel(count_ref, key_ref, raw_ref, out_ref):
    key = key_ref[...]
    chan = key // WIN
    slot = lax.broadcasted_iota(jnp.int32, (1, SLOTS), 1)
    live = slot < count_ref[0]
    owner = jnp.where(live, chan // QC, -1).astype(F32)
    owner_col = jnp.sum(jnp.where(diagonal(SLOTS), owner, 0.0), axis=1, keepdims=True)
    row = lax.broadcasted_iota(jnp.int32, (SLOTS, SLOTS), 0)
    col = lax.broadcasted_iota(jnp.int32, (SLOTS, SLOTS), 1)
    earlier = jnp.where((owner_col == owner) & (row < col), 1.0, 0.0)
    rank = jnp.sum(earlier, axis=0, keepdims=True)
    flat = jnp.where(live, owner * 2.0 + rank, -1.0)
    pick = jnp.where(flat == row.astype(F32), 1.0, 0.0)
    place = (key % WIN * QC + chan % QC + 1).astype(F32)
    place_col = jnp.sum(pick * place, axis=1, keepdims=True)
    out_ref[:, SAMPLES:] = jnp.broadcast_to(place_col, (SLOTS, TAIL)).astype(BF16)
    out_ref[:, :SAMPLES] = jnp.dot(pick.astype(BF16), raw_ref[...], preferred_element_type=F32).astype(BF16)


def fetch_kernel(after_hbm, basis_hbm, taper_hbm, turn_hbm, basis_ref, taper_ref, turn_ref, sem):
    del after_hbm
    loads = [
        pltpu.make_async_copy(basis_hbm, basis_ref, sem.at[0]),
        pltpu.make_async_copy(taper_hbm, taper_ref, sem.at[1]),
        pltpu.make_async_copy(turn_hbm, turn_ref, sem.at[2]),
    ]
    for c in loads:
        c.start()
    for c in loads:
        c.wait()


def band_mean(energy):
    row = lax.broadcasted_iota(jnp.int32, (FREQS, FREQS), 0)
    col = lax.broadcasted_iota(jnp.int32, (FREQS, FREQS), 1)
    inside = jnp.where(jnp.abs(row - col) <= HALFWIN, 1.0, 0.0).astype(BF16)
    high = energy.astype(BF16)
    left = energy - high.astype(F32)
    middle = left.astype(BF16)
    low = (left - middle.astype(F32)).astype(BF16)
    rows = energy.shape[0]
    sums = jnp.dot(jnp.concatenate([low, middle, high], axis=0), inside, preferred_element_type=F32)
    total = sums[:rows] + sums[rows : 2 * rows] + sums[2 * rows :]
    pos = lax.broadcasted_iota(jnp.int32, (1, FREQS), 1)
    count = jnp.minimum(pos, HALFWIN) + jnp.minimum(FREQS - 1 - pos, HALFWIN) + 1
    return total / count.astype(F32)


def whiten_kernel(place_ref, recv_ref, basis_ref, taper_ref, keep_ref, give_ref):
    place_col = recv_ref[:, SAMPLES : SAMPLES + 1].astype(F32)
    place = jnp.sum(jnp.where(diagonal(SLOTS), place_col, 0.0), axis=0, keepdims=True)
    row = lax.broadcasted_iota(jnp.int32, (SEG_DEV, SLOTS), 0)
    wanted = row // QC * QC + (row + place_ref[4] * HALF) % QC + 1
    pick = jnp.where(place == wanted.astype(F32), 1.0, 0.0).astype(BF16)
    values = jnp.dot(pick, recv_ref[:, :SAMPLES], preferred_element_type=F32)
    values = values - jnp.sum(values, axis=1, keepdims=True) * (1.0 / SAMPLES)
    tapered = (values * taper_ref[...]).astype(BF16)
    spectrum = jnp.dot(tapered, basis_ref[...], preferred_element_type=F32)
    real, imag = spectrum[:, :FREQS], spectrum[:, FREQS:]
    inverse = lax.rsqrt(band_mean(real * real + imag * imag) + EPSILON)
    real, imag = (real * inverse).astype(BF16), (imag * inverse).astype(BF16)
    for w in range(WIN):
        for h, out_ref in enumerate((keep_ref, give_ref)):
            rows = slice(w * QC + h * HALF, w * QC + (h + 1) * HALF)
            out_ref[:, 2 * w * FREQS : (2 * w + 1) * FREQS] = real[rows]
            out_ref[:, (2 * w + 1) * FREQS : (2 * w + 2) * FREQS] = imag[rows]


def group_kernel(moves, n_in, *refs):
    outs = refs[n_in:]
    for i, h, o, p in moves:
        outs[o][p * HALF : (p + 1) * HALF, :] = refs[i][h * HALF : (h + 1) * HALF, :]


def grouped(moves, halves, arrays, after):
    return pl.pallas_call(
        functools.partial(group_kernel, moves, len(arrays) + len(after)),
        in_specs=[VMEM] * len(arrays) + [ANY] * len(after),
        out_specs=[VMEM] * len(halves),
        out_shape=[jax.ShapeDtypeStruct((n * HALF, SPEC), BF16) for n in halves],
        compiler_params=pltpu.CompilerParams(vmem_limit_bytes=MIB),
        cost_estimate=pl.CostEstimate(flops=0, bytes_accessed=2 * MIB, transcendentals=0),
    )(*arrays, *after)


def gate_kernel(*refs):
    del refs


def gated(value, after):
    return pl.pallas_call(
        gate_kernel,
        in_specs=[ANY] * (1 + len(after)),
        out_specs=ANY,
        out_shape=jax.ShapeDtypeStruct(value.shape, value.dtype),
        input_output_aliases={0: 0},
        compiler_params=pltpu.CompilerParams(vmem_limit_bytes=MIB),
        cost_estimate=SMALL,
    )(value, *after)


def rotate_kernel(halves, place_ref, own0, own1, small_ref, out_ref, token_ref, turn_ref, whole, turned, expand):
    col = lax.broadcasted_iota(jnp.int32, (HALF, SIDE), 1) // LAGS
    row = lax.broadcasted_iota(jnp.int32, (HALF, SIDE), 0)
    for g, own in enumerate((own0, own1)):
        whole[g * QC : (g + 1) * QC, :] = own[...]
    for k in range(0, SPEC, FREQS):
        turned[k : k + FREQS, :] = whole[:, k : k + FREQS].T
    core = place_ref[4]
    for g, (other, flip) in enumerate(halves):
        base = (1 - core if other else core) * QC + (1 - core if flip else core) * HALF
        expand[g * HALF : (g + 1) * HALF, :] = jnp.where(col == base + row, 1.0, 0.0).astype(BF16)
    many = FREQS // FINE
    fine_cos = small_ref[2 * many : 2 * many + FINE, :]
    fine_sin = small_ref[2 * many + FINE :, :]
    first_half = jnp.where(lax.broadcasted_iota(jnp.int32, (FINE, 128), 0) == 0, 0.5, 1.0)
    for a in range(many):
        cos, sin = small_ref[a : a + 1, :], small_ref[many + a : many + a + 1, :]
        weight = first_half if a == 0 else 1.0
        turn_ref[a * FINE : (a + 1) * FINE, :] = (cos * fine_cos - sin * fine_sin) * weight
        turn_ref[FREQS + a * FINE : FREQS + (a + 1) * FINE, :] = (sin * fine_cos + cos * fine_sin) * weight
    token_ref[...] = jnp.zeros_like(token_ref)
    step = 256
    per = FREQS // step

    def body(s, carry):
        w, k0 = s // per, pl.multiple_of(lax.rem(s, per) * step, step)
        re = pl.ds(pl.multiple_of(w * 2 * FREQS + k0, step), step)
        im = pl.ds(pl.multiple_of((w * 2 + 1) * FREQS + k0, step), step)
        cos = turn_ref[pl.ds(k0, step), :]
        sin = turn_ref[pl.ds(FREQS + k0, step), :]
        for n in range(SIDE // 256):
            a2 = jnp.dot(turned[re, :], expand[:, n * 256 : (n + 1) * 256], preferred_element_type=F32)
            b2 = jnp.dot(turned[im, :], expand[:, n * 256 : (n + 1) * 256], preferred_element_type=F32)
            for h in range(2):
                a, b = a2[:, h * 128 : (h + 1) * 128], b2[:, h * 128 : (h + 1) * 128]
                cols = slice(n * 256 + h * 128, n * 256 + (h + 1) * 128)
                out_ref[re, cols] = (a * cos - b * sin).astype(BF16)
                out_ref[im, cols] = (a * sin + b * cos).astype(BF16)
        return carry

    lax.fori_loop(0, WIN * per, body, 0)


def rotate(place, halves, own0, own1, turn):
    return pl.pallas_call(
        functools.partial(rotate_kernel, halves),
        in_specs=[SMEM, VMEM, VMEM, VMEM],
        out_specs=[VMEM, VMEM],
        out_shape=[jax.ShapeDtypeStruct((SPEC, SIDE), BF16), TOKEN],
        scratch_shapes=[
            pltpu.VMEM((2 * FREQS, 128), F32),
            pltpu.VMEM((2 * QC, SPEC), BF16),
            pltpu.VMEM((SPEC, 2 * QC), BF16),
            pltpu.VMEM((2 * QC, SIDE), BF16),
        ],
        compiler_params=pltpu.CompilerParams(vmem_limit_bytes=8 * MIB),
        cost_estimate=SMALL,
    )(place, own0, own1, turn)


def matmul_kernel(sources, n_in, place_ref, *refs):
    rot_refs = refs[n_in : n_in + 2]
    out_ref, token_ref, left, acc, in_sem, out_sem = refs[-6:]
    z, xh, y, xl, core = (place_ref[i] for i in range(5))
    loads, begin = [], 0
    for n in range(n_in):
        rows = refs[n].shape[0]
        loads.append(pltpu.make_async_copy(refs[n], left.at[pl.ds(begin, rows)], in_sem.at[n]))
        begin += rows
    for c in loads:
        c.start()
    token_ref[...] = jnp.zeros_like(token_ref)
    ids = []
    for other, offsets, dq in sources:
        c = 1 - core if other else core
        for dp, dx in offsets:
            p = lax.rem(jnp.where(c == 0, y, z) + dp + 4, 4)
            q = lax.rem(jnp.where(c == 0, z, y) + dq + 4, 4)
            block = (jnp.where(c == 0, q, p) * NXH + lax.rem(xh + dx, NXH)) * NY + jnp.where(c == 0, p, q)
            ids.append(block * 2 + c)
    for c in loads:
        c.wait()

    def stores(step):
        chip, part = divmod(step, SIDE // NT)
        cols = pl.ds(pl.multiple_of((1 - xl if chip else xl) * SIDE + part * NT, NT), NT)
        slot = step % 2
        return [
            pltpu.make_async_copy(acc.at[slot, u], out_ref.at[i, :, cols], out_sem.at[slot, u])
            for u, i in enumerate(ids)
        ]

    for step in range(TILES):
        if step >= 2:
            for c in stores(step - 2):
                c.wait()
        chip, part = divmod(step, SIDE // NT)
        tile = rot_refs[chip][:, part * NT : (part + 1) * NT]
        product = jnp.dot(left[...], tile, preferred_element_type=F32)
        acc[step % 2] = product.reshape(acc.shape[1:])
        for c in stores(step):
            c.start()
    for step in range(TILES - 2, TILES):
        for c in stores(step):
            c.wait()


def matmul(place, carried, rotated, out):
    arrays = [value for value, _, _, _ in carried]
    sources = [(other, at, dq) for _, other, at, dq in carried]
    rows = sum(len(at) for _, _, at, _ in carried) * HALF
    operands = [place, *arrays, *rotated]
    in_specs = [SMEM] + [ANY] * len(arrays) + [VMEM] * 2
    aliases = {}
    if out is not None:
        aliases = {len(operands): 0}
        operands.append(out)
        in_specs.append(ANY)
    return pl.pallas_call(
        functools.partial(matmul_kernel, sources, len(arrays)),
        in_specs=in_specs,
        out_specs=[ANY, VMEM],
        scratch_shapes=[
            pltpu.VMEM((rows, SPEC), BF16),
            pltpu.VMEM((2, rows // HALF, HALF, NT), F32),
            pltpu.SemaphoreType.DMA((len(sources),)),
            pltpu.SemaphoreType.DMA((2, rows // HALF)),
        ],
        out_shape=[jax.ShapeDtypeStruct((NZ * NXH * NY * 2, HALF, COLS), F32), TOKEN],
        input_output_aliases=aliases,
        compiler_params=pltpu.CompilerParams(vmem_limit_bytes=12 * MIB),
        cost_estimate=SMALL,
    )(*operands)


def permuted(value, move):
    sizes = (NZ, NXH, NY, NXL, NCORE)
    pairs = []
    for source in range(DEVICES):
        place = np.unravel_index(source, sizes)
        to = [int(t) % s for t, s in zip(move(*(int(p) for p in place)), sizes, strict=True)]
        pairs.append((source, int(np.ravel_multi_index(to, sizes))))
    return lax.ppermute(value, ("blk", "freq"), pairs)


def first(value, d):
    return permuted(value, lambda z, xh, y, xl, c: (z + d * c, xh, y + d * (1 - c), xl, c))


def second(value, d, swap=0):
    return permuted(value, lambda z, xh, y, xl, c: (z + d * (1 - c), xh, y + d * c, xl, c + swap))


def across(value):
    return permuted(value, lambda z, xh, y, xl, c: (z, xh + 1, y, xl, c))


def sibling(value):
    return permuted(value, lambda z, xh, y, xl, c: (z, xh, y, xl, c + 1))


def neighbour(value):
    return permuted(value, lambda z, xh, y, xl, c: (z, xh, y, xl + 1, c))


def local(raw, seg_chan, seg_win, file_count):
    basis, taper, turn = (jnp.asarray(t) for t in tables())
    blk, freq = lax.axis_index("blk"), lax.axis_index("freq")
    z, xh, y = blk // (NXH * NY), blk // NY % NXH, blk % NY
    place = jnp.stack([z, xh, y, freq // NCORE, freq % NCORE]).astype(jnp.int32)

    packed = pl.pallas_call(
        pack_kernel,
        in_specs=[SMEM, VMEM, VMEM],
        out_specs=VMEM,
        out_shape=jax.ShapeDtypeStruct((SLOTS, SAMPLES + TAIL), BF16),
        compiler_params=pltpu.CompilerParams(vmem_limit_bytes=8 * MIB),
    )(file_count, (seg_chan * WIN + seg_win).reshape(1, SLOTS), raw)
    arrived = lax.all_to_all(
        packed.reshape(DEVICES, SLOTS // DEVICES, SAMPLES + TAIL),
        ("blk", "freq"),
        split_axis=0,
        concat_axis=0,
        tiled=True,
    ).reshape(SLOTS, SAMPLES + TAIL)
    basis, taper, turn = pl.pallas_call(
        fetch_kernel,
        in_specs=[ANY, HBM, HBM, HBM],
        out_specs=[VMEM] * 3,
        out_shape=[jax.ShapeDtypeStruct(t.shape, t.dtype) for t in (basis, taper, turn)],
        scratch_shapes=[pltpu.SemaphoreType.DMA((3,))],
        compiler_params=pltpu.CompilerParams(vmem_limit_bytes=MIB),
        cost_estimate=SMALL,
    )(packed, basis, taper, turn)
    keep, give = pl.pallas_call(
        whiten_kernel,
        in_specs=[SMEM] + [VMEM] * 3,
        out_specs=[VMEM] * 2,
        out_shape=[jax.ShapeDtypeStruct((HALF, SPEC), BF16)] * 2,
        compiler_params=pltpu.CompilerParams(vmem_limit_bytes=8 * MIB),
    )(place, arrived, basis, taper)

    unit = jnp.concatenate([keep, sibling(give)], axis=0)
    beyond = across(unit)
    ahead, behind = first(unit, 1), first(unit, -1)
    opposite = first(unit, 2)
    near_side, token = rotate(place, [(0, 0), (1, 0), (1, 1), (0, 1)], unit, sibling(unit), turn)
    beyond_ahead, beyond_behind, beyond_opposite = first(beyond, 1), first(beyond, -1), first(beyond, 2)
    (turned,) = grouped([(0, h, 0, h) for h in range(2)], [2], [unit], [ahead, behind, opposite])
    facing = neighbour(turned)
    facing_sib = sibling(facing)
    arrays = [unit, ahead, behind, opposite, beyond, beyond_ahead, beyond_behind, beyond_opposite]
    line_at = [(0, 0), (-1, 0), (1, 0), (2, 0), (0, 1), (-1, 1), (1, 1), (2, 1)]
    moves = [(i, h, h, i) for i in range(8) for h in range(2)]
    moves += [(i, h, h + 2, p) for i, h, _, p in moves]
    kept, given, later_kept, later_given = grouped(moves, [8] * 4, arrays, [facing, token])
    far_side, _ = rotate(place, [(0, 0), (1, 0), (1, 1), (0, 1)], facing, facing_sib, turn)
    rotated = (near_side, far_side)
    kept_up, given_down = second(kept, 1), second(given, -1, swap=1)
    later_kept, later_given = gated(later_kept, [facing_sib]), gated(later_given, [facing_sib])
    kept_down, given_up = second(later_kept, -1), second(later_given, 1, swap=1)

    def product(out, *carried):
        return matmul(place, [(value, other, line_at, dq) for value, other, dq in carried], rotated, out)

    out, done = product(None, (kept, False, 0), (sibling(given), True, 0))
    kept_up, given_down = gated(kept_up, [done]), gated(given_down, [done])
    kept_far, given_far = second(kept_up, 1), first(given_down, -1)
    out, _ = product(out, (kept_up, False, -1), (given_down, True, 1))
    out, _ = product(out, (kept_down, False, 1), (given_up, True, -1))
    out, _ = product(out, (kept_far, False, -2), (given_far, True, 2))
    return out.reshape(NZ * NXH * NY, QC, COLS)


def solution(mesh):
    in_specs = (
        P(("blk", "freq"), None),
        P(("blk", "freq")),
        P(("blk", "freq")),
        P(("blk", "freq")),
    )
    out_specs = P(None, "freq", "blk")
    return jax.shard_map(local, mesh=mesh, in_specs=in_specs, out_specs=out_specs, check_vma=False)
```

```python
import functools
import math

import jax
import jax.numpy as jnp
import ml_dtypes
import numpy as np
from jax import lax
from jax.experimental import pallas as pl
from jax.experimental.pallas import tpu as pltpu
from jax.sharding import PartitionSpec as P

SAMPLES = 1024
FREQS = 512
FINE = 64
LAGS = 16
HALFWIN = 64
WIN = 4
EPSILON = 1e-06

NZ, NXH, NY = 4, 2, 4
NXL, NCORE = 2, 2
QC = 32
HALF = QC // 2
CB = QC * NXL * NCORE
SEG_DEV = QC * WIN
SLOTS = 256
DEVICES = 128
SPEC = WIN * 2 * FREQS
COLS = CB * LAGS
SIDE = COLS // NXL
TAIL = 128
NT = 1024
TILES = COLS // NT
GROUP = 4
F32, BF16 = jnp.float32, jnp.bfloat16
MIB = 1024 * 1024
SMALL = pl.CostEstimate(flops=1024, bytes_accessed=1024, transcendentals=0)
TOKEN = jax.ShapeDtypeStruct((8, 128), F32)
ANY = pl.BlockSpec(memory_space=pl.ANY)
HBM = pl.BlockSpec(memory_space=pltpu.HBM)
VMEM = pl.BlockSpec(memory_space=pltpu.VMEM)
SMEM = pl.BlockSpec(memory_space=pltpu.SMEM)


def tables():
    n = np.arange(SAMPLES)[:, None]
    k = np.arange(FREQS)[None, :]
    angle = 2.0 * math.pi / SAMPLES * ((n * k) % SAMPLES)
    basis = np.concatenate([np.cos(angle), -np.sin(angle)], axis=1).astype(ml_dtypes.bfloat16)
    taper = (0.5 - 0.5 * np.cos(2.0 * math.pi / SAMPLES * (n[:, 0] + 0.5)))[None, :].astype(np.float32)
    lag = np.arange(128)[None, :] % LAGS - LAGS // 2
    coarse = 2.0 * math.pi / SAMPLES * ((lag * FINE * np.arange(FREQS // FINE)[:, None]) % SAMPLES)
    fine = 2.0 * math.pi / SAMPLES * ((lag * np.arange(FINE)[:, None]) % SAMPLES)
    gain = 2.0 / math.sqrt(2.0 * WIN * FREQS)
    turn = np.concatenate([np.cos(coarse), np.sin(coarse), gain * np.cos(fine), gain * np.sin(fine)], axis=0)
    turn = turn.astype(np.float32)
    return basis, taper, turn


def diagonal(size):
    return lax.broadcasted_iota(jnp.int32, (size, size), 0) == lax.broadcasted_iota(jnp.int32, (size, size), 1)


def pack_kernel(count_ref, key_ref, raw_ref, out_ref):
    key = key_ref[...]
    chan = key // WIN
    slot = lax.broadcasted_iota(jnp.int32, (1, SLOTS), 1)
    live = slot < count_ref[0]
    owner = jnp.where(live, chan // QC, -1).astype(F32)
    owner_col = jnp.sum(jnp.where(diagonal(SLOTS), owner, 0.0), axis=1, keepdims=True)
    row = lax.broadcasted_iota(jnp.int32, (SLOTS, SLOTS), 0)
    col = lax.broadcasted_iota(jnp.int32, (SLOTS, SLOTS), 1)
    earlier = jnp.where((owner_col == owner) & (row < col), 1.0, 0.0)
    rank = jnp.sum(earlier, axis=0, keepdims=True)
    flat = jnp.where(live, owner * 2.0 + rank, -1.0)
    pick = jnp.where(flat == row.astype(F32), 1.0, 0.0)
    place = (key % WIN * QC + chan % QC + 1).astype(F32)
    place_col = jnp.sum(pick * place, axis=1, keepdims=True)
    place_all = jnp.broadcast_to(place_col, (SLOTS, TAIL)).astype(BF16)
    out_ref[:, :, SAMPLES:] = place_all.reshape(DEVICES, SLOTS // DEVICES, TAIL)
    sent = jnp.dot(pick.astype(BF16), raw_ref[...], preferred_element_type=F32).astype(BF16)
    out_ref[:, :, :SAMPLES] = sent.reshape(DEVICES, SLOTS // DEVICES, SAMPLES)


def fetch_kernel(after_hbm, basis_hbm, taper_hbm, turn_hbm, basis_ref, taper_ref, turn_ref, sem):
    del after_hbm
    loads = [
        pltpu.make_async_copy(basis_hbm, basis_ref, sem.at[0]),
        pltpu.make_async_copy(taper_hbm, taper_ref, sem.at[1]),
        pltpu.make_async_copy(turn_hbm, turn_ref, sem.at[2]),
    ]
    for c in loads:
        c.start()
    for c in loads:
        c.wait()


def band_mean(energy):
    row = lax.broadcasted_iota(jnp.int32, (FREQS, FREQS), 0)
    col = lax.broadcasted_iota(jnp.int32, (FREQS, FREQS), 1)
    inside = jnp.where(jnp.abs(row - col) <= HALFWIN, 1.0, 0.0).astype(BF16)
    high = energy.astype(BF16)
    left = energy - high.astype(F32)
    middle = left.astype(BF16)
    low = (left - middle.astype(F32)).astype(BF16)
    rows = energy.shape[0]
    sums = jnp.dot(jnp.concatenate([low, middle, high], axis=0), inside, preferred_element_type=F32)
    total = sums[:rows] + sums[rows : 2 * rows] + sums[2 * rows :]
    pos = lax.broadcasted_iota(jnp.int32, (1, FREQS), 1)
    count = jnp.minimum(pos, HALFWIN) + jnp.minimum(FREQS - 1 - pos, HALFWIN) + 1
    return total / count.astype(F32)


def whiten_kernel(place_ref, recv_ref, basis_ref, taper_ref, keep_ref, give_ref):
    place_col = recv_ref[:, SAMPLES : SAMPLES + 1].astype(F32)
    place = jnp.sum(jnp.where(diagonal(SLOTS), place_col, 0.0), axis=0, keepdims=True)
    row = lax.broadcasted_iota(jnp.int32, (SEG_DEV, SLOTS), 0)
    wanted = row // QC * QC + (row + place_ref[4] * HALF) % QC + 1
    pick = jnp.where(place == wanted.astype(F32), 1.0, 0.0).astype(BF16)
    values = jnp.dot(pick, recv_ref[:, :SAMPLES], preferred_element_type=F32)
    values = values - jnp.sum(values, axis=1, keepdims=True) * (1.0 / SAMPLES)
    tapered = (values * taper_ref[...]).astype(BF16)
    spectrum = jnp.dot(tapered, basis_ref[...], preferred_element_type=F32)
    real, imag = spectrum[:, :FREQS], spectrum[:, FREQS:]
    inverse = lax.rsqrt(band_mean(real * real + imag * imag) + EPSILON)
    real, imag = (real * inverse).astype(BF16), (imag * inverse).astype(BF16)
    for w in range(WIN):
        for h, out_ref in enumerate((keep_ref, give_ref)):
            rows = slice(w * QC + h * HALF, w * QC + (h + 1) * HALF)
            out_ref[:, 2 * w * FREQS : (2 * w + 1) * FREQS] = real[rows]
            out_ref[:, (2 * w + 1) * FREQS : (2 * w + 2) * FREQS] = imag[rows]


def group_kernel(moves, n_in, *refs):
    outs = refs[n_in:]
    for i, h, o, p in moves:
        outs[o][p * HALF : (p + 1) * HALF, :] = refs[i][h * HALF : (h + 1) * HALF, :]


def grouped(moves, halves, arrays, after):
    return pl.pallas_call(
        functools.partial(group_kernel, moves, len(arrays) + len(after)),
        in_specs=[VMEM] * len(arrays) + [ANY] * len(after),
        out_specs=[VMEM] * len(halves),
        out_shape=[jax.ShapeDtypeStruct((n * HALF, SPEC), BF16) for n in halves],
        compiler_params=pltpu.CompilerParams(vmem_limit_bytes=MIB),
        cost_estimate=pl.CostEstimate(flops=0, bytes_accessed=2 * MIB, transcendentals=0),
    )(*arrays, *after)


def gate_kernel(*refs):
    del refs


def gated(value, after):
    return pl.pallas_call(
        gate_kernel,
        in_specs=[ANY] * (1 + len(after)),
        out_specs=ANY,
        out_shape=jax.ShapeDtypeStruct(value.shape, value.dtype),
        input_output_aliases={0: 0},
        compiler_params=pltpu.CompilerParams(vmem_limit_bytes=MIB),
        cost_estimate=SMALL,
    )(value, *after)


def rotate_kernel(halves, place_ref, own0, own1, small_ref, out_ref, token_ref, turn_ref, whole, turned, expand):
    col = lax.broadcasted_iota(jnp.int32, (HALF, SIDE), 1) // LAGS
    row = lax.broadcasted_iota(jnp.int32, (HALF, SIDE), 0)
    for g, own in enumerate((own0, own1)):
        whole[g * QC : (g + 1) * QC, :] = own[...]
    for k in range(0, SPEC, FREQS):
        turned[k : k + FREQS, :] = whole[:, k : k + FREQS].T
    core = place_ref[4]
    for g, (other, flip) in enumerate(halves):
        base = (1 - core if other else core) * QC + (1 - core if flip else core) * HALF
        expand[g * HALF : (g + 1) * HALF, :] = jnp.where(col == base + row, 1.0, 0.0).astype(BF16)
    many = FREQS // FINE
    fine_cos = small_ref[2 * many : 2 * many + FINE, :]
    fine_sin = small_ref[2 * many + FINE :, :]
    first_half = jnp.where(lax.broadcasted_iota(jnp.int32, (FINE, 128), 0) == 0, 0.5, 1.0)
    for a in range(many):
        cos, sin = small_ref[a : a + 1, :], small_ref[many + a : many + a + 1, :]
        weight = first_half if a == 0 else 1.0
        turn_ref[a * FINE : (a + 1) * FINE, :] = (cos * fine_cos - sin * fine_sin) * weight
        turn_ref[FREQS + a * FINE : FREQS + (a + 1) * FINE, :] = (sin * fine_cos + cos * fine_sin) * weight
    token_ref[...] = jnp.zeros_like(token_ref)
    step = 256
    per = FREQS // step

    def body(s, carry):
        w, k0 = s // per, pl.multiple_of(lax.rem(s, per) * step, step)
        re = pl.ds(pl.multiple_of(w * 2 * FREQS + k0, step), step)
        im = pl.ds(pl.multiple_of((w * 2 + 1) * FREQS + k0, step), step)
        cos = turn_ref[pl.ds(k0, step), :]
        sin = turn_ref[pl.ds(FREQS + k0, step), :]
        for n in range(SIDE // 256):
            a2 = jnp.dot(turned[re, :], expand[:, n * 256 : (n + 1) * 256], preferred_element_type=F32)
            b2 = jnp.dot(turned[im, :], expand[:, n * 256 : (n + 1) * 256], preferred_element_type=F32)
            for h in range(2):
                a, b = a2[:, h * 128 : (h + 1) * 128], b2[:, h * 128 : (h + 1) * 128]
                cols = slice(n * 256 + h * 128, n * 256 + (h + 1) * 128)
                out_ref[re, cols] = (a * cos - b * sin).astype(BF16)
                out_ref[im, cols] = (a * sin + b * cos).astype(BF16)
        return carry

    lax.fori_loop(0, WIN * per, body, 0)


def rotate(place, halves, own0, own1, turn):
    return pl.pallas_call(
        functools.partial(rotate_kernel, halves),
        in_specs=[SMEM, VMEM, VMEM, VMEM],
        out_specs=[VMEM, VMEM],
        out_shape=[jax.ShapeDtypeStruct((SPEC, SIDE), BF16), TOKEN],
        scratch_shapes=[
            pltpu.VMEM((2 * FREQS, 128), F32),
            pltpu.VMEM((2 * QC, SPEC), BF16),
            pltpu.VMEM((SPEC, 2 * QC), BF16),
            pltpu.VMEM((2 * QC, SIDE), BF16),
        ],
        compiler_params=pltpu.CompilerParams(vmem_limit_bytes=8 * MIB),
        cost_estimate=SMALL,
    )(place, own0, own1, turn)


def matmul_kernel(sources, n_in, place_ref, *refs):
    rot_refs = refs[n_in : n_in + 2]
    out_ref, token_ref, left, acc, in_sem, out_sem = refs[-6:]
    z, xh, y, xl, core = (place_ref[i] for i in range(5))
    loads, begin = [], 0
    for n in range(n_in):
        rows = refs[n].shape[0]
        loads.append(pltpu.make_async_copy(refs[n], left.at[pl.ds(begin, rows)], in_sem.at[n]))
        begin += rows
    for c in loads:
        c.start()
    token_ref[...] = jnp.zeros_like(token_ref)
    ids = []
    for other, offsets, dq in sources:
        c = 1 - core if other else core
        for dp, dx in offsets:
            p = lax.rem(jnp.where(c == 0, y, z) + dp + 4, 4)
            q = lax.rem(jnp.where(c == 0, z, y) + dq + 4, 4)
            block = (jnp.where(c == 0, q, p) * NXH + lax.rem(xh + dx, NXH)) * NY + jnp.where(c == 0, p, q)
            ids.append(block * 2 + c)
    for c in loads:
        c.wait()

    def stores(step):
        chip, part = divmod(step, SIDE // NT)
        cols = pl.ds(pl.multiple_of((1 - xl if chip else xl) * SIDE + part * NT, NT), NT)
        slot = step % 2
        return [
            pltpu.make_async_copy(acc.at[slot, u], out_ref.at[i, :, cols], out_sem.at[slot, u])
            for u, i in enumerate(ids)
        ]

    for step in range(TILES):
        if step >= 2:
            for c in stores(step - 2):
                c.wait()
        chip, part = divmod(step, SIDE // NT)
        tile = rot_refs[chip][:, part * NT : (part + 1) * NT]
        product = jnp.dot(left[...], tile, preferred_element_type=F32)
        acc[step % 2] = product.reshape(acc.shape[1:])
        for c in stores(step):
            c.start()
    for step in range(TILES - 2, TILES):
        for c in stores(step):
            c.wait()


def matmul(place, carried, rotated, out):
    arrays = [value for value, _, _, _ in carried]
    sources = [(other, at, dq) for _, other, at, dq in carried]
    rows = sum(len(at) for _, _, at, _ in carried) * HALF
    operands = [place, *arrays, *rotated]
    in_specs = [SMEM] + [ANY] * len(arrays) + [VMEM] * 2
    aliases = {}
    if out is not None:
        aliases = {len(operands): 0}
        operands.append(out)
        in_specs.append(ANY)
    return pl.pallas_call(
        functools.partial(matmul_kernel, sources, len(arrays)),
        in_specs=in_specs,
        out_specs=[ANY, VMEM],
        scratch_shapes=[
            pltpu.VMEM((rows, SPEC), BF16),
            pltpu.VMEM((2, rows // HALF, HALF, NT), F32),
            pltpu.SemaphoreType.DMA((len(sources),)),
            pltpu.SemaphoreType.DMA((2, rows // HALF)),
        ],
        out_shape=[jax.ShapeDtypeStruct((NZ * NXH * NY * 2, HALF, COLS), F32), TOKEN],
        input_output_aliases=aliases,
        compiler_params=pltpu.CompilerParams(vmem_limit_bytes=12 * MIB),
        cost_estimate=SMALL,
    )(*operands)


def permuted(value, move):
    sizes = (NZ, NXH, NY, NXL, NCORE)
    pairs = []
    for source in range(DEVICES):
        place = np.unravel_index(source, sizes)
        to = [int(t) % s for t, s in zip(move(*(int(p) for p in place)), sizes, strict=True)]
        pairs.append((source, int(np.ravel_multi_index(to, sizes))))
    return lax.ppermute(value, ("blk", "freq"), pairs)


def first(value, d):
    return permuted(value, lambda z, xh, y, xl, c: (z + d * c, xh, y + d * (1 - c), xl, c))


def second(value, d, swap=0):
    return permuted(value, lambda z, xh, y, xl, c: (z + d * (1 - c), xh, y + d * c, xl, c + swap))


def across(value):
    return permuted(value, lambda z, xh, y, xl, c: (z, xh + 1, y, xl, c))


def sibling(value):
    return permuted(value, lambda z, xh, y, xl, c: (z, xh, y, xl, c + 1))


def neighbour(value):
    return permuted(value, lambda z, xh, y, xl, c: (z, xh, y, xl + 1, c))


def local(raw, seg_chan, seg_win, file_count):
    basis, taper, turn = (jnp.asarray(t) for t in tables())
    blk, freq = lax.axis_index("blk"), lax.axis_index("freq")
    z, xh, y = blk // (NXH * NY), blk // NY % NXH, blk % NY
    place = jnp.stack([z, xh, y, freq // NCORE, freq % NCORE]).astype(jnp.int32)

    packed = pl.pallas_call(
        pack_kernel,
        in_specs=[SMEM, VMEM, VMEM],
        out_specs=VMEM,
        out_shape=jax.ShapeDtypeStruct((DEVICES, SLOTS // DEVICES, SAMPLES + TAIL), BF16),
        compiler_params=pltpu.CompilerParams(vmem_limit_bytes=8 * MIB),
    )(file_count, (seg_chan * WIN + seg_win).reshape(1, SLOTS), raw)
    arrived = lax.all_to_all(
        packed,
        ("blk", "freq"),
        split_axis=0,
        concat_axis=0,
        tiled=True,
    ).reshape(SLOTS, SAMPLES + TAIL)
    basis, taper, turn = pl.pallas_call(
        fetch_kernel,
        in_specs=[ANY, HBM, HBM, HBM],
        out_specs=[VMEM] * 3,
        out_shape=[jax.ShapeDtypeStruct(t.shape, t.dtype) for t in (basis, taper, turn)],
        scratch_shapes=[pltpu.SemaphoreType.DMA((3,))],
        compiler_params=pltpu.CompilerParams(vmem_limit_bytes=MIB),
        cost_estimate=SMALL,
    )(packed, basis, taper, turn)
    keep, give = pl.pallas_call(
        whiten_kernel,
        in_specs=[SMEM] + [VMEM] * 3,
        out_specs=[VMEM] * 2,
        out_shape=[jax.ShapeDtypeStruct((HALF, SPEC), BF16)] * 2,
        compiler_params=pltpu.CompilerParams(vmem_limit_bytes=8 * MIB),
    )(place, arrived, basis, taper)

    unit = jnp.concatenate([keep, sibling(give)], axis=0)
    beyond = across(unit)
    ahead, behind = first(unit, 1), first(unit, -1)
    opposite = first(unit, 2)
    near_side, token = rotate(place, [(0, 0), (1, 0), (1, 1), (0, 1)], unit, sibling(unit), turn)
    beyond_ahead, beyond_behind, beyond_opposite = first(beyond, 1), first(beyond, -1), first(beyond, 2)
    (turned,) = grouped([(0, h, 0, h) for h in range(2)], [2], [unit], [ahead, behind, opposite])
    facing = neighbour(turned)
    facing_sib = sibling(facing)
    arrays = [unit, ahead, behind, opposite, beyond, beyond_ahead, beyond_behind, beyond_opposite]
    line_at = [(0, 0), (-1, 0), (1, 0), (2, 0), (0, 1), (-1, 1), (1, 1), (2, 1)]
    moves = [(i, h, h, i) for i in range(8) for h in range(2)]
    moves += [(i, h, h + 2, p) for i, h, _, p in moves]
    kept, given, later_kept, later_given = grouped(moves, [8] * 4, arrays, [facing, token])
    far_side, _ = rotate(place, [(0, 0), (1, 0), (1, 1), (0, 1)], facing, facing_sib, turn)
    rotated = (near_side, far_side)
    kept_up, given_down = second(kept, 1), second(given, -1, swap=1)
    later_kept, later_given = gated(later_kept, [facing_sib]), gated(later_given, [facing_sib])
    kept_down, given_up = second(later_kept, -1), second(later_given, 1, swap=1)

    def product(out, *carried):
        return matmul(place, [(value, other, line_at, dq) for value, other, dq in carried], rotated, out)

    out, done = product(None, (kept, False, 0), (sibling(given), True, 0))
    kept_up, given_down = gated(kept_up, [done]), gated(given_down, [done])
    kept_far, given_far = second(kept_up, 1), first(given_down, -1)
    out, _ = product(out, (kept_up, False, -1), (given_down, True, 1))
    out, _ = product(out, (kept_down, False, 1), (given_up, True, -1))
    out, _ = product(out, (kept_far, False, -2), (given_far, True, 2))
    return out.reshape(NZ * NXH * NY, QC, COLS)


def solution(mesh):
    in_specs = (
        P(("blk", "freq"), None),
        P(("blk", "freq")),
        P(("blk", "freq")),
        P(("blk", "freq")),
    )
    out_specs = P(None, "freq", "blk")
    return jax.shard_map(local, mesh=mesh, in_specs=in_specs, out_specs=out_specs, check_vma=False)
```
